32 devices in a mesh: row: 16 (over z, y, core), tp: 2 (over x).
Axes of the slice: x: 2, y: 2, z: 4, core: 2. Of those that a mesh axis runs over, the one named last changes fastest.
Arguments:
- tokens: bfloat16 [16384, 768], P('row'), may hold values from -6 to 6
- doc_ids: int32 [16, 1024], P('row'), may hold values from 0 to 7, never falling along the last dimension, each value on 1 to 512 neighbouring positions
- dilations: int32 [5], replicated, may hold values from 1 to 16, as said below
- cotangent: bfloat16 [16384, 768], P('row'), may hold values from -6 to 6
- w_query: bfloat16 [768, 768], replicated, may hold values from -0.21875 to 0.21875
- w_key: bfloat16 [768, 768], replicated, may hold values from -0.21875 to 0.21875
- w_value: bfloat16 [768, 768], replicated, may hold values from -0.21875 to 0.21875
- w_out: bfloat16 [768, 768], replicated, may hold values from -0.21875 to 0.21875
- w_up: bfloat16 [768, 3072], P(None, 'tp'), may hold values from -2 to 2
- w_down: bfloat16 [3072, 768], P('tp'), may hold values from -2 to 2
- gain_attn: float32 [768], replicated, may hold values from 0.1 to 1.9
- gain_sub: float32 [768], replicated, may hold values from 0.1 to 1.9
- gain_ffn: float32 [768], replicated, may hold values from 0.1 to 1.9
- gain_mid: float32 [3072], P('tp'), may hold values from 0.1 to 1.9
Outputs:
- output: bfloat16 [16384, 768], P('row')
- grad_tokens: float32 [16384, 768], P('row')
- grad_query: float32 [768, 768], P('row')
- grad_key: float32 [768, 768], P('row')
- grad_value: float32 [768, 768], P('row')
- grad_out: float32 [768, 768], P('row')
- grad_up: float32 [768, 3072], P('row', 'tp')
- grad_down: float32 [3072, 768], P('tp', 'row')
- grad_gain_attn: float32 [768], P('row')
- grad_gain_sub: float32 [768], P('row')
- grad_gain_ffn: float32 [768], P('row')
- grad_gain_mid: float32 [3072], P(('tp', 'row'))
The draws below stay inside these ranges and needn't reach their ends.
Inputs may be any that keep to these rules, and one draw needn't show every extreme that they name: `doc_ids`: within each row document numbers never fall; a document lies in one row and spans at most 512 positions. `dilations`: each dilation is a power of two drawn from the seed; some pattern has dilation 1 and some has dilation 16.
All inputs are finite; a program needn't handle non-finite values.
Results may differ from the reference program's by a relative error of at most 0.014.
Values may be sent and summed in bfloat16 or wider, within the bound.
A program may use at most 256 MiB of HBM per device.

```python
import math
import jax
import jax.numpy as jnp
import numpy as np
from jax import lax

D = 768
HEADS = 12
HEAD_DIM = 64
FF = 3072
PATTERNS = 5
ROW_LEN = 1024
DOCS = 8
ROWS = 16
TOKENS = 16384


def draw_dilations(key, part):
    key = jax.random.fold_in(key, 7)
    first_key, second_key = jax.random.split(key)
    exponents = jax.random.randint(first_key, (PATTERNS,), 0, 5, dtype=jnp.int32)
    order = jax.random.permutation(second_key, PATTERNS)
    exponents = exponents.at[order[0]].set(0).at[order[1]].set(4)
    return jnp.left_shift(jnp.ones((PATTERNS,), jnp.int32), exponents)


def rising_scale(count, lowest, highest):
    place = jnp.arange(count, dtype=jnp.float32) / (count - 1)
    return lowest * jnp.exp(place * jnp.log(highest / lowest))


def draw_w_up(key, part):
    key = jax.random.fold_in(key, 11)
    entries = jax.random.truncated_normal(key, -3.0, 3.0, (D, FF), jnp.float32)
    column_scale = rising_scale(FF, 0.5, 2.0)
    return (entries * column_scale[None, :] * D ** (-0.5)).astype(jnp.bfloat16)


def draw_w_down(key, part):
    key = jax.random.fold_in(key, 13)
    entries = jax.random.truncated_normal(key, -3.0, 3.0, (FF, D), jnp.float32)
    row_scale = rising_scale(FF, 0.5, 2.0)
    return (entries * row_scale[:, None] * FF ** (-0.5)).astype(jnp.bfloat16)


def block_levels(stream_key, extent, cuts, low, top_value):
    level, own = 1.0, jax.random.fold_in(stream_key, 6)
    for axis_at, blocks in cuts:
        draws = jnp.exp(jax.random.uniform(jax.random.fold_in(own, axis_at), (blocks,), jnp.float32, low / len(cuts), top_value / len(cuts)))
        level = level * jnp.repeat(draws, extent[axis_at] // blocks).reshape([-1 if axis == axis_at else 1 for axis in range(len(extent))])
    return level


def split_up(amount, total, limit, slope):
    loads = [(1 << 20) // math.isqrt(rank ** slope) + 1 for rank in range(2, amount + 1)]
    spare, holding = total - limit - (amount - 1), [1] * (amount - 1)
    while spare > 0:
        candidates = [i for i in range(amount - 1) if holding[i] < limit]
        mass, remaining = sum([loads[i] for i in candidates]), spare
        for i in candidates:
            addition = min(limit - holding[i], max(1, remaining * loads[i] // mass), spare)
            holding[i] = holding[i] + addition
            spare = spare - addition
    return np.array([limit] + holding)


def ragged(rng, amount, total, limit, skew):
    if amount == 2:
        one = jax.random.randint(rng, (), max(1, total - limit), min(limit, total - 1) + 1)
        return jnp.stack([one, total - one])
    tallies = jnp.asarray(split_up(amount, total, limit, skew), jnp.int32)
    twos = (amount - 1) // 2
    source_of, taker = tallies[1:1 + 2 * twos:2], tallies[2:2 + 2 * twos:2]
    margin = jnp.minimum(source_of - 1, limit - taker)
    moved = jax.random.randint(jax.random.fold_in(rng, 1), (twos,), 0, 1 << 20) % (margin + 1)
    tallies = tallies.at[1:1 + 2 * twos:2].set(source_of - moved).at[2:2 + 2 * twos:2].set(taker + moved)
    return tallies[jax.random.permutation(jax.random.fold_in(rng, 2), amount)]


def gaussian(own_key, extent, spread, limit, cuts=(), kind=jnp.bfloat16):
    values = spread * jax.random.normal(own_key, extent, jnp.float32)
    if cuts:
        values = values * block_levels(own_key, extent, cuts, -0.22, 0.18)
    return jnp.clip(values, -limit, limit).astype(kind)


def setup_inputs(seed: int = 0) -> dict:
    streams_of = jax.random.split(jax.random.key(seed), 15)
    return {
        "tokens": gaussian(streams_of[0], (TOKENS, D), 1.0, 6.0, ((0, 16),)),
        "doc_ids": jax.vmap(lambda own: jnp.searchsorted(jnp.cumsum(ragged(own, DOCS, ROW_LEN, ROW_LEN // 2, 2)), jnp.arange(ROW_LEN), side="right"))(jax.random.split(streams_of[1], ROWS)).reshape((ROWS, ROW_LEN)).astype(jnp.int32),
        "dilations": draw_dilations(jax.random.fold_in(streams_of[14], 71), 0),
        "cotangent": gaussian(streams_of[3], (TOKENS, D), 1.0, 6.0, ((0, 16),)),
        "w_query": gaussian(streams_of[4], (D, D), D ** -0.5, 0.21875),
        "w_key": gaussian(streams_of[5], (D, D), D ** -0.5, 0.21875),
        "w_value": gaussian(streams_of[6], (D, D), D ** -0.5, 0.21875),
        "w_out": gaussian(streams_of[7], (D, D), D ** -0.5, 0.21875),
        "w_up": draw_w_up(jax.random.fold_in(streams_of[14], 71), 0),
        "w_down": draw_w_down(jax.random.fold_in(streams_of[14], 71), 0),
        "gain_attn": jnp.clip(1.0 + 0.18 * jax.random.normal(streams_of[10], (D,), jnp.float32), 0.1, 1.9),
        "gain_sub": jnp.clip(1.0 + 0.18 * jax.random.normal(streams_of[11], (D,), jnp.float32), 0.1, 1.9),
        "gain_ffn": jnp.clip(1.0 + 0.18 * jax.random.normal(streams_of[12], (D,), jnp.float32), 0.1, 1.9),
        "gain_mid": jnp.clip(1.0 + 0.18 * jax.random.normal(streams_of[13], (FF,), jnp.float32), 0.1, 1.9),
    }


HIGH = lax.Precision.HIGHEST
EPS = 1e-05

@jax.custom_vjp
def low(v):
    return lax.optimization_barrier(v.astype(jnp.bfloat16)).astype(jnp.float32)

@jax.custom_vjp
def low_back(v):
    return v

def low_keep(v):
    return (low(v), None)

def low_pass(kept, grad):
    return (grad,)

def back_keep(v):
    return (v, None)

def back_low(kept, grad):
    return (low(grad),)
low.defvjp(low_keep, low_pass)
low_back.defvjp(back_keep, back_low)

def matmul(left, right):
    return jnp.dot(left, right, precision=HIGH, preferred_element_type=jnp.float32)

def norm(value, gain):
    row_mean = lax.optimization_barrier(jnp.mean(value, -1, keepdims=True))
    centred = value - row_mean
    return centred * lax.rsqrt(lax.optimization_barrier(jnp.mean(centred * centred, -1, keepdims=True)) + EPS) * gain

def mid_norm(value, gain):
    row_mean = lax.optimization_barrier(jnp.mean(value, -1, keepdims=True))
    variance = lax.optimization_barrier(jnp.mean(value * value, -1, keepdims=True)) - row_mean * row_mean
    return (value - row_mean) * lax.rsqrt(variance + EPS) * gain

def selection(dilations, positions):
    head_ids = jnp.arange(HEADS, dtype=jnp.int32)
    left_side = positions[None, None, :] % dilations[:, None, None]
    right_side = head_ids[None, :, None] % dilations[:, None, None]
    return (left_side == right_side).astype(jnp.float32)

def multiplicity(dilations, doc_row):
    positions = jnp.arange(ROW_LEN, dtype=jnp.int32)
    selected = selection(dilations, positions)
    counts = jnp.zeros((HEADS, ROW_LEN, ROW_LEN), jnp.float32)
    for pattern in range(PATTERNS):
        counts = counts + selected[pattern][:, :, None] * selected[pattern][:, None, :]
    allowed = (positions[:, None] >= positions[None, :]) & (doc_row[:, None] == doc_row[None, :])
    return counts * allowed.astype(jnp.float32)[None]

def layer(row_in, params, weights_mult):
    w_query, w_key, w_value, w_out, w_up, w_down, gain_attn, gain_sub, gain_ffn, gain_mid = params
    normed = low(norm(row_in, gain_attn))
    queries = low_back(low(matmul(normed, w_query))).reshape(ROW_LEN, HEADS, HEAD_DIM)
    keys = low_back(low(matmul(normed, w_key))).reshape(ROW_LEN, HEADS, HEAD_DIM)
    values = low_back(low(matmul(normed, w_value))).reshape(ROW_LEN, HEADS, HEAD_DIM)
    scores = low_back(jnp.einsum('ihe,jhe->hij', queries, keys, precision=HIGH) * HEAD_DIM ** (-0.5))
    masked = jnp.where(weights_mult > 0, scores, -1e+30)
    row_max = lax.optimization_barrier(jnp.max(masked, -1, keepdims=True))
    expo = weights_mult * jnp.exp(masked - row_max)
    attn_prob = low(expo / lax.optimization_barrier(jnp.sum(expo, -1, keepdims=True)))
    attended = jnp.einsum('hij,jhe->ihe', attn_prob, values, precision=HIGH).reshape(ROW_LEN, HEADS * HEAD_DIM)
    attended = low_back(attended)
    sub_out = low(norm(attended, gain_sub))
    mid_res = row_in + low_back(matmul(sub_out, w_out))
    ffn_in = low(norm(mid_res, gain_ffn))
    hidden_pre = low_back(matmul(ffn_in, w_up))
    hidden_act = jax.nn.gelu(hidden_pre, approximate=False)
    mid_out = low(mid_norm(hidden_act, gain_mid))
    return mid_res + matmul(mid_out, w_down)

def reference(tokens, doc_ids, dilations, cotangent, w_query, w_key, w_value, w_out, w_up, w_down, gain_attn, gain_sub, gain_ffn, gain_mid):
    params = (w_query.astype(jnp.float32), w_key.astype(jnp.float32), w_value.astype(jnp.float32), w_out.astype(jnp.float32), w_up.astype(jnp.float32), w_down.astype(jnp.float32), gain_attn.astype(jnp.float32), gain_sub.astype(jnp.float32), gain_ffn.astype(jnp.float32), gain_mid.astype(jnp.float32))
    rows_in = tokens.astype(jnp.float32).reshape(ROWS, ROW_LEN, D)
    cot_rows = cotangent.astype(jnp.float32).reshape(ROWS, ROW_LEN, D)

    def per_row(totals, items):
        row_in, cot_row, doc_row = items

        def forward(value, weights):
            return layer(value, weights, multiplicity(dilations, doc_row))
        result, pullback = jax.vjp(forward, row_in, params)
        grad_in, grad_params = pullback(cot_row)
        totals = jax.tree.map(jnp.add, totals, grad_params)
        return (totals, (result.astype(jnp.bfloat16), grad_in))
    start_totals = jax.tree.map(jnp.zeros_like, params)
    totals, (outputs, grad_rows) = lax.scan(per_row, start_totals, (rows_in, cot_rows, doc_ids))
    return (outputs.reshape(TOKENS, D), grad_rows.reshape(TOKENS, D), totals[0], totals[1], totals[2], totals[3], totals[4], totals[5], totals[6], totals[7], totals[8], totals[9])
```

```python
import functools

import jax
import jax.numpy as jnp
from jax import lax
from jax.experimental import pallas as pl
from jax.experimental.pallas import tpu as pltpu
from jax.sharding import PartitionSpec as P

MESH = pl.DeviceIdType.MESH
HEADS = 12
HEAD_DIM = 64
FF = 3072
EPS = 1e-05
F32 = jnp.float32
BF16 = jnp.bfloat16
LOG2E = 1.4426950408889634
CHUNK = 256
WINDOW = 512
LANES = 128
MIB = 2**20


def dot(left, right, left_dim, right_dim):
    return lax.dot_general(
        left, right, (((left_dim,), (right_dim,)), ((), ())), preferred_element_type=F32
    )


def moments(value):
    mean = jnp.mean(value, -1, keepdims=True)
    centred = value - mean
    inv = lax.rsqrt(jnp.mean(centred * centred, -1, keepdims=True) + EPS)
    return centred * inv, inv


def norm_grad(hat, inv, gain, grad):
    scaled = grad * gain
    first = jnp.mean(scaled, -1, keepdims=True)
    second = jnp.mean(scaled * hat, -1, keepdims=True)
    return inv * (scaled - first - hat * second)


def repeat(tile, rows, columns):
    tall = jnp.concatenate([tile] * (rows // tile.shape[0]), 0)
    return jnp.concatenate([tall] * (columns // tile.shape[1]), 1)


def layer_kernel(
    places,
    dil,
    tok,
    doc,
    cot,
    wq,
    wk,
    wv,
    wo,
    wup_far,
    wdn,
    ga,
    gs,
    gf,
    gm,
    out_far,
    gtok,
    o_query,
    o_key,
    o_value,
    o_out,
    o_up,
    o_down,
    o_gain,
    qs,
    ks,
    vs,
    att,
    mid,
    ffn_in,
    mid_out,
    grad_pre,
    ring_h,
    ring_d,
    gffn_own,
    gffn_got,
    ffp_own,
    ffp_got,
    weights_c,
    doc_col,
    lse,
    delta,
    stat_tile,
    stat_own,
    stat_got,
    gain_mid_sum,
    gain_own,
    gain_got,
    item_u,
    item_d,
    wup_near,
    got_core,
    got_y,
    got_z,
    half_own,
    half_got,
    stat_sem,
    gffn_sem,
    ffp_sem,
    item_sem,
    gain_sem,
    half_sem,
    load_sem,
    store_sem,
):
    nz, ny = places
    row, tp = lax.axis_index("row"), lax.axis_index("tp")
    core = lax.rem(row, 2)
    y_at = lax.rem(row // 2, ny)
    z_at = row // (2 * ny)
    to_x = (row, 1 - tp)
    to_core = (row + 1 - 2 * core, tp)
    to_y = (row + 2 - 4 * y_at, tp)
    to_z = [
        (lax.rem(z_at + k, nz) * (2 * ny) + lax.rem(row, 2 * ny), tp) for k in range(1, nz)
    ]
    length, width = tok.shape
    half = wdn.shape[0]
    chunks = length // CHUNK
    pairs = width // LANES
    piece = width // (nz * ny * 2)

    load = pltpu.make_async_copy(wup_far, wup_near, load_sem.at[0])
    load.start()
    barrier = pltpu.get_barrier_semaphore()
    partners = [to_x, to_core, to_y] + to_z
    for partner in partners:
        pl.semaphore_signal(barrier, inc=1, device_id=partner, device_id_type=MESH)
    pl.semaphore_wait(barrier, len(partners))

    def remote(src, dst, sems, at, partner):
        return pltpu.make_async_remote_copy(
            src_ref=src,
            dst_ref=dst,
            send_sem=sems.at[0, at],
            recv_sem=sems.at[1, at],
            device_id=partner,
            device_id_type=MESH,
        )

    lane = lax.broadcasted_iota(jnp.int32, (1, LANES), 1)
    low_lane = lane < HEAD_DIM
    lane_f = [low_lane.astype(F32), 1.0 - low_lane.astype(F32)]
    lane_b = [value.astype(BF16) for value in lane_f]

    row_at = lax.broadcasted_iota(jnp.int32, (16, LANES), 0)
    col_at = lax.broadcasted_iota(jnp.int32, (16, LANES), 1)
    for head in range(HEADS):
        row_count = jnp.zeros((16, LANES), F32)
        col_count = jnp.zeros((16, LANES), F32)
        for pattern in range(dil.shape[0]):
            last = dil[pattern] - 1
            row_count += (((row_at - head) & last) == 0).astype(F32)
            col_count += (((col_at - head) & last) == 0).astype(F32)
        weights_c[head] = jnp.minimum(row_count, col_count)
    for block in range(length // LANES):
        ids = doc[:, block * LANES : (block + 1) * LANES].astype(F32)
        doc_col[block * LANES : (block + 1) * LANES, :] = jnp.broadcast_to(ids, (LANES, LANES)).T
    doc_row = doc[...].astype(F32)
    bias = gtok
    gain_mid_sum[...] = jnp.zeros_like(gain_mid_sum)
    gain_own[...] = jnp.zeros_like(gain_own)

    def project(at):
        rows = pl.ds(at * CHUNK, CHUNK)
        hat, _ = moments(tok[rows, :].astype(F32))
        value = (hat * ga[...]).astype(BF16)
        qs[rows, :] = dot(value, wq[...], 1, 0).astype(BF16)
        ks[rows, :] = dot(value, wk[...], 1, 0).astype(BF16)
        vs[rows, :] = dot(value, wv[...], 1, 0).astype(BF16)

    def attend(at):
        first = at * CHUNK
        start = max(0, first - WINDOW)
        span = first + CHUNK - start
        rows, keys = pl.ds(first, CHUNK), pl.ds(start, span)
        query_at = first + lax.broadcasted_iota(jnp.int32, (CHUNK, LANES), 0)
        key_at = lax.broadcasted_iota(jnp.int32, (CHUNK, LANES), 1)
        own_docs = doc_col[rows, :]
        for block in range(span // LANES):
            low = start + block * LANES
            allowed = (key_at + low <= query_at) & (own_docs == doc_row[:, low : low + LANES])
            bias[0:CHUNK, block * LANES : (block + 1) * LANES] = jnp.where(allowed, 0.0, -1e30)

        def pair_step(pair, carry):
            lanes = pl.ds(pl.multiple_of(pair * LANES, LANES), LANES)
            query, key, value = qs[rows, lanes], ks[keys, lanes], vs[keys, lanes]
            tops, parts = [], []
            for side in range(2):
                scores = dot(query * lane_b[side], key, 1, 1) * (HEAD_DIM**-0.5 * LOG2E)
                scores = scores + bias[0:CHUNK, :span]
                top = jnp.max(scores, -1, keepdims=True)
                expo = jnp.exp2(scores - top) * repeat(weights_c[2 * pair + side], CHUNK, span)
                tops.append(top)
                parts.append(
                    dot(expo.astype(BF16), value * lane_b[side] + lane_b[1 - side], 1, 0)
                )
            total = pltpu.roll(jnp.where(low_lane, parts[1], parts[0]), HEAD_DIM, 1)
            att[rows, lanes] = jnp.where(low_lane, parts[0], parts[1]) / total
            log_sum = (jnp.where(low_lane, tops[0], tops[1]) + jnp.log2(total)).T
            lse[pair, 0:1, rows] = log_sum[0:1, :]
            lse[pair, 1:2, rows] = log_sum[HEAD_DIM : HEAD_DIM + 1, :]
            return carry

        lax.fori_loop(0, pairs, pair_step, 0)

    STRIP = 32

    def feed(at):
        rows = pl.ds(at * CHUNK, CHUNK)
        hat, _ = moments(att[rows, :])
        sub = (hat * gs[...]).astype(BF16)
        mid_res = tok[rows, :].astype(F32) + dot(sub, wo[...], 1, 0)
        mid[rows, :] = mid_res
        hat, _ = moments(mid_res)
        value = (hat * gf[...]).astype(BF16)
        ffn_in[rows, :] = value
        ring_h[...] = dot(value, wup_near[...].reshape(width, half), 1, 0)
        ring_d[...] = dot(cot[rows, :], wdn[...], 1, 1)

        def strip(index, carry):
            part = pl.ds(pl.multiple_of(index * STRIP, STRIP), STRIP)
            pre = ring_h[part, :]
            act = 0.5 * pre * (1.0 + lax.erf(pre * 0.7071067811865476))
            scaled = ring_d[part, :] * gm[...]
            sums = [
                jnp.sum(value, -1, keepdims=True)
                for value in (act, act * act, scaled, scaled * act)
            ]
            tile = jnp.where(lane == 0, sums[0], jnp.where(lane == 1, sums[1], 0.0))
            tile = jnp.where(lane == 2, sums[2], jnp.where(lane == 3, sums[3], tile))
            stat_tile[part, :] = tile
            return carry

        lax.fori_loop(0, CHUNK // STRIP, strip, 0)
        stat_own[at] = stat_tile[...].T[0:8, :]
        remote(stat_own.at[at], stat_got.at[at], stat_sem, at, to_x).start()

    def gffn_copy(at):
        rows = pl.ds(at * CHUNK, CHUNK)
        return remote(gffn_own.at[rows], gffn_got.at[rows], gffn_sem, at, to_x)

    def ffp_copy(at):
        rows = pl.ds(at * CHUNK, CHUNK)
        return remote(ffp_own.at[rows], ffp_got.at[rows], ffp_sem, at, to_x)

    def feed_back(at):
        rows = pl.ds(at * CHUNK, CHUNK)
        remote(stat_own.at[at], stat_got.at[at], stat_sem, at, to_x).wait()
        both = stat_own[at] + stat_got[at]
        both = jnp.concatenate([both, jnp.zeros((LANES - 8, CHUNK), F32)], 0).T
        mean = both[:, 0:1] / FF
        inv = lax.rsqrt(both[:, 1:2] / FF - mean * mean + EPS)
        first = both[:, 2:3] / FF
        second = inv * (both[:, 3:4] - mean * both[:, 2:3]) / FF
        tile = jnp.where(lane == 0, mean, jnp.where(lane == 1, inv, 0.0))
        stat_tile[...] = jnp.where(lane == 2, first, jnp.where(lane == 3, second, tile))

        def strip(index, carry):
            part = pl.ds(pl.multiple_of(index * STRIP, STRIP), STRIP)
            target = pl.ds(pl.multiple_of(at * CHUNK + index * STRIP, STRIP), STRIP)
            stats = stat_tile[part, :]
            pre = ring_h[part, :]
            grad = ring_d[part, :]
            cdf = 0.5 * (1.0 + lax.erf(pre * 0.7071067811865476))
            slope = cdf + pre * (jnp.exp2(pre * pre * (-0.5 * LOG2E)) * 0.3989422804014327)
            hat = (pre * cdf - stats[:, 0:1]) * stats[:, 1:2]
            mid_out[target, :] = (hat * gm[...]).astype(BF16)
            gain_part = grad * hat
            gain_mid_sum[...] += sum(
                gain_part[8 * i : 8 * i + 8, :] for i in range(STRIP // 8)
            )
            back = stats[:, 1:2] * (grad * gm[...] - stats[:, 2:3] - hat * stats[:, 3:4])
            grad_pre[target, :] = (back * slope).astype(BF16)
            return carry

        lax.fori_loop(0, CHUNK // STRIP, strip, 0)
        gffn_own[rows, :] = dot(grad_pre[rows, :], wup_near[...].reshape(width, half), 1, 1).astype(BF16)
        gffn_copy(at).start()
        ffp_own[rows, :] = dot(mid_out[rows, :], wdn[...], 1, 0).astype(BF16)

    for at in range(chunks + 1):
        if at < chunks:
            project(at)
            attend(at)
        if at == 0:
            load.wait()
        if at >= 1:
            feed_back(at - 1)
        if at < chunks:
            feed(at)
        if at == 2:
            ffp_copy(0).start()
    for at in range(1, chunks):
        ffp_copy(at).start()

    item_a = wup_near
    items = (item_u, item_d, item_a)

    def core_copy(which):
        return remote(
            items[which].at[:, :, 1 - core], got_core.at[which], item_sem, 8 * which, to_core
        )

    def y_copy(which):
        return remote(
            items[which].at[:, 1 - y_at, core], got_y.at[which], item_sem, 8 * which + 1, to_y
        )

    def z_copies(which):
        return [
            remote(
                items[which].at[lax.rem(z_at + k, nz), y_at, core],
                got_z.at[which, k - 1],
                item_sem,
                8 * which + 1 + k,
                to_z[k - 1],
            )
            for k in range(1, nz)
        ]

    def start_core(which):
        core_copy(which).start()

    def start_y(which):
        core_copy(which).wait()
        item = items[which]

        def add(index, carry):
            z_to, y_to = index // ny, lax.rem(index, ny)
            total = item[z_to, y_to, core].astype(F32) + got_core[which, z_to, y_to].astype(F32)
            item[z_to, y_to, core] = total.astype(BF16)
            return carry

        lax.fori_loop(0, nz * ny, add, 0)
        y_copy(which).start()

    def start_z(which):
        y_copy(which).wait()
        item = items[which]

        def add(z_to, carry):
            total = item[z_to, y_at, core].astype(F32) + got_y[which, z_to].astype(F32)
            item[z_to, y_at, core] = total.astype(BF16)
            return carry

        lax.fori_loop(0, nz, add, 0)
        for copy in z_copies(which):
            copy.start()

    def finish(which):
        for copy in z_copies(which):
            copy.wait()
        total = items[which][z_at, y_at, core].astype(F32)
        for k in range(1, nz):
            total = total + got_z[which, k - 1].astype(F32)
        return total

    COLUMNS = 512

    def outer(item, left, right):
        def step(index, carry):
            columns = pl.ds(pl.multiple_of(index * COLUMNS, COLUMNS), COLUMNS)
            product = dot(left[...], right[:, columns], 0, 0).astype(BF16)
            item[:, :, :, :, columns] = product.reshape(nz, ny, 2, piece, COLUMNS)
            return carry

        lax.fori_loop(0, half // COLUMNS, step, 0)

    outer(item_u, ffn_in, grad_pre)
    start_core(0)
    outer(item_d, cot, mid_out)
    start_core(1)

    grad_res = ffn_in
    grad_att = grad_pre
    sub_out = gffn_own
    normed = gffn_got
    for at in range(chunks):
        rows = pl.ds(at * CHUNK, CHUNK)
        gffn_copy(at).wait()
        grad = gffn_own[rows, :].astype(F32) + gffn_got[rows, :].astype(F32)
        hat, inv = moments(mid[rows, :])
        gain_own[2:3, :] += jnp.sum(grad * hat, 0, keepdims=True)
        grad_mid = cot[rows, :].astype(F32) + norm_grad(hat, inv, gf[...], grad)
        gtok[rows, :] = grad_mid
        grad_low = grad_mid.astype(BF16)
        grad_res[rows, :] = grad_low
        grad = dot(grad_low, wo[...], 1, 1)
        hat, inv = moments(att[rows, :])
        sub_out[rows, :] = (hat * gs[...]).astype(BF16)
        gain_own[1:2, :] += jnp.sum(grad * hat, 0, keepdims=True)
        grad_att[rows, width : 2 * width] = norm_grad(hat, inv, gs[...], grad).astype(BF16)
        hat, _ = moments(tok[rows, :].astype(F32))
        normed[rows, :] = (hat * ga[...]).astype(BF16)
        if at == 0:
            start_y(0)
        if at == 1:
            start_y(1)

    def mask_ref(which):
        ring = ring_h if which < 6 else ring_d
        return ring, slice((which % 6) * CHUNK, (which % 6 + 1) * CHUNK)

    tiles = [
        (key, query)
        for key in range(chunks)
        for query in range(key, min(chunks, key + WINDOW // CHUNK + 1))
    ]
    key_off = lax.broadcasted_iota(jnp.int32, (CHUNK, LANES), 0)
    query_off = lax.broadcasted_iota(jnp.int32, (CHUNK, LANES), 1)
    for which, (key, query) in enumerate(tiles):
        ring, columns = mask_ref(which)
        key_docs = doc_col[key * CHUNK : (key + 1) * CHUNK, :]
        for block in range(CHUNK // LANES):
            low = query * CHUNK + block * LANES
            allowed = key_docs == doc_row[:, low : low + LANES]
            if key == query:
                allowed = allowed & (key_off + key * CHUNK <= query_off + low)
            begin = columns.start + block * LANES
            ring[:, begin : begin + LANES] = jnp.where(allowed, 0.0, -1e30)

    select = (lax.broadcasted_iota(jnp.int32, (8, LANES), 1) // HEAD_DIM) == (
        lax.broadcasted_iota(jnp.int32, (8, LANES), 0)
    )
    select = select.astype(F32).astype(BF16)
    half_width = width // 2

    def dq_part(block):
        begin = 3 * CHUNK + block * LANES
        return ring_d, slice(begin, begin + LANES)

    def pair_back(step, carry):
        pair = lax.rem(tp * (pairs // 2) + step, pairs)
        low = pl.multiple_of(pair * LANES, LANES)
        lanes = pl.ds(low, LANES)
        upper = pl.ds(pl.multiple_of(width + low, LANES), LANES)
        product = grad_att[:, upper].astype(F32) * att[:, lanes]
        high = product.astype(BF16)
        rest = (product - high.astype(F32)).astype(BF16)
        delta[...] = dot(select, high, 1, 1) + dot(select, rest, 1, 1)
        for block in range(chunks):
            ring, columns = dq_part(block)
            ring[:, columns] = jnp.zeros((CHUNK, LANES), F32)
        for key_block in range(chunks):
            keys = slice(key_block * CHUNK, (key_block + 1) * CHUNK)
            key, value = ks[keys, lanes], vs[keys, lanes]
            key_two = jnp.concatenate([key * lane_b[0], key * lane_b[1]], 0)
            value_two = jnp.concatenate([value * lane_b[0], value * lane_b[1]], 0)
            dk_sum = jnp.zeros((CHUNK, LANES), F32)
            dv_sum = jnp.zeros((CHUNK, LANES), F32)
            for which, (key_at, query_at) in enumerate(tiles):
                if key_at != key_block:
                    continue
                ring, columns = mask_ref(which)
                queries = slice(query_at * CHUNK, (query_at + 1) * CHUNK)
                query = qs[queries, lanes]
                grad_out = grad_att[queries, upper]
                scores = dot(key_two, query, 1, 1)
                grad_prob = dot(value_two, grad_out, 1, 1)
                grad_scores = []
                for side in range(2):
                    mine = slice(side * CHUNK, (side + 1) * CHUNK)
                    power = scores[mine, :] * (HEAD_DIM**-0.5 * LOG2E) + ring[:, columns]
                    power = power - lse[pair, side : side + 1, queries]
                    prob = jnp.exp2(power) * repeat(weights_c[2 * pair + side], CHUNK, CHUNK)
                    dv_sum += dot(prob.astype(BF16), grad_out * lane_b[side], 1, 0)
                    grad_score = prob * (grad_prob[mine, :] - delta[side : side + 1, queries])
                    grad_score = grad_score.astype(BF16)
                    dk_sum += dot(grad_score, query * lane_b[side], 1, 0)
                    grad_scores.append(grad_score)
                ring, columns = dq_part(query_at)
                ring[:, columns] += dot(jnp.concatenate(grad_scores, 0), key_two, 0, 0)
            mid_out[keys, upper] = (dk_sum * HEAD_DIM**-0.5).astype(BF16)
            grad_pre[keys, lanes] = dv_sum.astype(BF16)
        for block in range(chunks):
            ring, columns = dq_part(block)
            grad = (ring[:, columns] * HEAD_DIM**-0.5).astype(BF16)
            mid_out[block * CHUNK : (block + 1) * CHUNK, lanes] = grad

        @pl.when(step == 0)
        def _():
            start_z(0)

        @pl.when(step == 2)
        def _():
            start_z(1)
            offset = pl.multiple_of(tp * half_width, LANES)
            offset_up = pl.multiple_of(width + tp * half_width, LANES)
            sources = (
                (normed, mid_out, offset),
                (normed, mid_out, offset_up),
                (normed, grad_pre, offset),
                (sub_out, grad_res, offset),
            )
            for index, (left, right, begin) in enumerate(sources):
                grad = dot(left[...], right[:, pl.ds(begin, half_width)], 0, 0).astype(BF16)
                item_a[:, :, :, :, index * half_width : (index + 1) * half_width] = grad.reshape(
                    nz, ny, 2, piece, half_width
                )
            start_core(2)

        @pl.when(step == 3)
        def _():
            start_y(2)
            o_up[...] = finish(0)

        @pl.when(step == 5)
        def _():
            o_down[...] = finish(1)
            start_z(2)

        return carry

    lax.fori_loop(0, pairs, pair_back, 0)

    for at in range(chunks):
        rows = pl.ds(at * CHUNK, CHUNK)
        grad = dot(mid_out[rows, 0:width], wq[...], 1, 1)
        grad += dot(mid_out[rows, width : 2 * width], wk[...], 1, 1)
        grad += dot(grad_pre[rows, 0:width], wv[...], 1, 1)
        hat, inv = moments(tok[rows, :].astype(F32))
        gain_own[0:1, :] += jnp.sum(grad * hat, 0, keepdims=True)
        gtok[rows, :] += norm_grad(hat, inv, ga[...], grad)

    for side in range(2):
        columns = slice(side * width, (side + 1) * width)
        gain_own[3 + side : 4 + side, :] = jnp.sum(gain_mid_sum[:, columns], 0, keepdims=True)
    for at, partner in ((0, to_core), (1, to_y)):
        copy = remote(gain_own, gain_got.at[at], gain_sem, at, partner)
        copy.start()
        copy.wait()
        gain_own[...] += gain_got[at]
    copies = [
        remote(gain_own, gain_got.at[1 + k], gain_sem, 1 + k, to_z[k - 1]) for k in range(1, nz)
    ]
    for copy in copies:
        copy.start()

    half_own[...] = finish(2).astype(BF16)
    half_copy = remote(half_own, half_got, half_sem, 0, to_x)
    half_copy.start()

    for at in range(chunks):
        rows = pl.ds(at * CHUNK, CHUNK)
        ffp_copy(at).wait()
        total = ffp_own[rows, :].astype(F32) + ffp_got[rows, :].astype(F32)
        ffp_own[rows, :] = (mid[rows, :] + total).astype(BF16)
        pltpu.make_async_copy(ffp_own.at[rows], out_far.at[rows], store_sem.at[at]).start()

    for copy in copies:
        copy.wait()
    total = gain_own[...]
    for k in range(1, nz):
        total = total + gain_got[1 + k]
    o_gain[0:8, :] = pltpu.roll(total, lax.rem(width - piece * row, width), 1)[:, :LANES]
    per_row = 2 * width // (nz * ny * 2)
    o_gain[8:16, :] = pltpu.roll(
        total, lax.rem(2 * width - per_row * row, width), 1
    )[:, :LANES]

    half_copy.wait()
    mine = pl.ds(pl.multiple_of(tp * half_width, LANES), half_width)
    other = pl.ds(pl.multiple_of((1 - tp) * half_width, LANES), half_width)
    for index, target in enumerate((o_query, o_key, o_value, o_out)):
        columns = slice(index * half_width, (index + 1) * half_width)
        target[:, mine] = half_own[:, columns].astype(F32)
        target[:, other] = half_got[:, columns].astype(F32)
    for at in range(chunks):
        rows = pl.ds(at * CHUNK, CHUNK)
        pltpu.make_async_copy(ffp_own.at[rows], out_far.at[rows], store_sem.at[at]).wait()


def fused_body(places, *args):
    (tokens, doc_ids, dilations, cotangent, w_query, w_key, w_value, w_out, w_up, w_down) = args[:10]
    gains = [gain.reshape(1, -1) for gain in args[10:]]
    nz, ny = places
    length, width = tokens.shape
    half = w_up.shape[1]
    piece = width // (2 * nz * ny)
    chunks = length // CHUNK
    vmem = pl.BlockSpec(memory_space=pltpu.VMEM)
    smem = pl.BlockSpec(memory_space=pltpu.SMEM)
    far = pl.BlockSpec(memory_space=pl.ANY)
    shape = jax.ShapeDtypeStruct
    low = functools.partial(pltpu.VMEM, dtype=BF16)
    full = functools.partial(pltpu.VMEM, dtype=F32)
    rows_low, rows_full = low((length, width)), full((length, width))
    item = low((nz, ny, 2, piece, half))
    dma = lambda count: pltpu.SemaphoreType.DMA((2, count))
    results = pl.pallas_call(
        functools.partial(layer_kernel, places),
        out_shape=[
            shape((length, width), BF16),
            shape((length, width), F32),
            shape((piece, width), F32),
            shape((piece, width), F32),
            shape((piece, width), F32),
            shape((piece, width), F32),
            shape((piece, half), F32),
            shape((piece, half), F32),
            shape((16, LANES), F32),
        ],
        in_specs=[smem] + [vmem] * 7 + [far] + [vmem] * 5,
        out_specs=[far] + [vmem] * 8,
        scratch_shapes=[
            rows_low,
            rows_low,
            rows_low,
            rows_full,
            rows_full,
            rows_low,
            low((length, half)),
            low((length, half)),
            full((CHUNK, half)),
            full((CHUNK, half)),
            rows_low,
            rows_low,
            rows_low,
            rows_low,
            full((HEADS, 16, LANES)),
            full((length, LANES)),
            full((width // LANES, 2, length)),
            full((8, length)),
            full((CHUNK, LANES)),
            full((chunks, 8, CHUNK)),
            full((chunks, 8, CHUNK)),
            full((8, half)),
            full((8, width)),
            full((1 + nz, 8, width)),
            item,
            item,
            item,
            low((3, nz, ny, piece, half)),
            low((3, nz, piece, half)),
            low((3, nz - 1, piece, half)),
            low((piece, half)),
            low((piece, half)),
            dma(chunks),
            dma(chunks),
            dma(chunks),
            dma(24),
            dma(1 + nz),
            dma(1),
            pltpu.SemaphoreType.DMA((1,)),
            pltpu.SemaphoreType.DMA((chunks,)),
        ],
        compiler_params=pltpu.CompilerParams(
            collective_id=0, has_side_effects=True, vmem_limit_bytes=63 * MIB
        ),
        name="layer",
    )(
        dilations,
        tokens,
        doc_ids.reshape(1, length),
        cotangent,
        w_query,
        w_key,
        w_value,
        w_out,
        w_up.reshape(nz, ny, 2, piece, half),
        w_down,
        *gains,
    )
    output, grad_tokens, g_query, g_key, g_value, g_out, g_up, g_down, g_gain = results
    row = lax.axis_index("row")
    at_mid = 8 + 3 + (row * 2 * piece) // width
    gain_mid_part = lax.dynamic_slice(g_gain, (at_mid, 0), (1, 2 * piece)).reshape(2 * piece)
    return (
        output,
        grad_tokens,
        g_query,
        g_key,
        g_value,
        g_out,
        g_up,
        g_down.T,
        g_gain[0, :piece],
        g_gain[1, :piece],
        g_gain[2, :piece],
        gain_mid_part,
    )


def norm_parts(value):
    row_mean = jnp.mean(value, -1, keepdims=True)
    centred = value - row_mean
    inv_std = lax.rsqrt(jnp.mean(centred * centred, -1, keepdims=True) + EPS)
    return (centred * inv_std, inv_std)


def norm_back(normed_hat, inv_std, gain, grad):
    scaled = grad * gain
    grad_value = inv_std * (
        scaled
        - jnp.mean(scaled, -1, keepdims=True)
        - normed_hat * jnp.mean(scaled * normed_hat, -1, keepdims=True)
    )
    return (grad_value, jnp.sum(grad * normed_hat, 0))


def selection(dilations, positions):
    head_ids = jnp.arange(HEADS, dtype=jnp.int32)
    left_side = positions[None, None, :] % dilations[:, None, None]
    right_side = head_ids[None, :, None] % dilations[:, None, None]
    return (left_side == right_side).astype(jnp.float32)


def pattern_weights(dilations, doc_row, query_pos, query_docs):
    key_pos = jnp.arange(doc_row.shape[0], dtype=jnp.int32)
    counts = jnp.einsum(
        "phi,phj->hij", selection(dilations, query_pos), selection(dilations, key_pos)
    )
    allowed = (query_pos[:, None] >= key_pos[None, :]) & (query_docs[:, None] == doc_row[None, :])
    return counts * allowed.astype(jnp.float32)[None]


def attn_forward(dilations, doc_row, key_heads, value_heads, query_block, query_pos, query_docs):
    score_scale = HEAD_DIM ** (-0.5)
    scores = (
        jnp.einsum("ihe,jhe->hij", query_block, key_heads, preferred_element_type=jnp.float32)
        * score_scale
    )
    weights_mult = pattern_weights(dilations, doc_row, query_pos, query_docs)
    masked = jnp.where(weights_mult > 0, scores, -1e30)
    row_max = jnp.max(masked, -1, keepdims=True)
    expo = weights_mult * jnp.exp(masked - row_max)
    totals = jnp.sum(expo, -1, keepdims=True)
    attn_prob = (expo / totals).astype(jnp.bfloat16)
    out_block = jnp.einsum(
        "hij,jhe->ihe", attn_prob, value_heads, preferred_element_type=jnp.float32
    )
    return (out_block, row_max[..., 0] + jnp.log(totals[..., 0]))


def attn_backward(
    dilations,
    doc_row,
    key_heads,
    value_heads,
    query_block,
    query_pos,
    query_docs,
    lse_block,
    grad_block,
):
    score_scale = HEAD_DIM ** (-0.5)
    scores = (
        jnp.einsum("ihe,jhe->hij", query_block, key_heads, preferred_element_type=jnp.float32)
        * score_scale
    )
    weights_mult = pattern_weights(dilations, doc_row, query_pos, query_docs)
    attn_full = weights_mult * jnp.exp(scores - lse_block[:, :, None])
    attn_low = attn_full.astype(jnp.bfloat16)
    value_part = jnp.einsum(
        "hij,ihe->jhe", attn_low, grad_block, preferred_element_type=jnp.float32
    )
    grad_prob = jnp.einsum(
        "ihe,jhe->hij", grad_block, value_heads, preferred_element_type=jnp.float32
    )
    row_delta = jnp.sum(attn_full * grad_prob, -1, keepdims=True)
    grad_scores = (attn_full * (grad_prob - row_delta)).astype(jnp.bfloat16)
    query_grad = (
        jnp.einsum("hij,jhe->ihe", grad_scores, key_heads, preferred_element_type=jnp.float32)
        * score_scale
    )
    key_part = (
        jnp.einsum("hij,ihe->jhe", grad_scores, query_block, preferred_element_type=jnp.float32)
        * score_scale
    )
    return (query_grad, key_part, value_part)


def general_body(
    tokens,
    doc_ids,
    dilations,
    cotangent,
    w_query,
    w_key,
    w_value,
    w_out,
    w_up,
    w_down,
    gain_attn,
    gain_sub,
    gain_ffn,
    gain_mid,
):
    row_len = tokens.shape[0]
    width = tokens.shape[1]
    block_rows = min(512, row_len)
    block_count = row_len // block_rows
    doc_row = doc_ids.reshape(row_len)
    row_in = tokens.astype(jnp.float32)
    attn_hat, attn_std = norm_parts(row_in)
    normed = (attn_hat * gain_attn).astype(jnp.bfloat16)
    keys_low = jnp.dot(normed, w_key, preferred_element_type=jnp.float32).astype(jnp.bfloat16)
    values_low = jnp.dot(normed, w_value, preferred_element_type=jnp.float32).astype(jnp.bfloat16)
    key_heads = keys_low.reshape(row_len, HEADS, HEAD_DIM)
    value_heads = values_low.reshape(row_len, HEADS, HEAD_DIM)
    queries = jnp.dot(normed, w_query, preferred_element_type=jnp.float32).astype(jnp.bfloat16)
    query_heads = queries.reshape(row_len, HEADS, HEAD_DIM)

    def attend(block_index):
        offset = block_index * block_rows
        query_block = lax.dynamic_slice_in_dim(query_heads, offset, block_rows, 0)
        query_pos = offset + jnp.arange(block_rows, dtype=jnp.int32)
        query_docs = lax.dynamic_slice_in_dim(doc_row, offset, block_rows, 0)
        return attn_forward(
            dilations, doc_row, key_heads, value_heads, query_block, query_pos, query_docs
        )

    out_blocks, log_sums = lax.map(attend, jnp.arange(block_count))
    attended = out_blocks.reshape(row_len, width)
    sub_hat, sub_std = norm_parts(attended)
    sub_out = (sub_hat * gain_sub).astype(jnp.bfloat16)
    mid_res = row_in + jnp.dot(sub_out, w_out, preferred_element_type=jnp.float32)
    ffn_hat, ffn_std = norm_parts(mid_res)
    ffn_in = (ffn_hat * gain_ffn).astype(jnp.bfloat16)
    hidden_pre = jnp.dot(ffn_in, w_up, preferred_element_type=jnp.float32)
    hidden_act = jax.nn.gelu(hidden_pre, approximate=False)
    sum_first, sum_second = lax.psum(
        (jnp.sum(hidden_act, -1), jnp.sum(hidden_act * hidden_act, -1)), "tp"
    )
    mid_mean = sum_first[:, None] / FF
    mid_std = lax.rsqrt(sum_second[:, None] / FF - mid_mean * mid_mean + EPS)
    mid_hat = (hidden_act - mid_mean) * mid_std
    mid_out = (mid_hat * gain_mid).astype(jnp.bfloat16)
    ffn_part = jnp.dot(mid_out, w_down, preferred_element_type=jnp.float32)
    ffn_total = lax.psum(ffn_part, "tp")
    output = (mid_res + ffn_total).astype(jnp.bfloat16)
    grad_down = jnp.einsum("lf,ld->fd", mid_out, cotangent, preferred_element_type=jnp.float32)
    grad_mid_out = jnp.einsum("ld,fd->lf", cotangent, w_down, preferred_element_type=jnp.float32)
    grad_gain_mid = jnp.sum(grad_mid_out * mid_hat, 0)
    scaled = grad_mid_out * gain_mid
    back_first, back_second = lax.psum((jnp.sum(scaled, -1), jnp.sum(scaled * mid_hat, -1)), "tp")
    grad_act = mid_std * (scaled - back_first[:, None] / FF - mid_hat * back_second[:, None] / FF)
    gelu_pull = jax.vjp(lambda value: jax.nn.gelu(value, approximate=False), hidden_pre)[1]
    grad_pre = gelu_pull(grad_act)[0].astype(jnp.bfloat16)
    grad_up = jnp.einsum("ld,lf->df", ffn_in, grad_pre, preferred_element_type=jnp.float32)
    sum_up, sum_down, sum_gain_mid = (
        lax.psum_scatter(grad_up, "row", scatter_dimension=0, tiled=True),
        lax.psum_scatter(grad_down, "row", scatter_dimension=1, tiled=True),
        lax.psum_scatter(grad_gain_mid, "row", scatter_dimension=0, tiled=True),
    )
    grad_ffn_part = jnp.einsum("lf,df->ld", grad_pre, w_up, preferred_element_type=jnp.float32)
    grad_ffn_in = lax.psum(grad_ffn_part, "tp")
    grad_mid_in, grad_gain_ffn = norm_back(ffn_hat, ffn_std, gain_ffn, grad_ffn_in)
    grad_mid_res = cotangent.astype(jnp.float32) + grad_mid_in
    grad_res_low = grad_mid_res.astype(jnp.bfloat16)
    grad_out = jnp.einsum("ld,le->de", sub_out, grad_res_low, preferred_element_type=jnp.float32)
    grad_sub_out = jnp.einsum("le,de->ld", grad_res_low, w_out, preferred_element_type=jnp.float32)
    grad_attended, grad_gain_sub = norm_back(sub_hat, sub_std, gain_sub, grad_sub_out)
    grad_att_low = grad_attended.astype(jnp.bfloat16)
    grad_heads = grad_att_low.reshape(row_len, HEADS, HEAD_DIM)

    def attend_back(running, block_index):
        key_sum, value_sum = running
        offset = block_index * block_rows
        query_block = lax.dynamic_slice_in_dim(query_heads, offset, block_rows, 0)
        query_pos = offset + jnp.arange(block_rows, dtype=jnp.int32)
        query_docs = lax.dynamic_slice_in_dim(doc_row, offset, block_rows, 0)
        grad_block = lax.dynamic_slice_in_dim(grad_heads, offset, block_rows, 0)
        query_grad, key_part, value_part = attn_backward(
            dilations,
            doc_row,
            key_heads,
            value_heads,
            query_block,
            query_pos,
            query_docs,
            log_sums[block_index],
            grad_block,
        )
        return ((key_sum + key_part, value_sum + value_part), query_grad)

    zero_heads = jnp.zeros((row_len, HEADS, HEAD_DIM), jnp.float32)
    (key_grad, value_grad), query_blocks = lax.scan(
        attend_back, (zero_heads, zero_heads), jnp.arange(block_count)
    )
    grad_queries = query_blocks.reshape(row_len, width).astype(jnp.bfloat16)
    grad_keys = key_grad.reshape(row_len, width).astype(jnp.bfloat16)
    grad_values = value_grad.reshape(row_len, width).astype(jnp.bfloat16)
    grad_query = jnp.einsum("ld,le->de", normed, grad_queries, preferred_element_type=jnp.float32)
    grad_key = jnp.einsum("ld,le->de", normed, grad_keys, preferred_element_type=jnp.float32)
    grad_value = jnp.einsum("ld,le->de", normed, grad_values, preferred_element_type=jnp.float32)
    grad_normed = (
        jnp.einsum("le,de->ld", grad_queries, w_query, preferred_element_type=jnp.float32)
        + jnp.einsum("le,de->ld", grad_keys, w_key, preferred_element_type=jnp.float32)
        + jnp.einsum("le,de->ld", grad_values, w_value, preferred_element_type=jnp.float32)
    )
    grad_row_in, grad_gain_attn = norm_back(attn_hat, attn_std, gain_attn, grad_normed)
    grad_tokens = grad_mid_res + grad_row_in
    sum_query, sum_key, sum_value, sum_out, sum_gain_attn, sum_gain_sub, sum_gain_ffn = (
        lax.psum_scatter(grad_query, "row", scatter_dimension=0, tiled=True),
        lax.psum_scatter(grad_key, "row", scatter_dimension=0, tiled=True),
        lax.psum_scatter(grad_value, "row", scatter_dimension=0, tiled=True),
        lax.psum_scatter(grad_out, "row", scatter_dimension=0, tiled=True),
        lax.psum_scatter(grad_gain_attn, "row", scatter_dimension=0, tiled=True),
        lax.psum_scatter(grad_gain_sub, "row", scatter_dimension=0, tiled=True),
        lax.psum_scatter(grad_gain_ffn, "row", scatter_dimension=0, tiled=True),
    )
    return (
        output,
        grad_tokens,
        sum_query,
        sum_key,
        sum_value,
        sum_out,
        sum_up,
        sum_down,
        sum_gain_attn,
        sum_gain_sub,
        sum_gain_ffn,
        sum_gain_mid,
    )


def solution(mesh):
    rows, columns = mesh.shape["row"], mesh.shape["tp"]
    if columns == 2 and rows == 16:
        body = functools.partial(fused_body, (rows // 4, 2))
    else:
        body = general_body
    return jax.shard_map(
        body,
        mesh=mesh,
        in_specs=(
            P("row", None),
            P("row", None),
            P(),
            P("row", None),
            P(),
            P(),
            P(),
            P(),
            P(None, "tp"),
            P("tp", None),
            P(),
            P(),
            P(),
            P("tp"),
        ),
        out_specs=(
            P("row", None),
            P("row", None),
            P("row", None),
            P("row", None),
            P("row", None),
            P("row", None),
            P("row", "tp"),
            P("tp", "row"),
            P("row"),
            P("row"),
            P("row"),
            P(("tp", "row")),
        ),
        check_vma=False,
    )
```

```python
import functools

import jax
import jax.numpy as jnp
from jax import lax
from jax.experimental import pallas as pl
from jax.experimental.pallas import tpu as pltpu
from jax.sharding import PartitionSpec as P

MESH = pl.DeviceIdType.MESH
HEADS = 12
HEAD_DIM = 64
FF = 3072
EPS = 1e-05
F32 = jnp.float32
BF16 = jnp.bfloat16
LOG2E = 1.4426950408889634
CHUNK = 256
WINDOW = 512
PAIR_GROUP = 2
COLUMNS = 512
LANES = 128
MIB = 2**20


def dot(left, right, left_dim, right_dim):
    return lax.dot_general(
        left, right, (((left_dim,), (right_dim,)), ((), ())), preferred_element_type=F32
    )


def moments(value):
    mean = jnp.mean(value, -1, keepdims=True)
    centred = value - mean
    inv = lax.rsqrt(jnp.mean(centred * centred, -1, keepdims=True) + EPS)
    return centred * inv, inv


def norm_grad(hat, inv, gain, grad):
    scaled = grad * gain
    first = jnp.mean(scaled, -1, keepdims=True)
    second = jnp.mean(scaled * hat, -1, keepdims=True)
    return inv * (scaled - first - hat * second)


def repeat(tile, rows, columns):
    tall = jnp.concatenate([tile] * (rows // tile.shape[0]), 0)
    return jnp.concatenate([tall] * (columns // tile.shape[1]), 1)


def layer_kernel(
    places,
    dil,
    doc,
    ga_flat,
    gs_flat,
    gf_flat,
    gm_flat,
    tok_far,
    cot_far,
    wq_far,
    wk_far,
    wv_far,
    wo_far,
    wup_far,
    wdn_far,
    out_far,
    gtok_far,
    o_query,
    o_key,
    o_value,
    o_out,
    o_up,
    o_down,
    o_gain,
    tok,
    cot,
    wq,
    wk,
    wv,
    wo,
    wup_near,
    wdn,
    gtok,
    qs,
    ks,
    vs,
    att,
    mid,
    ffn_in,
    mid_out,
    grad_pre,
    ring_h,
    ring_d,
    gffn_own,
    gffn_got,
    ffp_own,
    ffp_got,
    weights_c,
    doc_col,
    lse,
    delta,
    stat_tile,
    stat_own,
    stat_got,
    gain_mid_sum,
    gain_own,
    gain_got,
    item_u,
    item_d,
    got_core,
    got_y,
    got_z,
    half_own,
    half_got,
    stat_sem,
    gffn_sem,
    ffp_sem,
    item_sem,
    gain_sem,
    half_sem,
    load_sem,
    store_sem,
):
    nz, ny = places
    row, tp = lax.axis_index("row"), lax.axis_index("tp")
    core = lax.rem(row, 2)
    y_at = lax.rem(row // 2, ny)
    z_at = row // (2 * ny)
    to_x = (row, 1 - tp)
    to_core = (row + 1 - 2 * core, tp)
    to_y = (row + 2 - 4 * y_at, tp)
    to_z = [
        (lax.rem(z_at + k, nz) * (2 * ny) + lax.rem(row, 2 * ny), tp) for k in range(1, nz)
    ]
    length, width = tok.shape
    half = wdn.shape[0]
    chunks = length // CHUNK
    pairs = width // LANES
    piece = width // (nz * ny * 2)

    ga, gs, gf, gm = [
        gain[...].reshape(1, gain.shape[0]) for gain in (ga_flat, gs_flat, gf_flat, gm_flat)
    ]
    loads = [
        pltpu.make_async_copy(far, near, load_sem.at[at])
        for at, (far, near) in enumerate(
            (
                (tok_far, tok),
                (wq_far, wq),
                (wk_far, wk),
                (wv_far, wv),
                (wo_far, wo),
                (wup_far, wup_near),
                (cot_far, cot),
                (wdn_far, wdn),
            )
        )
    ]
    for load in loads:
        load.start()
    barrier = pltpu.get_barrier_semaphore()
    partners = [to_x, to_core, to_y] + to_z
    for partner in partners:
        pl.semaphore_signal(barrier, inc=1, device_id=partner, device_id_type=MESH)

    def remote(src, dst, sems, at, partner):
        return pltpu.make_async_remote_copy(
            src_ref=src,
            dst_ref=dst,
            send_sem=sems.at[0, at],
            recv_sem=sems.at[1, at],
            device_id=partner,
            device_id_type=MESH,
        )

    lane = lax.broadcasted_iota(jnp.int32, (1, LANES), 1)
    low_lane = lane < HEAD_DIM
    lane_f = [low_lane.astype(F32), 1.0 - low_lane.astype(F32)]
    lane_b = [value.astype(BF16) for value in lane_f]

    row_at = lax.broadcasted_iota(jnp.int32, (16, LANES), 0)
    col_at = lax.broadcasted_iota(jnp.int32, (16, LANES), 1)
    for head in range(HEADS):
        row_count = jnp.zeros((16, LANES), F32)
        col_count = jnp.zeros((16, LANES), F32)
        for pattern in range(dil.shape[0]):
            last = dil[pattern] - 1
            row_count += (((row_at - head) & last) == 0).astype(F32)
            col_count += (((col_at - head) & last) == 0).astype(F32)
        weights_c[head] = jnp.minimum(row_count, col_count)
    for block in range(length // LANES):
        ids = doc[:, block * LANES : (block + 1) * LANES].astype(F32)
        doc_col[block * LANES : (block + 1) * LANES, :] = jnp.broadcast_to(ids, (LANES, LANES)).T
    doc_row = doc[...].astype(F32)
    bias = gtok
    value_t = ffp_own
    gain_mid_sum[...] = jnp.zeros_like(gain_mid_sum)
    gain_own[...] = jnp.zeros_like(gain_own)

    def project(at):
        rows = pl.ds(at * CHUNK, CHUNK)
        hat, _ = moments(tok[rows, :].astype(F32))
        value = (hat * ga).astype(BF16)
        qs[rows, :] = dot(value, wq[...], 1, 0).astype(BF16)
        ks[rows, :] = dot(value, wk[...], 1, 0).astype(BF16)
        vs[rows, :] = dot(value, wv[...], 1, 0).astype(BF16)

    def value_block(pair, block):
        if block < 3:
            return pl.ds(pl.multiple_of(pair * LANES, LANES), LANES), slice(
                block * CHUNK, (block + 1) * CHUNK
            )
        first = pl.multiple_of(width + (pair // 3) * LANES, LANES)
        return pl.ds(first, LANES), pl.ds(pl.multiple_of(lax.rem(pair, 3) * CHUNK, LANES), CHUNK)

    def attend(at):
        first = at * CHUNK
        start = max(0, first - WINDOW)
        span = first + CHUNK - start
        rows, keys = pl.ds(first, CHUNK), pl.ds(start, span)
        key_off = lax.broadcasted_iota(jnp.int32, (CHUNK, LANES), 0)
        query_off = lax.broadcasted_iota(jnp.int32, (CHUNK, LANES), 1)
        for block in range(span // CHUNK):
            low = start + block * CHUNK
            key_docs = doc_col[low : low + CHUNK, :]
            for side in range(CHUNK // LANES):
                begin = first + side * LANES
                allowed = key_docs == doc_row[:, begin : begin + LANES]
                allowed = allowed & (key_off + low <= query_off + begin)
                bias[block * CHUNK : (block + 1) * CHUNK, side * LANES : (side + 1) * LANES] = (
                    jnp.where(allowed, 0.0, -1e30)
                )

        def flip(pair, carry):
            lanes = pl.ds(pl.multiple_of(pair * LANES, LANES), LANES)
            value_t[value_block(pair, at)] = vs[rows, lanes].T
            return carry

        lax.fori_loop(0, pairs, flip, 0)
        ones = jnp.ones((16, CHUNK), BF16)

        def pair_step(step, carry):
            group = [step * PAIR_GROUP + at for at in range(PAIR_GROUP)]
            scores = []
            for pair in group:
                lanes = pl.ds(pl.multiple_of(pair * LANES, LANES), LANES)
                query = qs[rows, lanes]
                query_two = jnp.concatenate([query * lane_b[0], query * lane_b[1]], 0)
                scores.append(dot(ks[keys, lanes], query_two, 1, 1))
            for pair, score in zip(group, scores):
                lanes = pl.ds(pl.multiple_of(pair * LANES, LANES), LANES)
                parts = []
                for side in range(2):
                    power = score[:, side * CHUNK : (side + 1) * CHUNK]
                    power = power * (HEAD_DIM**-0.5 * LOG2E) + bias[0:span, 0:CHUNK]
                    top = jnp.max(power, 0, keepdims=True)
                    expo = jnp.exp2(power - top) * repeat(weights_c[2 * pair + side], span, CHUNK)
                    expo = expo.astype(BF16)
                    total = jnp.zeros((HEAD_DIM + 16, CHUNK), F32)
                    for block in range(span // CHUNK):
                        value = value_t[value_block(pair, start // CHUNK + block)]
                        value = value[side * HEAD_DIM : (side + 1) * HEAD_DIM, :]
                        total += dot(
                            jnp.concatenate([value, ones], 0),
                            expo[block * CHUNK : (block + 1) * CHUNK, :],
                            1,
                            0,
                        )
                    summed = total[HEAD_DIM : HEAD_DIM + 1, :]
                    parts.append(total[:HEAD_DIM, :] * (1.0 / summed))
                    lse[pair, side : side + 1, rows] = top + jnp.log2(summed)
                att[rows, lanes] = jnp.concatenate(parts, 0).T
            return carry

        lax.fori_loop(0, pairs // PAIR_GROUP, pair_step, 0)

    STRIP = 32

    def feed(at):
        rows = pl.ds(at * CHUNK, CHUNK)
        hat, _ = moments(att[rows, :])
        sub = (hat * gs).astype(BF16)
        mid_res = tok[rows, :].astype(F32) + dot(sub, wo[...], 1, 0)
        mid[rows, :] = mid_res
        hat, _ = moments(mid_res)
        value = (hat * gf).astype(BF16)
        ffn_in[rows, :] = value
        ring_h[...] = dot(value, wup_near[...].reshape(width, half), 1, 0)
        ring_d[...] = dot(cot[rows, :], wdn[...], 1, 1)

        def strip(index, carry):
            part = pl.ds(pl.multiple_of(index * STRIP, STRIP), STRIP)
            pre = ring_h[part, :]
            act = 0.5 * pre * (1.0 + lax.erf(pre * 0.7071067811865476))
            scaled = ring_d[part, :] * gm
            sums = [
                jnp.sum(value, -1, keepdims=True)
                for value in (act, act * act, scaled, scaled * act)
            ]
            tile = jnp.where(lane == 0, sums[0], jnp.where(lane == 1, sums[1], 0.0))
            tile = jnp.where(lane == 2, sums[2], jnp.where(lane == 3, sums[3], tile))
            stat_tile[part, :] = tile
            return carry

        lax.fori_loop(0, CHUNK // STRIP, strip, 0)
        stat_own[at] = stat_tile[...].T[0:8, :]
        remote(stat_own.at[at], stat_got.at[at], stat_sem, at, to_x).start()

    def gffn_copy(at):
        rows = pl.ds(at * CHUNK, CHUNK)
        return remote(gffn_own.at[rows], gffn_got.at[rows], gffn_sem, at, to_x)

    def ffp_copy(at):
        rows = pl.ds(at * CHUNK, CHUNK)
        return remote(ffp_own.at[rows], ffp_got.at[rows], ffp_sem, at, to_x)

    def feed_back(at):
        rows = pl.ds(at * CHUNK, CHUNK)
        remote(stat_own.at[at], stat_got.at[at], stat_sem, at, to_x).wait()
        both = stat_own[at] + stat_got[at]
        both = jnp.concatenate([both, jnp.zeros((LANES - 8, CHUNK), F32)], 0).T
        mean = both[:, 0:1] / FF
        inv = lax.rsqrt(both[:, 1:2] / FF - mean * mean + EPS)
        first = both[:, 2:3] / FF
        second = inv * (both[:, 3:4] - mean * both[:, 2:3]) / FF
        tile = jnp.where(lane == 0, mean, jnp.where(lane == 1, inv, 0.0))
        stat_tile[...] = jnp.where(lane == 2, first, jnp.where(lane == 3, second, tile))

        def strip(index, carry):
            part = pl.ds(pl.multiple_of(index * STRIP, STRIP), STRIP)
            target = pl.ds(pl.multiple_of(at * CHUNK + index * STRIP, STRIP), STRIP)
            stats = stat_tile[part, :]
            pre = ring_h[part, :]
            grad = ring_d[part, :]
            cdf = 0.5 * (1.0 + lax.erf(pre * 0.7071067811865476))
            slope = cdf + pre * (jnp.exp2(pre * pre * (-0.5 * LOG2E)) * 0.3989422804014327)
            hat = (pre * cdf - stats[:, 0:1]) * stats[:, 1:2]
            mid_out[target, :] = (hat * gm).astype(BF16)
            gain_part = grad * hat
            gain_mid_sum[...] += sum(
                gain_part[8 * i : 8 * i + 8, :] for i in range(STRIP // 8)
            )
            back = stats[:, 1:2] * (grad * gm - stats[:, 2:3] - hat * stats[:, 3:4])
            grad_pre[target, :] = (back * slope).astype(BF16)
            return carry

        lax.fori_loop(0, CHUNK // STRIP, strip, 0)
        gffn_own[rows, :] = dot(grad_pre[rows, :], wup_near[...].reshape(width, half), 1, 1).astype(BF16)
        gffn_copy(at).start()

    for at in range(chunks + 1):
        if at == 0:
            for load in loads[:4]:
                load.wait()
        if at < chunks:
            project(at)
            attend(at)
        if at == 0:
            for load in loads[4:]:
                load.wait()
            pl.semaphore_wait(barrier, len(partners))
        if at >= 1:
            feed_back(at - 1)
        if at < chunks:
            feed(at)

    item_a = wup_near
    items = [(item, part) for item in (item_u, item_d, item_a) for part in range(half // COLUMNS)]

    def item_part(which):
        return items[which][0], slice(items[which][1] * COLUMNS, (items[which][1] + 1) * COLUMNS)

    def core_slot(which):
        return got_core.at[which % 6]

    def y_slot(which):
        return got_y.at[which % 6]

    def core_copy(which):
        item, columns = item_part(which)
        return remote(
            item.at[:, :, 1 - core, :, columns], core_slot(which), item_sem, 8 * which, to_core
        )

    def y_copy(which):
        item, columns = item_part(which)
        return remote(
            item.at[:, 1 - y_at, core, :, columns],
            y_slot(which),
            item_sem,
            8 * which + 1,
            to_y,
        )

    def z_copies(which):
        item, columns = item_part(which)
        return [
            remote(
                item.at[lax.rem(z_at + k, nz), y_at, core, :, columns],
                got_z.at[which, k - 1],
                item_sem,
                8 * which + 1 + k,
                to_z[k - 1],
            )
            for k in range(1, nz)
        ]

    def start_core(which):
        core_copy(which).start()

    def start_y(which):
        core_copy(which).wait()
        item, columns = item_part(which)

        def add(index, carry):
            z_to, y_to = index // ny, lax.rem(index, ny)
            total = item[z_to, y_to, core, :, columns].astype(F32)
            total += got_core[which % 6, z_to, y_to].astype(F32)
            item[z_to, y_to, core, :, columns] = total.astype(BF16)
            return carry

        lax.fori_loop(0, nz * ny, add, 0)
        y_copy(which).start()

    def start_z(which):
        y_copy(which).wait()
        item, columns = item_part(which)

        def add(z_to, carry):
            total = item[z_to, y_at, core, :, columns].astype(F32)
            total += got_y[which % 6, z_to].astype(F32)
            item[z_to, y_at, core, :, columns] = total.astype(BF16)
            return carry

        lax.fori_loop(0, nz, add, 0)
        for copy in z_copies(which):
            copy.start()

    def finish(which):
        for copy in z_copies(which):
            copy.wait()
        item, columns = item_part(which)
        total = item[z_at, y_at, core, :, columns].astype(F32)
        for k in range(1, nz):
            total = total + got_z[which, k - 1].astype(F32)
        if which < 3:
            o_up[:, columns] = total
        elif which < 6:
            o_down[:, columns] = total
        else:
            half_own[:, columns] = total.astype(BF16)

    def outer(item, left, right, part):
        columns = slice(part * COLUMNS, (part + 1) * COLUMNS)
        product = dot(left[...], right[:, columns], 0, 0).astype(BF16)
        item[:, :, :, :, columns] = product.reshape(nz, ny, 2, piece, COLUMNS)

    gain_stage = [
        remote(gain_own, gain_got.at[at], gain_sem, at, partner)
        for at, partner in ((0, to_core), (1, to_y))
    ]
    gain_last = [
        remote(gain_own, gain_got.at[1 + k], gain_sem, 1 + k, to_z[k - 1]) for k in range(1, nz)
    ]

    def gain_add(at):
        gain_stage[at].wait()
        gain_own[...] += gain_got[at]

    for part in range(3):
        outer(item_u, ffn_in, grad_pre, part)
        start_core(part)
    start_y(0)
    for part in range(3):
        outer(item_d, cot, mid_out, part)
        start_core(3 + part)
        if part < 2:
            start_y(1 + part)
    start_y(3)
    for at in range(chunks):
        rows = pl.ds(at * CHUNK, CHUNK)
        ffp_own[rows, :] = dot(mid_out[rows, :], wdn[...], 1, 0).astype(BF16)
        ffp_copy(at).start()
    start_y(4)
    start_z(0)

    grad_res = ffn_in
    grad_att = grad_pre
    sub_out = gffn_own
    normed = gffn_got
    for at in range(chunks):
        rows = pl.ds(at * CHUNK, CHUNK)
        gffn_copy(at).wait()
        grad = gffn_own[rows, :].astype(F32) + gffn_got[rows, :].astype(F32)
        hat, inv = moments(mid[rows, :])
        gain_own[2:3, :] += jnp.sum(grad * hat, 0, keepdims=True)
        grad_mid = cot[rows, :].astype(F32) + norm_grad(hat, inv, gf, grad)
        gtok[rows, :] = grad_mid
        grad_low = grad_mid.astype(BF16)
        grad_res[rows, :] = grad_low
        grad = dot(grad_low, wo[...], 1, 1)
        hat, inv = moments(att[rows, :])
        sub_out[rows, :] = (hat * gs).astype(BF16)
        gain_own[1:2, :] += jnp.sum(grad * hat, 0, keepdims=True)
        grad_att[rows, width : 2 * width] = norm_grad(hat, inv, gs, grad).astype(BF16)
        hat, _ = moments(tok[rows, :].astype(F32))
        normed[rows, :] = (hat * ga).astype(BF16)
        if at == 0:
            start_y(5)
            start_z(1)
        if at == 1:
            start_z(2)
        if at == 2:
            finish(0)
        if at == 3:
            start_z(3)
            finish(1)
    for side in range(2):
        columns = slice(side * width, (side + 1) * width)
        gain_own[3 + side : 4 + side, :] = jnp.sum(gain_mid_sum[:, columns], 0, keepdims=True)
    gain_stage[0].start()

    def mask_ref(which):
        ring = ring_h if which < 6 else ring_d
        return ring, slice((which % 6) * CHUNK, (which % 6 + 1) * CHUNK)

    tiles = [
        (key, query)
        for key in range(chunks)
        for query in range(key, min(chunks, key + WINDOW // CHUNK + 1))
    ]
    key_off = lax.broadcasted_iota(jnp.int32, (CHUNK, LANES), 0)
    query_off = lax.broadcasted_iota(jnp.int32, (CHUNK, LANES), 1)
    for which, (key, query) in enumerate(tiles):
        ring, columns = mask_ref(which)
        key_docs = doc_col[key * CHUNK : (key + 1) * CHUNK, :]
        for block in range(CHUNK // LANES):
            low = query * CHUNK + block * LANES
            allowed = key_docs == doc_row[:, low : low + LANES]
            if key == query:
                allowed = allowed & (key_off + key * CHUNK <= query_off + low)
            begin = columns.start + block * LANES
            ring[:, begin : begin + LANES] = jnp.where(allowed, 0.0, -1e30)

    select = (lax.broadcasted_iota(jnp.int32, (8, LANES), 1) // HEAD_DIM) == (
        lax.broadcasted_iota(jnp.int32, (8, LANES), 0)
    )
    select = select.astype(F32).astype(BF16)
    half_width = width // 2

    dq_columns = slice(3 * CHUNK, half)

    def dq_part(block):
        low = (block % 2) * LANES
        begin = 3 * CHUNK + (block // 2) * CHUNK
        return slice(low, low + LANES), slice(begin, begin + CHUNK)

    def pair_back(step, carry):
        pair = lax.rem(tp * (pairs // 2) + step, pairs)
        low = pl.multiple_of(pair * LANES, LANES)
        lanes = pl.ds(low, LANES)
        upper = pl.ds(pl.multiple_of(width + low, LANES), LANES)
        product = grad_att[:, upper].astype(F32) * att[:, lanes]
        high = product.astype(BF16)
        rest = (product - high.astype(F32)).astype(BF16)
        delta[...] = dot(select, high, 1, 1) + dot(select, rest, 1, 1)
        ring_d[0:LANES, dq_columns] = jnp.zeros((LANES, half - 3 * CHUNK), F32)
        ring_d[LANES:CHUNK, dq_columns] = jnp.zeros((LANES, half - 3 * CHUNK), F32)
        for key_block in range(chunks):
            keys = slice(key_block * CHUNK, (key_block + 1) * CHUNK)
            key, value = ks[keys, lanes], vs[keys, lanes]
            key_t = key.T
            dk_sum = jnp.zeros((CHUNK, LANES), F32)
            dv_sum = jnp.zeros((CHUNK, LANES), F32)
            for which, (key_at, query_at) in enumerate(tiles):
                if key_at != key_block:
                    continue
                ring, columns = mask_ref(which)
                queries = slice(query_at * CHUNK, (query_at + 1) * CHUNK)
                query = qs[queries, lanes]
                grad_out = grad_att[queries, upper]
                query_two = jnp.concatenate([query * lane_b[0], query * lane_b[1]], 0)
                grad_two = jnp.concatenate([grad_out * lane_b[0], grad_out * lane_b[1]], 0)
                scores = dot(key, query_two, 1, 1)
                grad_prob = dot(value, grad_two, 1, 1)
                probs, grad_scores, grad_queries = [], [], []
                for side in range(2):
                    mine = slice(side * CHUNK, (side + 1) * CHUNK)
                    power = scores[:, mine] * (HEAD_DIM**-0.5 * LOG2E) + ring[:, columns]
                    power = power - lse[pair, side : side + 1, queries]
                    prob = jnp.exp2(power) * repeat(weights_c[2 * pair + side], CHUNK, CHUNK)
                    probs.append(prob.astype(BF16))
                    grad_score = prob * (grad_prob[:, mine] - delta[side : side + 1, queries])
                    grad_score = grad_score.astype(BF16)
                    grad_scores.append(grad_score)
                    grad_queries.append(
                        dot(key_t[side * HEAD_DIM : (side + 1) * HEAD_DIM, :], grad_score, 1, 0)
                    )
                dv_sum += dot(jnp.concatenate(probs, 1), grad_two, 1, 0)
                dk_sum += dot(jnp.concatenate(grad_scores, 1), query_two, 1, 0)
                part = dq_part(query_at)
                ring_d[part] += jnp.concatenate(grad_queries, 0)
            mid_out[keys, upper] = (dk_sum * HEAD_DIM**-0.5).astype(BF16)
            grad_pre[keys, lanes] = dv_sum.astype(BF16)
        for block in range(chunks):
            grad = (ring_d[dq_part(block)] * HEAD_DIM**-0.5).astype(BF16)
            mid_out[block * CHUNK : (block + 1) * CHUNK, lanes] = grad.T

        def own_grads(part):
            offset = pl.multiple_of(tp * half_width + part * LANES, LANES)
            offset_up = pl.multiple_of(width + tp * half_width + part * LANES, LANES)
            right = [
                mid_out[:, pl.ds(offset, LANES)],
                mid_out[:, pl.ds(offset_up, LANES)],
                grad_pre[:, pl.ds(offset, LANES)],
            ]
            grad = dot(normed[...], jnp.concatenate(right, 1), 0, 0).astype(BF16)
            low = part * COLUMNS
            item_a[:, :, :, :, low : low + 3 * LANES] = grad.reshape(
                nz, ny, 2, piece, 3 * LANES
            )
            grad = dot(sub_out[...], grad_res[:, pl.ds(offset, LANES)], 0, 0).astype(BF16)
            item_a[:, :, :, :, low + 3 * LANES : low + COLUMNS] = grad.reshape(
                nz, ny, 2, piece, LANES
            )
            start_core(6 + part)

        @pl.when(step == 0)
        def _():
            gain_add(0)
            gain_stage[1].start()
            start_z(4)
            finish(2)
            own_grads(0)

        @pl.when(step == 1)
        def _():
            gain_add(1)
            for copy in gain_last:
                copy.start()
            start_z(5)
            finish(3)
            start_y(6)
            own_grads(1)

        @pl.when(step == 2)
        def _():
            finish(4)
            start_y(7)
            own_grads(2)

        @pl.when(step == 3)
        def _():
            finish(5)
            start_z(6)
            start_y(8)

        @pl.when(step == 4)
        def _():
            start_z(7)

        @pl.when(step == 5)
        def _():
            finish(6)

        return carry

    lax.fori_loop(0, pairs, pair_back, 0)

    stores = []

    def store(near, far, at):
        copy = pltpu.make_async_copy(near, far, store_sem.at[at])
        copy.start()
        stores.append(copy)

    for at in range(chunks):
        rows = pl.ds(at * CHUNK, CHUNK)
        grad = dot(mid_out[rows, 0:width], wq[...], 1, 1)
        grad += dot(mid_out[rows, width : 2 * width], wk[...], 1, 1)
        grad += dot(grad_pre[rows, 0:width], wv[...], 1, 1)
        hat, inv = moments(tok[rows, :].astype(F32))
        gtok[rows, :] += norm_grad(hat, inv, ga, grad)
        store(gtok.at[rows], gtok_far.at[rows], at)
        if at == 0:
            start_z(8)
    finish(7)
    finish(8)
    half_copy = remote(half_own, half_got, half_sem, 0, to_x)
    half_copy.start()

    for copy in gain_last:
        copy.wait()
    total = gain_own[...]
    for k in range(1, nz):
        total = total + gain_got[1 + k]
    o_gain[0:8, :] = pltpu.roll(total, lax.rem(width - piece * row, width), 1)[:, :LANES]
    per_row = 2 * piece
    o_gain[8:16, :] = pltpu.roll(total, lax.rem(2 * width - per_row * row, width), 1)[:, :LANES]

    for at in range(chunks):
        rows = pl.ds(at * CHUNK, CHUNK)
        ffp_copy(at).wait()
        total = ffp_own[rows, :].astype(F32) + ffp_got[rows, :].astype(F32)
        ffp_own[rows, :] = (mid[rows, :] + total).astype(BF16)
        store(ffp_own.at[rows], out_far.at[rows], chunks + at)

    half_copy.wait()
    mine_at = pl.multiple_of(tp * half_width, LANES)
    other_at = pl.multiple_of((1 - tp) * half_width, LANES)
    for part in range(pairs // 2):
        mine, other = (
            pl.ds(pl.multiple_of(begin + part * LANES, LANES), LANES)
            for begin in (mine_at, other_at)
        )
        for index, target in enumerate((o_query, o_key, o_value, o_out)):
            low = part * COLUMNS + index * LANES
            target[:, mine] = half_own[:, low : low + LANES].astype(F32)
            target[:, other] = half_got[:, low : low + LANES].astype(F32)
    own_rows = pl.ds(pl.multiple_of(piece * row, 16), piece)
    product = wq[own_rows, :].astype(F32) * o_query[...]
    product += wk[own_rows, :].astype(F32) * o_key[...]
    product += wv[own_rows, :].astype(F32) * o_value[...]
    total = jnp.broadcast_to(jnp.sum(product, -1, keepdims=True), (piece, LANES))
    total = jnp.concatenate([total, jnp.zeros((LANES - piece, LANES), F32)], 0).T
    gain = pltpu.roll(repeat(ga, 8, width), lax.rem(width - piece * row, width), 1)
    o_gain[0:1, :] = total[0:1, :] / gain[0:1, :LANES]
    for copy in stores:
        copy.wait()


def write_kernel(places, *refs):
    far_in, gain_in, far_out, gains_out = refs[:8], refs[8], refs[9:17], refs[17:21]
    near, sems = refs[21:29], refs[29]
    g_attn, g_sub, g_ffn, g_mid = gains_out
    nz, ny = places
    row = lax.axis_index("row")
    width = far_in[0].shape[1]
    piece = far_in[2].shape[0]
    steps = []
    for at in range(8):
        length = far_in[at].shape[0]
        size = CHUNK if length > CHUNK else length
        for begin in range(0, length, size):
            rows, which = pl.ds(begin, size), len(steps)
            steps.append(
                (
                    pltpu.make_async_copy(
                        far_in[at].at[rows], near[at].at[rows], sems.at[0, which]
                    ),
                    pltpu.make_async_copy(
                        near[at].at[rows], far_out[at].at[rows], sems.at[1, which]
                    ),
                )
            )
    for load, _ in steps:
        load.start()
    tile = gain_in[...]
    g_attn[...] = tile[0, :piece]
    g_sub[...] = tile[1, :piece]
    g_ffn[...] = tile[2, :piece]
    later = (2 * piece * row) // width
    g_mid[...] = jnp.where(later == 0, tile[11, : 2 * piece], tile[12, : 2 * piece])
    for load, save in steps:
        load.wait()
        save.start()
    for _, save in steps:
        save.wait()


def fused_body(places, *args):
    (tokens, doc_ids, dilations, cotangent, w_query, w_key, w_value, w_out, w_up, w_down) = args[:10]
    gains = args[10:]
    nz, ny = places
    length, width = tokens.shape
    half = w_up.shape[1]
    piece = width // (2 * nz * ny)
    chunks = length // CHUNK
    vmem = pl.BlockSpec(memory_space=pltpu.VMEM)
    smem = pl.BlockSpec(memory_space=pltpu.SMEM)
    far = pl.BlockSpec(memory_space=pl.ANY)
    shape = jax.ShapeDtypeStruct
    low = functools.partial(pltpu.VMEM, dtype=BF16)
    full = functools.partial(pltpu.VMEM, dtype=F32)
    rows_low, rows_full = low((length, width)), full((length, width))
    item = low((nz, ny, 2, piece, half))
    square = low((width, width))
    count = 3 * half // COLUMNS
    dma = lambda number: pltpu.SemaphoreType.DMA((2, number))
    big = [
        shape((length, width), BF16),
        shape((length, width), F32),
        shape((piece, width), F32),
        shape((piece, width), F32),
        shape((piece, width), F32),
        shape((piece, width), F32),
        shape((piece, half), F32),
        shape((piece, half), F32),
    ]
    results = pl.pallas_call(
        functools.partial(layer_kernel, places),
        out_shape=big + [shape((16, LANES), F32)],
        in_specs=[smem] + [vmem] * 5 + [far] * 8,
        out_specs=[far] * 2 + [vmem] * 7,
        scratch_shapes=[
            rows_low,
            rows_low,
            square,
            square,
            square,
            square,
            item,
            low((half, width)),
            rows_full,
            rows_low,
            rows_low,
            rows_low,
            rows_full,
            rows_full,
            rows_low,
            low((length, half)),
            low((length, half)),
            full((CHUNK, half)),
            full((CHUNK, half)),
            rows_low,
            rows_low,
            rows_low,
            rows_low,
            full((HEADS, 16, LANES)),
            full((length, LANES)),
            full((width // LANES, 2, length)),
            full((8, length)),
            full((CHUNK, LANES)),
            full((chunks, 8, CHUNK)),
            full((chunks, 8, CHUNK)),
            full((8, half)),
            full((8, width)),
            full((1 + nz, 8, width)),
            item,
            item,
            low((6, nz, ny, piece, COLUMNS)),
            low((6, nz, piece, COLUMNS)),
            low((count, nz - 1, piece, COLUMNS)),
            low((piece, half)),
            low((piece, half)),
            dma(chunks),
            dma(chunks),
            dma(chunks),
            dma(8 * count),
            dma(1 + nz),
            dma(1),
            pltpu.SemaphoreType.DMA((8,)),
            pltpu.SemaphoreType.DMA((2 * chunks,)),
        ],
        compiler_params=pltpu.CompilerParams(
            collective_id=0, has_side_effects=True, vmem_limit_bytes=63 * MIB
        ),
        name="layer",
    )(
        dilations,
        doc_ids.reshape(1, length),
        *gains,
        tokens,
        cotangent,
        w_query,
        w_key,
        w_value,
        w_out,
        w_up.reshape(nz, ny, 2, piece, half),
        w_down,
    )
    flat = shape((piece,), F32)
    moves = 2 * (length // CHUNK) + 6
    final = pl.pallas_call(
        functools.partial(write_kernel, places),
        out_shape=big + [flat, flat, flat, shape((2 * piece,), F32)],
        in_specs=[far] * 8 + [vmem],
        out_specs=[far] * 8 + [vmem] * 4,
        scratch_shapes=[pltpu.VMEM(one.shape, one.dtype) for one in big]
        + [pltpu.SemaphoreType.DMA((2, moves))],
        compiler_params=pltpu.CompilerParams(vmem_limit_bytes=63 * MIB),
        name="write",
    )(*results)
    return (*final[:7], final[7].T, *final[8:])


def norm_parts(value):
    row_mean = jnp.mean(value, -1, keepdims=True)
    centred = value - row_mean
    inv_std = lax.rsqrt(jnp.mean(centred * centred, -1, keepdims=True) + EPS)
    return (centred * inv_std, inv_std)


def norm_back(normed_hat, inv_std, gain, grad):
    scaled = grad * gain
    grad_value = inv_std * (
        scaled
        - jnp.mean(scaled, -1, keepdims=True)
        - normed_hat * jnp.mean(scaled * normed_hat, -1, keepdims=True)
    )
    return (grad_value, jnp.sum(grad * normed_hat, 0))


def selection(dilations, positions):
    head_ids = jnp.arange(HEADS, dtype=jnp.int32)
    left_side = positions[None, None, :] % dilations[:, None, None]
    right_side = head_ids[None, :, None] % dilations[:, None, None]
    return (left_side == right_side).astype(jnp.float32)


def pattern_weights(dilations, doc_row, query_pos, query_docs):
    key_pos = jnp.arange(doc_row.shape[0], dtype=jnp.int32)
    counts = jnp.einsum(
        "phi,phj->hij", selection(dilations, query_pos), selection(dilations, key_pos)
    )
    allowed = (query_pos[:, None] >= key_pos[None, :]) & (query_docs[:, None] == doc_row[None, :])
    return counts * allowed.astype(jnp.float32)[None]


def attn_forward(dilations, doc_row, key_heads, value_heads, query_block, query_pos, query_docs):
    score_scale = HEAD_DIM ** (-0.5)
    scores = (
        jnp.einsum("ihe,jhe->hij", query_block, key_heads, preferred_element_type=jnp.float32)
        * score_scale
    )
    weights_mult = pattern_weights(dilations, doc_row, query_pos, query_docs)
    masked = jnp.where(weights_mult > 0, scores, -1e30)
    row_max = jnp.max(masked, -1, keepdims=True)
    expo = weights_mult * jnp.exp(masked - row_max)
    totals = jnp.sum(expo, -1, keepdims=True)
    attn_prob = (expo / totals).astype(jnp.bfloat16)
    out_block = jnp.einsum(
        "hij,jhe->ihe", attn_prob, value_heads, preferred_element_type=jnp.float32
    )
    return (out_block, row_max[..., 0] + jnp.log(totals[..., 0]))


def attn_backward(
    dilations,
    doc_row,
    key_heads,
    value_heads,
    query_block,
    query_pos,
    query_docs,
    lse_block,
    grad_block,
):
    score_scale = HEAD_DIM ** (-0.5)
    scores = (
        jnp.einsum("ihe,jhe->hij", query_block, key_heads, preferred_element_type=jnp.float32)
        * score_scale
    )
    weights_mult = pattern_weights(dilations, doc_row, query_pos, query_docs)
    attn_full = weights_mult * jnp.exp(scores - lse_block[:, :, None])
    attn_low = attn_full.astype(jnp.bfloat16)
    value_part = jnp.einsum(
        "hij,ihe->jhe", attn_low, grad_block, preferred_element_type=jnp.float32
    )
    grad_prob = jnp.einsum(
        "ihe,jhe->hij", grad_block, value_heads, preferred_element_type=jnp.float32
    )
    row_delta = jnp.sum(attn_full * grad_prob, -1, keepdims=True)
    grad_scores = (attn_full * (grad_prob - row_delta)).astype(jnp.bfloat16)
    query_grad = (
        jnp.einsum("hij,jhe->ihe", grad_scores, key_heads, preferred_element_type=jnp.float32)
        * score_scale
    )
    key_part = (
        jnp.einsum("hij,ihe->jhe", grad_scores, query_block, preferred_element_type=jnp.float32)
        * score_scale
    )
    return (query_grad, key_part, value_part)


def general_body(
    tokens,
    doc_ids,
    dilations,
    cotangent,
    w_query,
    w_key,
    w_value,
    w_out,
    w_up,
    w_down,
    gain_attn,
    gain_sub,
    gain_ffn,
    gain_mid,
):
    row_len = tokens.shape[0]
    width = tokens.shape[1]
    block_rows = min(512, row_len)
    block_count = row_len // block_rows
    doc_row = doc_ids.reshape(row_len)
    row_in = tokens.astype(jnp.float32)
    attn_hat, attn_std = norm_parts(row_in)
    normed = (attn_hat * gain_attn).astype(jnp.bfloat16)
    keys_low = jnp.dot(normed, w_key, preferred_element_type=jnp.float32).astype(jnp.bfloat16)
    values_low = jnp.dot(normed, w_value, preferred_element_type=jnp.float32).astype(jnp.bfloat16)
    key_heads = keys_low.reshape(row_len, HEADS, HEAD_DIM)
    value_heads = values_low.reshape(row_len, HEADS, HEAD_DIM)
    queries = jnp.dot(normed, w_query, preferred_element_type=jnp.float32).astype(jnp.bfloat16)
    query_heads = queries.reshape(row_len, HEADS, HEAD_DIM)

    def attend(block_index):
        offset = block_index * block_rows
        query_block = lax.dynamic_slice_in_dim(query_heads, offset, block_rows, 0)
        query_pos = offset + jnp.arange(block_rows, dtype=jnp.int32)
        query_docs = lax.dynamic_slice_in_dim(doc_row, offset, block_rows, 0)
        return attn_forward(
            dilations, doc_row, key_heads, value_heads, query_block, query_pos, query_docs
        )

    out_blocks, log_sums = lax.map(attend, jnp.arange(block_count))
    attended = out_blocks.reshape(row_len, width)
    sub_hat, sub_std = norm_parts(attended)
    sub_out = (sub_hat * gain_sub).astype(jnp.bfloat16)
    mid_res = row_in + jnp.dot(sub_out, w_out, preferred_element_type=jnp.float32)
    ffn_hat, ffn_std = norm_parts(mid_res)
    ffn_in = (ffn_hat * gain_ffn).astype(jnp.bfloat16)
    hidden_pre = jnp.dot(ffn_in, w_up, preferred_element_type=jnp.float32)
    hidden_act = jax.nn.gelu(hidden_pre, approximate=False)
    sum_first, sum_second = lax.psum(
        (jnp.sum(hidden_act, -1), jnp.sum(hidden_act * hidden_act, -1)), "tp"
    )
    mid_mean = sum_first[:, None] / FF
    mid_std = lax.rsqrt(sum_second[:, None] / FF - mid_mean * mid_mean + EPS)
    mid_hat = (hidden_act - mid_mean) * mid_std
    mid_out = (mid_hat * gain_mid).astype(jnp.bfloat16)
    ffn_part = jnp.dot(mid_out, w_down, preferred_element_type=jnp.float32)
    ffn_total = lax.psum(ffn_part, "tp")
    output = (mid_res + ffn_total).astype(jnp.bfloat16)
    grad_down = jnp.einsum("lf,ld->fd", mid_out, cotangent, preferred_element_type=jnp.float32)
    grad_mid_out = jnp.einsum("ld,fd->lf", cotangent, w_down, preferred_element_type=jnp.float32)
    grad_gain_mid = jnp.sum(grad_mid_out * mid_hat, 0)
    scaled = grad_mid_out * gain_mid
    back_first, back_second = lax.psum((jnp.sum(scaled, -1), jnp.sum(scaled * mid_hat, -1)), "tp")
    grad_act = mid_std * (scaled - back_first[:, None] / FF - mid_hat * back_second[:, None] / FF)
    gelu_pull = jax.vjp(lambda value: jax.nn.gelu(value, approximate=False), hidden_pre)[1]
    grad_pre = gelu_pull(grad_act)[0].astype(jnp.bfloat16)
    grad_up = jnp.einsum("ld,lf->df", ffn_in, grad_pre, preferred_element_type=jnp.float32)
    sum_up, sum_down, sum_gain_mid = (
        lax.psum_scatter(grad_up, "row", scatter_dimension=0, tiled=True),
        lax.psum_scatter(grad_down, "row", scatter_dimension=1, tiled=True),
        lax.psum_scatter(grad_gain_mid, "row", scatter_dimension=0, tiled=True),
    )
    grad_ffn_part = jnp.einsum("lf,df->ld", grad_pre, w_up, preferred_element_type=jnp.float32)
    grad_ffn_in = lax.psum(grad_ffn_part, "tp")
    grad_mid_in, grad_gain_ffn = norm_back(ffn_hat, ffn_std, gain_ffn, grad_ffn_in)
    grad_mid_res = cotangent.astype(jnp.float32) + grad_mid_in
    grad_res_low = grad_mid_res.astype(jnp.bfloat16)
    grad_out = jnp.einsum("ld,le->de", sub_out, grad_res_low, preferred_element_type=jnp.float32)
    grad_sub_out = jnp.einsum("le,de->ld", grad_res_low, w_out, preferred_element_type=jnp.float32)
    grad_attended, grad_gain_sub = norm_back(sub_hat, sub_std, gain_sub, grad_sub_out)
    grad_att_low = grad_attended.astype(jnp.bfloat16)
    grad_heads = grad_att_low.reshape(row_len, HEADS, HEAD_DIM)

    def attend_back(running, block_index):
        key_sum, value_sum = running
        offset = block_index * block_rows
        query_block = lax.dynamic_slice_in_dim(query_heads, offset, block_rows, 0)
        query_pos = offset + jnp.arange(block_rows, dtype=jnp.int32)
        query_docs = lax.dynamic_slice_in_dim(doc_row, offset, block_rows, 0)
        grad_block = lax.dynamic_slice_in_dim(grad_heads, offset, block_rows, 0)
        query_grad, key_part, value_part = attn_backward(
            dilations,
            doc_row,
            key_heads,
            value_heads,
            query_block,
            query_pos,
            query_docs,
            log_sums[block_index],
            grad_block,
        )
        return ((key_sum + key_part, value_sum + value_part), query_grad)

    zero_heads = jnp.zeros((row_len, HEADS, HEAD_DIM), jnp.float32)
    (key_grad, value_grad), query_blocks = lax.scan(
        attend_back, (zero_heads, zero_heads), jnp.arange(block_count)
    )
    grad_queries = query_blocks.reshape(row_len, width).astype(jnp.bfloat16)
    grad_keys = key_grad.reshape(row_len, width).astype(jnp.bfloat16)
    grad_values = value_grad.reshape(row_len, width).astype(jnp.bfloat16)
    grad_query = jnp.einsum("ld,le->de", normed, grad_queries, preferred_element_type=jnp.float32)
    grad_key = jnp.einsum("ld,le->de", normed, grad_keys, preferred_element_type=jnp.float32)
    grad_value = jnp.einsum("ld,le->de", normed, grad_values, preferred_element_type=jnp.float32)
    grad_normed = (
        jnp.einsum("le,de->ld", grad_queries, w_query, preferred_element_type=jnp.float32)
        + jnp.einsum("le,de->ld", grad_keys, w_key, preferred_element_type=jnp.float32)
        + jnp.einsum("le,de->ld", grad_values, w_value, preferred_element_type=jnp.float32)
    )
    grad_row_in, grad_gain_attn = norm_back(attn_hat, attn_std, gain_attn, grad_normed)
    grad_tokens = grad_mid_res + grad_row_in
    sum_query, sum_key, sum_value, sum_out, sum_gain_attn, sum_gain_sub, sum_gain_ffn = (
        lax.psum_scatter(grad_query, "row", scatter_dimension=0, tiled=True),
        lax.psum_scatter(grad_key, "row", scatter_dimension=0, tiled=True),
        lax.psum_scatter(grad_value, "row", scatter_dimension=0, tiled=True),
        lax.psum_scatter(grad_out, "row", scatter_dimension=0, tiled=True),
        lax.psum_scatter(grad_gain_attn, "row", scatter_dimension=0, tiled=True),
        lax.psum_scatter(grad_gain_sub, "row", scatter_dimension=0, tiled=True),
        lax.psum_scatter(grad_gain_ffn, "row", scatter_dimension=0, tiled=True),
    )
    return (
        output,
        grad_tokens,
        sum_query,
        sum_key,
        sum_value,
        sum_out,
        sum_up,
        sum_down,
        sum_gain_attn,
        sum_gain_sub,
        sum_gain_ffn,
        sum_gain_mid,
    )


def solution(mesh):
    rows, columns = mesh.shape["row"], mesh.shape["tp"]
    if columns == 2 and rows == 16:
        body = functools.partial(fused_body, (rows // 4, 2))
    else:
        body = general_body
    return jax.shard_map(
        body,
        mesh=mesh,
        in_specs=(
            P("row", None),
            P("row", None),
            P(),
            P("row", None),
            P(),
            P(),
            P(),
            P(),
            P(None, "tp"),
            P("tp", None),
            P(),
            P(),
            P(),
            P("tp"),
        ),
        out_specs=(
            P("row", None),
            P("row", None),
            P("row", None),
            P("row", None),
            P("row", None),
            P("row", None),
            P("row", "tp"),
            P("tp", "row"),
            P("row"),
            P("row"),
            P("row"),
            P(("tp", "row")),
        ),
        check_vma=False,
    )
```

```python
import functools

import jax
import jax.numpy as jnp
from jax import lax
from jax.experimental import pallas as pl
from jax.experimental.pallas import tpu as pltpu
from jax.sharding import PartitionSpec as P

MESH = pl.DeviceIdType.MESH
HEADS = 12
HEAD_DIM = 64
FF = 3072
EPS = 1e-05
F32 = jnp.float32
BF16 = jnp.bfloat16
LOG2E = 1.4426950408889634
CHUNK = 256
WINDOW = 512
PAIR_GROUP = 2
COLUMNS = 512
LANES = 128
MIB = 2**20


def dot(left, right, left_dim, right_dim):
    return lax.dot_general(
        left, right, (((left_dim,), (right_dim,)), ((), ())), preferred_element_type=F32
    )


def moments(value):
    mean = jnp.mean(value, -1, keepdims=True)
    centred = value - mean
    inv = lax.rsqrt(jnp.mean(centred * centred, -1, keepdims=True) + EPS)
    return centred * inv, inv


def norm_grad(hat, inv, gain, grad):
    scaled = grad * gain
    first = jnp.mean(scaled, -1, keepdims=True)
    second = jnp.mean(scaled * hat, -1, keepdims=True)
    return inv * (scaled - first - hat * second)


def repeat(tile, rows, columns):
    tall = jnp.concatenate([tile] * (rows // tile.shape[0]), 0)
    return jnp.concatenate([tall] * (columns // tile.shape[1]), 1)


def layer_kernel(
    places,
    dil,
    doc,
    ga_flat,
    gs_flat,
    gf_flat,
    gm_flat,
    tok_far,
    cot_far,
    wq_far,
    wk_far,
    wv_far,
    wo_far,
    wup_far,
    wdn_far,
    out_far,
    gtok_far,
    o_query,
    o_key,
    o_value,
    o_out,
    o_up,
    o_down,
    o_gain,
    tok,
    cot,
    wq,
    wk,
    wv,
    wo,
    wup_near,
    wdn,
    gtok,
    qs,
    ks,
    vs,
    att,
    mid,
    ffn_in,
    mid_out,
    grad_pre,
    ring_h,
    ring_d,
    gffn_own,
    gffn_got,
    ffp_own,
    ffp_got,
    weights_c,
    doc_col,
    lse,
    delta,
    stat_own,
    stat_got,
    gain_mid_sum,
    gain_own,
    gain_got,
    item_u,
    item_d,
    got_core,
    got_y,
    got_z,
    half_own,
    half_got,
    stat_sem,
    gffn_sem,
    ffp_sem,
    item_sem,
    gain_sem,
    half_sem,
    load_sem,
    store_sem,
):
    nz, ny = places
    row, tp = lax.axis_index("row"), lax.axis_index("tp")
    core = lax.rem(row, 2)
    y_at = lax.rem(row // 2, ny)
    z_at = row // (2 * ny)
    to_x = (row, 1 - tp)
    to_core = (row + 1 - 2 * core, tp)
    to_y = (row + 2 - 4 * y_at, tp)
    to_z = [
        (lax.rem(z_at + k, nz) * (2 * ny) + lax.rem(row, 2 * ny), tp) for k in range(1, nz)
    ]
    length, width = tok.shape
    half = wdn.shape[0]
    chunks = length // CHUNK
    pairs = width // LANES
    piece = width // (nz * ny * 2)

    ga, gs, gf, gm = [
        gain[...].reshape(1, gain.shape[0]) for gain in (ga_flat, gs_flat, gf_flat, gm_flat)
    ]
    loads = [
        pltpu.make_async_copy(far, near, load_sem.at[at])
        for at, (far, near) in enumerate(
            (
                (tok_far, tok),
                (wq_far, wq),
                (wk_far, wk),
                (wv_far, wv),
                (wo_far, wo),
                (wup_far, wup_near),
                (cot_far, cot),
                (wdn_far, wdn),
            )
        )
    ]
    for load in loads:
        load.start()
    barrier = pltpu.get_barrier_semaphore()
    partners = [to_x, to_core, to_y] + to_z
    for partner in partners:
        pl.semaphore_signal(barrier, inc=1, device_id=partner, device_id_type=MESH)

    def remote(src, dst, sems, at, partner):
        return pltpu.make_async_remote_copy(
            src_ref=src,
            dst_ref=dst,
            send_sem=sems.at[0, at],
            recv_sem=sems.at[1, at],
            device_id=partner,
            device_id_type=MESH,
        )

    lane = lax.broadcasted_iota(jnp.int32, (1, LANES), 1)
    low_lane = lane < HEAD_DIM
    lane_f = [low_lane.astype(F32), 1.0 - low_lane.astype(F32)]
    lane_b = [value.astype(BF16) for value in lane_f]

    row_at = lax.broadcasted_iota(jnp.int32, (16, LANES), 0)
    col_at = lax.broadcasted_iota(jnp.int32, (16, LANES), 1)
    for head in range(HEADS):
        row_count = jnp.zeros((16, LANES), F32)
        col_count = jnp.zeros((16, LANES), F32)
        for pattern in range(dil.shape[0]):
            last = dil[pattern] - 1
            row_count += (((row_at - head) & last) == 0).astype(F32)
            col_count += (((col_at - head) & last) == 0).astype(F32)
        weights_c[head] = jnp.minimum(row_count, col_count)
    for block in range(length // LANES):
        ids = doc[:, block * LANES : (block + 1) * LANES].astype(F32)
        doc_col[block * LANES : (block + 1) * LANES, :] = jnp.broadcast_to(ids, (LANES, LANES)).T
    doc_row = doc[...].astype(F32)
    bias = gtok
    value_t = ffp_own
    gain_mid_sum[...] = jnp.zeros_like(gain_mid_sum)
    gain_own[...] = jnp.zeros_like(gain_own)

    def project(at):
        rows = pl.ds(at * CHUNK, CHUNK)
        hat, _ = moments(tok[rows, :].astype(F32))
        value = (hat * ga).astype(BF16)
        qs[rows, :] = dot(value, wq[...], 1, 0).astype(BF16)
        ks[rows, :] = dot(value, wk[...], 1, 0).astype(BF16)
        vs[rows, :] = dot(value, wv[...], 1, 0).astype(BF16)

    def value_block(pair, block):
        if block < 3:
            return pl.ds(pl.multiple_of(pair * LANES, LANES), LANES), slice(
                block * CHUNK, (block + 1) * CHUNK
            )
        first = pl.multiple_of(width + (pair // 3) * LANES, LANES)
        return pl.ds(first, LANES), pl.ds(pl.multiple_of(lax.rem(pair, 3) * CHUNK, LANES), CHUNK)

    def attend(at):
        first = at * CHUNK
        start = max(0, first - WINDOW)
        span = first + CHUNK - start
        rows, keys = pl.ds(first, CHUNK), pl.ds(start, span)
        key_off = lax.broadcasted_iota(jnp.int32, (CHUNK, LANES), 0)
        query_off = lax.broadcasted_iota(jnp.int32, (CHUNK, LANES), 1)
        for block in range(span // CHUNK):
            low = start + block * CHUNK
            key_docs = doc_col[low : low + CHUNK, :]
            for side in range(CHUNK // LANES):
                begin = first + side * LANES
                allowed = key_docs == doc_row[:, begin : begin + LANES]
                allowed = allowed & (key_off + low <= query_off + begin)
                bias[block * CHUNK : (block + 1) * CHUNK, side * LANES : (side + 1) * LANES] = (
                    jnp.where(allowed, 0.0, -1e30)
                )

        def flip(pair, carry):
            lanes = pl.ds(pl.multiple_of(pair * LANES, LANES), LANES)
            value_t[value_block(pair, at)] = vs[rows, lanes].T
            return carry

        lax.fori_loop(0, pairs, flip, 0)
        ones = jnp.ones((16, CHUNK), BF16)

        def pair_step(step, carry):
            group = [step * PAIR_GROUP + at for at in range(PAIR_GROUP)]
            scores = []
            for pair in group:
                lanes = pl.ds(pl.multiple_of(pair * LANES, LANES), LANES)
                query = qs[rows, lanes]
                query_two = jnp.concatenate([query * lane_b[0], query * lane_b[1]], 0)
                scores.append(dot(ks[keys, lanes], query_two, 1, 1))
            for pair, score in zip(group, scores):
                lanes = pl.ds(pl.multiple_of(pair * LANES, LANES), LANES)
                parts = []
                for side in range(2):
                    power = score[:, side * CHUNK : (side + 1) * CHUNK]
                    power = power * (HEAD_DIM**-0.5 * LOG2E) + bias[0:span, 0:CHUNK]
                    top = jnp.max(power, 0, keepdims=True)
                    expo = jnp.exp2(power - top) * repeat(weights_c[2 * pair + side], span, CHUNK)
                    expo = expo.astype(BF16)
                    total = jnp.zeros((HEAD_DIM + 16, CHUNK), F32)
                    for block in range(span // CHUNK):
                        value = value_t[value_block(pair, start // CHUNK + block)]
                        value = value[side * HEAD_DIM : (side + 1) * HEAD_DIM, :]
                        total += dot(
                            jnp.concatenate([value, ones], 0),
                            expo[block * CHUNK : (block + 1) * CHUNK, :],
                            1,
                            0,
                        )
                    summed = total[HEAD_DIM : HEAD_DIM + 1, :]
                    parts.append(total[:HEAD_DIM, :] * (1.0 / summed))
                    lse[pair, side : side + 1, rows] = top + jnp.log2(summed)
                att[rows, lanes] = jnp.concatenate(parts, 0).T
            return carry

        lax.fori_loop(0, pairs // PAIR_GROUP, pair_step, 0)

    blocks = [slice(low, low + COLUMNS) for low in range(0, half, COLUMNS)]

    def fold(value):
        return sum(value[:, low : low + LANES] for low in range(0, COLUMNS, LANES))

    def feed(at):
        rows = pl.ds(at * CHUNK, CHUNK)
        hat, _ = moments(att[rows, :])
        sub = (hat * gs).astype(BF16)
        mid_res = tok[rows, :].astype(F32) + dot(sub, wo[...], 1, 0)
        mid[rows, :] = mid_res
        hat, _ = moments(mid_res)
        value = (hat * gf).astype(BF16)
        ffn_in[rows, :] = value
        sums = [jnp.zeros((CHUNK, LANES), F32)] * 4
        for part in blocks:
            weights = wup_near[:, :, :, :, part].reshape(width, COLUMNS)
            pre = dot(value, weights, 1, 0)
            grad = dot(cot[rows, :], wdn[part, :], 1, 1)
            ring_h[:, part] = pre
            ring_d[:, part] = grad
            act = 0.5 * pre * (1.0 + lax.erf(pre * 0.7071067811865476))
            scaled = grad * gm[:, part]
            terms = (act, act * act, scaled, scaled * act)
            sums = [total + fold(term) for total, term in zip(sums, terms)]
        sums = [jnp.sum(total, -1, keepdims=True) for total in sums]
        tile = jnp.where(lane == 0, sums[0], jnp.where(lane == 1, sums[1], 0.0))
        tile = jnp.where(lane == 2, sums[2], jnp.where(lane == 3, sums[3], tile))
        stat_own[at] = tile.T[0:8, :]
        remote(stat_own.at[at], stat_got.at[at], stat_sem, at, to_x).start()

    def gffn_copy(at):
        rows = pl.ds(at * CHUNK, CHUNK)
        return remote(gffn_own.at[rows], gffn_got.at[rows], gffn_sem, at, to_x)

    def ffp_copy(at):
        rows = pl.ds(at * CHUNK, CHUNK)
        return remote(ffp_own.at[rows], ffp_got.at[rows], ffp_sem, at, to_x)

    def feed_back(at):
        rows = pl.ds(at * CHUNK, CHUNK)
        remote(stat_own.at[at], stat_got.at[at], stat_sem, at, to_x).wait()
        both = stat_own[at] + stat_got[at]
        both = jnp.concatenate([both, jnp.zeros((LANES - 8, CHUNK), F32)], 0).T
        mean = both[:, 0:1] / FF
        inv = lax.rsqrt(both[:, 1:2] / FF - mean * mean + EPS)
        first = both[:, 2:3] / FF
        second = inv * (both[:, 3:4] - mean * both[:, 2:3]) / FF
        total = jnp.zeros((CHUNK, width), F32)
        for part in blocks:
            pre = ring_h[:, part]
            grad = ring_d[:, part]
            cdf = 0.5 * (1.0 + lax.erf(pre * 0.7071067811865476))
            slope = cdf + pre * (jnp.exp2(pre * pre * (-0.5 * LOG2E)) * 0.3989422804014327)
            hat = (pre * cdf - mean) * inv
            mid_out[rows, part] = (hat * gm[:, part]).astype(BF16)
            gain_part = grad * hat
            gain_mid_sum[:, part] += sum(gain_part[8 * i : 8 * i + 8, :] for i in range(CHUNK // 8))
            back = inv * (grad * gm[:, part] - first - hat * second)
            back = (back * slope).astype(BF16)
            grad_pre[rows, part] = back
            total += dot(back, wup_near[:, :, :, :, part].reshape(width, COLUMNS), 1, 1)
        gffn_own[rows, :] = total.astype(BF16)

    def project_down(at):
        rows = pl.ds(at * CHUNK, CHUNK)
        ffp_own[rows, :] = dot(mid_out[rows, :], wdn[...], 1, 0).astype(BF16)

    for at in range(chunks + 1):
        if at == 0:
            for load in loads[:4]:
                load.wait()
        if at < chunks:
            project(at)
            attend(at)
        if at == 0:
            for load in loads[4:]:
                load.wait()
            pl.semaphore_wait(barrier, len(partners))
        if at == chunks:
            for early in range(chunks - 1):
                project_down(early)
        if at >= 1:
            feed_back(at - 1)
        if at < chunks:
            feed(at)
        if at >= 1:
            gffn_copy(at - 1).start()

    item_a = wup_near
    items = [(item, part) for item in (item_u, item_d, item_a) for part in range(half // COLUMNS)]

    def item_part(which):
        return items[which][0], slice(items[which][1] * COLUMNS, (items[which][1] + 1) * COLUMNS)

    def core_slot(which):
        return got_core.at[which % 6]

    def y_slot(which):
        return got_y.at[which % 6]

    def core_copy(which):
        item, columns = item_part(which)
        return remote(
            item.at[:, :, 1 - core, :, columns], core_slot(which), item_sem, 8 * which, to_core
        )

    def y_copy(which):
        item, columns = item_part(which)
        return remote(
            item.at[:, 1 - y_at, core, :, columns],
            y_slot(which),
            item_sem,
            8 * which + 1,
            to_y,
        )

    def z_copies(which):
        item, columns = item_part(which)
        return [
            remote(
                item.at[lax.rem(z_at + k, nz), y_at, core, :, columns],
                got_z.at[which, k - 1],
                item_sem,
                8 * which + 1 + k,
                to_z[k - 1],
            )
            for k in range(1, nz)
        ]

    def start_core(which):
        core_copy(which).start()

    def start_y(which):
        core_copy(which).wait()
        item, columns = item_part(which)

        def add(index, carry):
            z_to, y_to = index // ny, lax.rem(index, ny)
            total = item[z_to, y_to, core, :, columns].astype(F32)
            total += got_core[which % 6, z_to, y_to].astype(F32)
            item[z_to, y_to, core, :, columns] = total.astype(BF16)
            return carry

        lax.fori_loop(0, nz * ny, add, 0)
        y_copy(which).start()

    def start_z(which):
        y_copy(which).wait()
        item, columns = item_part(which)

        def add(z_to, carry):
            total = item[z_to, y_at, core, :, columns].astype(F32)
            total += got_y[which % 6, z_to].astype(F32)
            item[z_to, y_at, core, :, columns] = total.astype(BF16)
            return carry

        lax.fori_loop(0, nz, add, 0)
        for copy in z_copies(which):
            copy.start()

    def finish(which):
        for copy in z_copies(which):
            copy.wait()
        item, columns = item_part(which)
        total = item[z_at, y_at, core, :, columns].astype(F32)
        for k in range(1, nz):
            total = total + got_z[which, k - 1].astype(F32)
        if which < 3:
            o_up[:, columns] = total
        elif which < 6:
            o_down[:, columns] = total
        else:
            half_own[:, columns] = total.astype(BF16)

    def outer(item, left, right, part):
        columns = slice(part * COLUMNS, (part + 1) * COLUMNS)
        product = dot(left[...], right[:, columns], 0, 0).astype(BF16)
        item[:, :, :, :, columns] = product.reshape(nz, ny, 2, piece, COLUMNS)

    gain_stage = [
        remote(gain_own, gain_got.at[at], gain_sem, at, partner)
        for at, partner in ((0, to_core), (1, to_y))
    ]
    gain_last = [
        remote(gain_own, gain_got.at[1 + k], gain_sem, 1 + k, to_z[k - 1]) for k in range(1, nz)
    ]

    def gain_add(at):
        gain_stage[at].wait()
        gain_own[...] += gain_got[at]

    for part in range(3):
        outer(item_u, ffn_in, grad_pre, part)
        start_core(part)
    start_y(0)
    for part in range(3):
        outer(item_d, cot, mid_out, part)
        start_core(3 + part)
        if part < 2:
            start_y(1 + part)
    start_y(3)
    project_down(chunks - 1)
    for at in range(chunks):
        ffp_copy(at).start()
    start_y(4)
    start_z(0)

    grad_res = ffn_in
    grad_att = grad_pre
    sub_out = gffn_own
    normed = gffn_got
    for at in range(chunks):
        rows = pl.ds(at * CHUNK, CHUNK)
        gffn_copy(at).wait()
        grad = gffn_own[rows, :].astype(F32) + gffn_got[rows, :].astype(F32)
        hat, inv = moments(mid[rows, :])
        gain_own[2:3, :] += jnp.sum(grad * hat, 0, keepdims=True)
        grad_mid = cot[rows, :].astype(F32) + norm_grad(hat, inv, gf, grad)
        gtok[rows, :] = grad_mid
        grad_low = grad_mid.astype(BF16)
        grad_res[rows, :] = grad_low
        grad = dot(grad_low, wo[...], 1, 1)
        hat, inv = moments(att[rows, :])
        sub_out[rows, :] = (hat * gs).astype(BF16)
        gain_own[1:2, :] += jnp.sum(grad * hat, 0, keepdims=True)
        grad_att[rows, width : 2 * width] = norm_grad(hat, inv, gs, grad).astype(BF16)
        hat, _ = moments(tok[rows, :].astype(F32))
        normed[rows, :] = (hat * ga).astype(BF16)
        if at == 0:
            start_y(5)
            start_z(1)
        if at == 2:
            start_z(2)
    for side in range(2):
        columns = slice(side * width, (side + 1) * width)
        gain_own[3 + side : 4 + side, :] = jnp.sum(gain_mid_sum[:, columns], 0, keepdims=True)
    gain_stage[0].start()

    def mask_ref(which):
        ring = ring_h if which < 6 else ring_d
        return ring, slice((which % 6) * CHUNK, (which % 6 + 1) * CHUNK)

    tiles = [
        (key, query)
        for key in range(chunks)
        for query in range(key, min(chunks, key + WINDOW // CHUNK + 1))
    ]
    key_off = lax.broadcasted_iota(jnp.int32, (CHUNK, LANES), 0)
    query_off = lax.broadcasted_iota(jnp.int32, (CHUNK, LANES), 1)
    for which, (key, query) in enumerate(tiles):
        ring, columns = mask_ref(which)
        key_docs = doc_col[key * CHUNK : (key + 1) * CHUNK, :]
        for block in range(CHUNK // LANES):
            low = query * CHUNK + block * LANES
            allowed = key_docs == doc_row[:, low : low + LANES]
            if key == query:
                allowed = allowed & (key_off + key * CHUNK <= query_off + low)
            begin = columns.start + block * LANES
            ring[:, begin : begin + LANES] = jnp.where(allowed, 0.0, -1e30)

    select = (lax.broadcasted_iota(jnp.int32, (8, LANES), 1) // HEAD_DIM) == (
        lax.broadcasted_iota(jnp.int32, (8, LANES), 0)
    )
    select = select.astype(F32).astype(BF16)
    half_width = width // 2

    dq_columns = slice(3 * CHUNK, half)

    def dq_part(block):
        low = (block % 2) * LANES
        begin = 3 * CHUNK + (block // 2) * CHUNK
        return slice(low, low + LANES), slice(begin, begin + CHUNK)

    def own_grads(part):
        offset = pl.multiple_of(tp * half_width + part * LANES, LANES)
        offset_up = pl.multiple_of(width + tp * half_width + part * LANES, LANES)
        right = [
            mid_out[:, pl.ds(offset, LANES)],
            mid_out[:, pl.ds(offset_up, LANES)],
            grad_pre[:, pl.ds(offset, LANES)],
        ]
        grad = dot(normed[...], jnp.concatenate(right, 1), 0, 0).astype(BF16)
        low = part * COLUMNS
        item_a[:, :, :, :, low : low + 3 * LANES] = grad.reshape(
            nz, ny, 2, piece, 3 * LANES
        )
        grad = dot(sub_out[...], grad_res[:, pl.ds(offset, LANES)], 0, 0).astype(BF16)
        item_a[:, :, :, :, low + 3 * LANES : low + COLUMNS] = grad.reshape(
            nz, ny, 2, piece, LANES
        )
        start_core(6 + part)

    def half_copy(part):
        columns = slice(part * COLUMNS, (part + 1) * COLUMNS)
        return remote(half_own.at[:, columns], half_got.at[:, columns], half_sem, part, to_x)

    def finish_own(part):
        finish(6 + part)
        half_copy(part).start()

    def gain_step(at):
        gain_add(at)
        if at == 0:
            gain_stage[1].start()
        else:
            for copy in gain_last:
                copy.start()

    schedule = {
        (0, False): [(gain_step, 0), (start_z, 3), (finish, 0), (finish, 1)],
        (0, True): [(start_z, 4), (finish, 2), (own_grads, 0)],
        (1, False): [(gain_step, 1), (start_z, 5), (start_y, 6), (finish, 3)],
        (1, True): [(own_grads, 1)],
        (2, False): [(start_z, 6), (start_y, 7), (finish, 4)],
        (2, True): [(own_grads, 2)],
        (3, False): [(start_z, 7), (start_y, 8), (finish, 5)],
        (3, True): [(finish_own, 0)],
        (4, False): [(start_z, 8)],
        (4, True): [(finish_own, 1)],
        (5, False): [],
        (5, True): [(finish_own, 2)],
    }

    def at_step(step, end):
        for (index, ending), events in schedule.items():
            if ending == end and events:

                @pl.when(step == index)
                def _():
                    for event, argument in events:
                        event(argument)

    def pair_back(step, carry):
        pair = lax.rem(tp * (pairs // 2) + step, pairs)
        low = pl.multiple_of(pair * LANES, LANES)
        lanes = pl.ds(low, LANES)
        upper = pl.ds(pl.multiple_of(width + low, LANES), LANES)
        product = grad_att[:, upper].astype(F32) * att[:, lanes]
        high = product.astype(BF16)
        rest = (product - high.astype(F32)).astype(BF16)
        delta[...] = dot(select, high, 1, 1) + dot(select, rest, 1, 1)
        ring_d[0:LANES, dq_columns] = jnp.zeros((LANES, half - 3 * CHUNK), F32)
        ring_d[LANES:CHUNK, dq_columns] = jnp.zeros((LANES, half - 3 * CHUNK), F32)
        for key_block in range(chunks):
            if key_block == 2:
                at_step(step, False)
            keys = slice(key_block * CHUNK, (key_block + 1) * CHUNK)
            key, value = ks[keys, lanes], vs[keys, lanes]
            key_t = key.T
            dk_sum = jnp.zeros((CHUNK, LANES), F32)
            dv_sum = jnp.zeros((CHUNK, LANES), F32)
            for which, (key_at, query_at) in enumerate(tiles):
                if key_at != key_block:
                    continue
                ring, columns = mask_ref(which)
                queries = slice(query_at * CHUNK, (query_at + 1) * CHUNK)
                query = qs[queries, lanes]
                grad_out = grad_att[queries, upper]
                query_two = jnp.concatenate([query * lane_b[0], query * lane_b[1]], 0)
                grad_two = jnp.concatenate([grad_out * lane_b[0], grad_out * lane_b[1]], 0)
                scores = dot(key, query_two, 1, 1)
                grad_prob = dot(value, grad_two, 1, 1)
                probs, grad_scores, grad_queries = [], [], []
                for side in range(2):
                    mine = slice(side * CHUNK, (side + 1) * CHUNK)
                    power = scores[:, mine] * (HEAD_DIM**-0.5 * LOG2E) + ring[:, columns]
                    power = power - lse[pair, side : side + 1, queries]
                    prob = jnp.exp2(power) * repeat(weights_c[2 * pair + side], CHUNK, CHUNK)
                    probs.append(prob.astype(BF16))
                    grad_score = prob * (grad_prob[:, mine] - delta[side : side + 1, queries])
                    grad_score = grad_score.astype(BF16)
                    grad_scores.append(grad_score)
                    grad_queries.append(
                        dot(key_t[side * HEAD_DIM : (side + 1) * HEAD_DIM, :], grad_score, 1, 0)
                    )
                dv_sum += dot(jnp.concatenate(probs, 1), grad_two, 1, 0)
                dk_sum += dot(jnp.concatenate(grad_scores, 1), query_two, 1, 0)
                part = dq_part(query_at)
                ring_d[part] += jnp.concatenate(grad_queries, 0)
            mid_out[keys, upper] = (dk_sum * HEAD_DIM**-0.5).astype(BF16)
            grad_pre[keys, lanes] = dv_sum.astype(BF16)
        for block in range(chunks):
            grad = (ring_d[dq_part(block)] * HEAD_DIM**-0.5).astype(BF16)
            mid_out[block * CHUNK : (block + 1) * CHUNK, lanes] = grad.T

        at_step(step, True)
        return carry

    lax.fori_loop(0, pairs, pair_back, 0)

    stores = []

    def store(near, far, at):
        copy = pltpu.make_async_copy(near, far, store_sem.at[at])
        copy.start()
        stores.append(copy)

    for at in range(chunks):
        rows = pl.ds(at * CHUNK, CHUNK)
        grad = dot(mid_out[rows, 0:width], wq[...], 1, 1)
        grad += dot(mid_out[rows, width : 2 * width], wk[...], 1, 1)
        grad += dot(grad_pre[rows, 0:width], wv[...], 1, 1)
        hat, inv = moments(tok[rows, :].astype(F32))
        gtok[rows, :] += norm_grad(hat, inv, ga, grad)
        store(gtok.at[rows], gtok_far.at[rows], at)

    for copy in gain_last:
        copy.wait()
    total = gain_own[...]
    for k in range(1, nz):
        total = total + gain_got[1 + k]
    o_gain[0:8, :] = pltpu.roll(total, lax.rem(width - piece * row, width), 1)[:, :LANES]
    per_row = 2 * piece
    o_gain[8:16, :] = pltpu.roll(total, lax.rem(2 * width - per_row * row, width), 1)[:, :LANES]

    for at in range(chunks):
        rows = pl.ds(at * CHUNK, CHUNK)
        ffp_copy(at).wait()
        total = ffp_own[rows, :].astype(F32) + ffp_got[rows, :].astype(F32)
        ffp_own[rows, :] = (mid[rows, :] + total).astype(BF16)
        store(ffp_own.at[rows], out_far.at[rows], chunks + at)

    for part in range(pairs // 2):
        half_copy(part).wait()
    mine_at = pl.multiple_of(tp * half_width, LANES)
    other_at = pl.multiple_of((1 - tp) * half_width, LANES)
    for part in range(pairs // 2):
        mine, other = (
            pl.ds(pl.multiple_of(begin + part * LANES, LANES), LANES)
            for begin in (mine_at, other_at)
        )
        for index, target in enumerate((o_query, o_key, o_value, o_out)):
            low = part * COLUMNS + index * LANES
            target[:, mine] = half_own[:, low : low + LANES].astype(F32)
            target[:, other] = half_got[:, low : low + LANES].astype(F32)
    own_rows = pl.ds(pl.multiple_of(piece * row, 16), piece)
    product = wq[own_rows, :].astype(F32) * o_query[...]
    product += wk[own_rows, :].astype(F32) * o_key[...]
    product += wv[own_rows, :].astype(F32) * o_value[...]
    total = jnp.broadcast_to(jnp.sum(product, -1, keepdims=True), (piece, LANES))
    total = jnp.concatenate([total, jnp.zeros((LANES - piece, LANES), F32)], 0).T
    gain = pltpu.roll(repeat(ga, 8, width), lax.rem(width - piece * row, width), 1)
    o_gain[0:1, :] = total[0:1, :] / gain[0:1, :LANES]
    for copy in stores:
        copy.wait()


def write_kernel(places, *refs):
    far_in, gain_in, far_out, gains_out = refs[:8], refs[8], refs[9:17], refs[17:21]
    near, sems = refs[21:29], refs[29]
    g_attn, g_sub, g_ffn, g_mid = gains_out
    nz, ny = places
    row = lax.axis_index("row")
    width = far_in[0].shape[1]
    piece = far_in[2].shape[0]
    steps = []
    for at in range(8):
        length = far_in[at].shape[0]
        size = CHUNK if length > CHUNK else length
        for begin in range(0, length, size):
            rows, which = pl.ds(begin, size), len(steps)
            steps.append(
                (
                    pltpu.make_async_copy(
                        far_in[at].at[rows], near[at].at[rows], sems.at[0, which]
                    ),
                    pltpu.make_async_copy(
                        near[at].at[rows], far_out[at].at[rows], sems.at[1, which]
                    ),
                )
            )
    for load, _ in steps:
        load.start()
    tile = gain_in[...]
    g_attn[...] = tile[0, :piece]
    g_sub[...] = tile[1, :piece]
    g_ffn[...] = tile[2, :piece]
    later = (2 * piece * row) // width
    g_mid[...] = jnp.where(later == 0, tile[11, : 2 * piece], tile[12, : 2 * piece])
    for load, save in steps:
        load.wait()
        save.start()
    for _, save in steps:
        save.wait()


def fused_body(places, *args):
    (tokens, doc_ids, dilations, cotangent, w_query, w_key, w_value, w_out, w_up, w_down) = args[:10]
    gains = args[10:]
    nz, ny = places
    length, width = tokens.shape
    half = w_up.shape[1]
    piece = width // (2 * nz * ny)
    chunks = length // CHUNK
    vmem = pl.BlockSpec(memory_space=pltpu.VMEM)
    smem = pl.BlockSpec(memory_space=pltpu.SMEM)
    far = pl.BlockSpec(memory_space=pl.ANY)
    shape = jax.ShapeDtypeStruct
    low = functools.partial(pltpu.VMEM, dtype=BF16)
    full = functools.partial(pltpu.VMEM, dtype=F32)
    rows_low, rows_full = low((length, width)), full((length, width))
    item = low((nz, ny, 2, piece, half))
    square = low((width, width))
    count = 3 * half // COLUMNS
    dma = lambda number: pltpu.SemaphoreType.DMA((2, number))
    big = [
        shape((length, width), BF16),
        shape((length, width), F32),
        shape((piece, width), F32),
        shape((piece, width), F32),
        shape((piece, width), F32),
        shape((piece, width), F32),
        shape((piece, half), F32),
        shape((piece, half), F32),
    ]
    results = pl.pallas_call(
        functools.partial(layer_kernel, places),
        out_shape=big + [shape((16, LANES), F32)],
        in_specs=[smem] + [vmem] * 5 + [far] * 8,
        out_specs=[far] * 2 + [vmem] * 7,
        scratch_shapes=[
            rows_low,
            rows_low,
            square,
            square,
            square,
            square,
            item,
            low((half, width)),
            rows_full,
            rows_low,
            rows_low,
            rows_low,
            rows_full,
            rows_full,
            rows_low,
            low((length, half)),
            low((length, half)),
            full((CHUNK, half)),
            full((CHUNK, half)),
            rows_low,
            rows_low,
            rows_low,
            rows_low,
            full((HEADS, 16, LANES)),
            full((length, LANES)),
            full((width // LANES, 2, length)),
            full((8, length)),
            full((chunks, 8, CHUNK)),
            full((chunks, 8, CHUNK)),
            full((8, half)),
            full((8, width)),
            full((1 + nz, 8, width)),
            item,
            item,
            low((6, nz, ny, piece, COLUMNS)),
            low((6, nz, piece, COLUMNS)),
            low((count, nz - 1, piece, COLUMNS)),
            low((piece, half)),
            low((piece, half)),
            dma(chunks),
            dma(chunks),
            dma(chunks),
            dma(8 * count),
            dma(1 + nz),
            dma(width // LANES // 2),
            pltpu.SemaphoreType.DMA((8,)),
            pltpu.SemaphoreType.DMA((2 * chunks,)),
        ],
        compiler_params=pltpu.CompilerParams(
            collective_id=0, has_side_effects=True, vmem_limit_bytes=63 * MIB
        ),
        name="layer",
    )(
        dilations,
        doc_ids.reshape(1, length),
        *gains,
        tokens,
        cotangent,
        w_query,
        w_key,
        w_value,
        w_out,
        w_up.reshape(nz, ny, 2, piece, half),
        w_down,
    )
    flat = shape((piece,), F32)
    moves = 2 * (length // CHUNK) + 6
    final = pl.pallas_call(
        functools.partial(write_kernel, places),
        out_shape=big + [flat, flat, flat, shape((2 * piece,), F32)],
        in_specs=[far] * 8 + [vmem],
        out_specs=[far] * 8 + [vmem] * 4,
        scratch_shapes=[pltpu.VMEM(one.shape, one.dtype) for one in big]
        + [pltpu.SemaphoreType.DMA((2, moves))],
        compiler_params=pltpu.CompilerParams(vmem_limit_bytes=63 * MIB),
        name="write",
    )(*results)
    return (*final[:7], final[7].T, *final[8:])


def norm_parts(value):
    row_mean = jnp.mean(value, -1, keepdims=True)
    centred = value - row_mean
    inv_std = lax.rsqrt(jnp.mean(centred * centred, -1, keepdims=True) + EPS)
    return (centred * inv_std, inv_std)


def norm_back(normed_hat, inv_std, gain, grad):
    scaled = grad * gain
    grad_value = inv_std * (
        scaled
        - jnp.mean(scaled, -1, keepdims=True)
        - normed_hat * jnp.mean(scaled * normed_hat, -1, keepdims=True)
    )
    return (grad_value, jnp.sum(grad * normed_hat, 0))


def selection(dilations, positions):
    head_ids = jnp.arange(HEADS, dtype=jnp.int32)
    left_side = positions[None, None, :] % dilations[:, None, None]
    right_side = head_ids[None, :, None] % dilations[:, None, None]
    return (left_side == right_side).astype(jnp.float32)


def pattern_weights(dilations, doc_row, query_pos, query_docs):
    key_pos = jnp.arange(doc_row.shape[0], dtype=jnp.int32)
    counts = jnp.einsum(
        "phi,phj->hij", selection(dilations, query_pos), selection(dilations, key_pos)
    )
    allowed = (query_pos[:, None] >= key_pos[None, :]) & (query_docs[:, None] == doc_row[None, :])
    return counts * allowed.astype(jnp.float32)[None]


def attn_forward(dilations, doc_row, key_heads, value_heads, query_block, query_pos, query_docs):
    score_scale = HEAD_DIM ** (-0.5)
    scores = (
        jnp.einsum("ihe,jhe->hij", query_block, key_heads, preferred_element_type=jnp.float32)
        * score_scale
    )
    weights_mult = pattern_weights(dilations, doc_row, query_pos, query_docs)
    masked = jnp.where(weights_mult > 0, scores, -1e30)
    row_max = jnp.max(masked, -1, keepdims=True)
    expo = weights_mult * jnp.exp(masked - row_max)
    totals = jnp.sum(expo, -1, keepdims=True)
    attn_prob = (expo / totals).astype(jnp.bfloat16)
    out_block = jnp.einsum(
        "hij,jhe->ihe", attn_prob, value_heads, preferred_element_type=jnp.float32
    )
    return (out_block, row_max[..., 0] + jnp.log(totals[..., 0]))


def attn_backward(
    dilations,
    doc_row,
    key_heads,
    value_heads,
    query_block,
    query_pos,
    query_docs,
    lse_block,
    grad_block,
):
    score_scale = HEAD_DIM ** (-0.5)
    scores = (
        jnp.einsum("ihe,jhe->hij", query_block, key_heads, preferred_element_type=jnp.float32)
        * score_scale
    )
    weights_mult = pattern_weights(dilations, doc_row, query_pos, query_docs)
    attn_full = weights_mult * jnp.exp(scores - lse_block[:, :, None])
    attn_low = attn_full.astype(jnp.bfloat16)
    value_part = jnp.einsum(
        "hij,ihe->jhe", attn_low, grad_block, preferred_element_type=jnp.float32
    )
    grad_prob = jnp.einsum(
        "ihe,jhe->hij", grad_block, value_heads, preferred_element_type=jnp.float32
    )
    row_delta = jnp.sum(attn_full * grad_prob, -1, keepdims=True)
    grad_scores = (attn_full * (grad_prob - row_delta)).astype(jnp.bfloat16)
    query_grad = (
        jnp.einsum("hij,jhe->ihe", grad_scores, key_heads, preferred_element_type=jnp.float32)
        * score_scale
    )
    key_part = (
        jnp.einsum("hij,ihe->jhe", grad_scores, query_block, preferred_element_type=jnp.float32)
        * score_scale
    )
    return (query_grad, key_part, value_part)


def general_body(
    tokens,
    doc_ids,
    dilations,
    cotangent,
    w_query,
    w_key,
    w_value,
    w_out,
    w_up,
    w_down,
    gain_attn,
    gain_sub,
    gain_ffn,
    gain_mid,
):
    row_len = tokens.shape[0]
    width = tokens.shape[1]
    block_rows = min(512, row_len)
    block_count = row_len // block_rows
    doc_row = doc_ids.reshape(row_len)
    row_in = tokens.astype(jnp.float32)
    attn_hat, attn_std = norm_parts(row_in)
    normed = (attn_hat * gain_attn).astype(jnp.bfloat16)
    keys_low = jnp.dot(normed, w_key, preferred_element_type=jnp.float32).astype(jnp.bfloat16)
    values_low = jnp.dot(normed, w_value, preferred_element_type=jnp.float32).astype(jnp.bfloat16)
    key_heads = keys_low.reshape(row_len, HEADS, HEAD_DIM)
    value_heads = values_low.reshape(row_len, HEADS, HEAD_DIM)
    queries = jnp.dot(normed, w_query, preferred_element_type=jnp.float32).astype(jnp.bfloat16)
    query_heads = queries.reshape(row_len, HEADS, HEAD_DIM)

    def attend(block_index):
        offset = block_index * block_rows
        query_block = lax.dynamic_slice_in_dim(query_heads, offset, block_rows, 0)
        query_pos = offset + jnp.arange(block_rows, dtype=jnp.int32)
        query_docs = lax.dynamic_slice_in_dim(doc_row, offset, block_rows, 0)
        return attn_forward(
            dilations, doc_row, key_heads, value_heads, query_block, query_pos, query_docs
        )

    out_blocks, log_sums = lax.map(attend, jnp.arange(block_count))
    attended = out_blocks.reshape(row_len, width)
    sub_hat, sub_std = norm_parts(attended)
    sub_out = (sub_hat * gain_sub).astype(jnp.bfloat16)
    mid_res = row_in + jnp.dot(sub_out, w_out, preferred_element_type=jnp.float32)
    ffn_hat, ffn_std = norm_parts(mid_res)
    ffn_in = (ffn_hat * gain_ffn).astype(jnp.bfloat16)
    hidden_pre = jnp.dot(ffn_in, w_up, preferred_element_type=jnp.float32)
    hidden_act = jax.nn.gelu(hidden_pre, approximate=False)
    sum_first, sum_second = lax.psum(
        (jnp.sum(hidden_act, -1), jnp.sum(hidden_act * hidden_act, -1)), "tp"
    )
    mid_mean = sum_first[:, None] / FF
    mid_std = lax.rsqrt(sum_second[:, None] / FF - mid_mean * mid_mean + EPS)
    mid_hat = (hidden_act - mid_mean) * mid_std
    mid_out = (mid_hat * gain_mid).astype(jnp.bfloat16)
    ffn_part = jnp.dot(mid_out, w_down, preferred_element_type=jnp.float32)
    ffn_total = lax.psum(ffn_part, "tp")
    output = (mid_res + ffn_total).astype(jnp.bfloat16)
    grad_down = jnp.einsum("lf,ld->fd", mid_out, cotangent, preferred_element_type=jnp.float32)
    grad_mid_out = jnp.einsum("ld,fd->lf", cotangent, w_down, preferred_element_type=jnp.float32)
    grad_gain_mid = jnp.sum(grad_mid_out * mid_hat, 0)
    scaled = grad_mid_out * gain_mid
    back_first, back_second = lax.psum((jnp.sum(scaled, -1), jnp.sum(scaled * mid_hat, -1)), "tp")
    grad_act = mid_std * (scaled - back_first[:, None] / FF - mid_hat * back_second[:, None] / FF)
    gelu_pull = jax.vjp(lambda value: jax.nn.gelu(value, approximate=False), hidden_pre)[1]
    grad_pre = gelu_pull(grad_act)[0].astype(jnp.bfloat16)
    grad_up = jnp.einsum("ld,lf->df", ffn_in, grad_pre, preferred_element_type=jnp.float32)
    sum_up, sum_down, sum_gain_mid = (
        lax.psum_scatter(grad_up, "row", scatter_dimension=0, tiled=True),
        lax.psum_scatter(grad_down, "row", scatter_dimension=1, tiled=True),
        lax.psum_scatter(grad_gain_mid, "row", scatter_dimension=0, tiled=True),
    )
    grad_ffn_part = jnp.einsum("lf,df->ld", grad_pre, w_up, preferred_element_type=jnp.float32)
    grad_ffn_in = lax.psum(grad_ffn_part, "tp")
    grad_mid_in, grad_gain_ffn = norm_back(ffn_hat, ffn_std, gain_ffn, grad_ffn_in)
    grad_mid_res = cotangent.astype(jnp.float32) + grad_mid_in
    grad_res_low = grad_mid_res.astype(jnp.bfloat16)
    grad_out = jnp.einsum("ld,le->de", sub_out, grad_res_low, preferred_element_type=jnp.float32)
    grad_sub_out = jnp.einsum("le,de->ld", grad_res_low, w_out, preferred_element_type=jnp.float32)
    grad_attended, grad_gain_sub = norm_back(sub_hat, sub_std, gain_sub, grad_sub_out)
    grad_att_low = grad_attended.astype(jnp.bfloat16)
    grad_heads = grad_att_low.reshape(row_len, HEADS, HEAD_DIM)

    def attend_back(running, block_index):
        key_sum, value_sum = running
        offset = block_index * block_rows
        query_block = lax.dynamic_slice_in_dim(query_heads, offset, block_rows, 0)
        query_pos = offset + jnp.arange(block_rows, dtype=jnp.int32)
        query_docs = lax.dynamic_slice_in_dim(doc_row, offset, block_rows, 0)
        grad_block = lax.dynamic_slice_in_dim(grad_heads, offset, block_rows, 0)
        query_grad, key_part, value_part = attn_backward(
            dilations,
            doc_row,
            key_heads,
            value_heads,
            query_block,
            query_pos,
            query_docs,
            log_sums[block_index],
            grad_block,
        )
        return ((key_sum + key_part, value_sum + value_part), query_grad)

    zero_heads = jnp.zeros((row_len, HEADS, HEAD_DIM), jnp.float32)
    (key_grad, value_grad), query_blocks = lax.scan(
        attend_back, (zero_heads, zero_heads), jnp.arange(block_count)
    )
    grad_queries = query_blocks.reshape(row_len, width).astype(jnp.bfloat16)
    grad_keys = key_grad.reshape(row_len, width).astype(jnp.bfloat16)
    grad_values = value_grad.reshape(row_len, width).astype(jnp.bfloat16)
    grad_query = jnp.einsum("ld,le->de", normed, grad_queries, preferred_element_type=jnp.float32)
    grad_key = jnp.einsum("ld,le->de", normed, grad_keys, preferred_element_type=jnp.float32)
    grad_value = jnp.einsum("ld,le->de", normed, grad_values, preferred_element_type=jnp.float32)
    grad_normed = (
        jnp.einsum("le,de->ld", grad_queries, w_query, preferred_element_type=jnp.float32)
        + jnp.einsum("le,de->ld", grad_keys, w_key, preferred_element_type=jnp.float32)
        + jnp.einsum("le,de->ld", grad_values, w_value, preferred_element_type=jnp.float32)
    )
    grad_row_in, grad_gain_attn = norm_back(attn_hat, attn_std, gain_attn, grad_normed)
    grad_tokens = grad_mid_res + grad_row_in
    sum_query, sum_key, sum_value, sum_out, sum_gain_attn, sum_gain_sub, sum_gain_ffn = (
        lax.psum_scatter(grad_query, "row", scatter_dimension=0, tiled=True),
        lax.psum_scatter(grad_key, "row", scatter_dimension=0, tiled=True),
        lax.psum_scatter(grad_value, "row", scatter_dimension=0, tiled=True),
        lax.psum_scatter(grad_out, "row", scatter_dimension=0, tiled=True),
        lax.psum_scatter(grad_gain_attn, "row", scatter_dimension=0, tiled=True),
        lax.psum_scatter(grad_gain_sub, "row", scatter_dimension=0, tiled=True),
        lax.psum_scatter(grad_gain_ffn, "row", scatter_dimension=0, tiled=True),
    )
    return (
        output,
        grad_tokens,
        sum_query,
        sum_key,
        sum_value,
        sum_out,
        sum_up,
        sum_down,
        sum_gain_attn,
        sum_gain_sub,
        sum_gain_ffn,
        sum_gain_mid,
    )


def solution(mesh):
    rows, columns = mesh.shape["row"], mesh.shape["tp"]
    if columns == 2 and rows == 16:
        body = functools.partial(fused_body, (rows // 4, 2))
    else:
        body = general_body
    return jax.shard_map(
        body,
        mesh=mesh,
        in_specs=(
            P("row", None),
            P("row", None),
            P(),
            P("row", None),
            P(),
            P(),
            P(),
            P(),
            P(None, "tp"),
            P("tp", None),
            P(),
            P(),
            P(),
            P("tp"),
        ),
        out_specs=(
            P("row", None),
            P("row", None),
            P("row", None),
            P("row", None),
            P("row", None),
            P("row", None),
            P("row", "tp"),
            P("tp", "row"),
            P("row"),
            P("row"),
            P("row"),
            P(("tp", "row")),
        ),
        check_vma=False,
    )
```

```python
import functools

import jax
import jax.numpy as jnp
from jax import lax
from jax.experimental import pallas as pl
from jax.experimental.pallas import tpu as pltpu
from jax.sharding import PartitionSpec as P

MESH = pl.DeviceIdType.MESH
HEADS = 12
HEAD_DIM = 64
FF = 3072
EPS = 1e-05
F32 = jnp.float32
BF16 = jnp.bfloat16
LOG2E = 1.4426950408889634
CHUNK = 256
WINDOW = 512
PAIR_GROUP = 2
COLUMNS = 512
LANES = 128
MIB = 2**20


def dot(left, right, left_dim, right_dim):
    return lax.dot_general(
        left, right, (((left_dim,), (right_dim,)), ((), ())), preferred_element_type=F32
    )


def moments(value):
    mean = jnp.mean(value, -1, keepdims=True)
    centred = value - mean
    inv = lax.rsqrt(jnp.mean(centred * centred, -1, keepdims=True) + EPS)
    return centred * inv, inv


def norm_grad(hat, inv, gain, grad):
    scaled = grad * gain
    first = jnp.mean(scaled, -1, keepdims=True)
    second = jnp.mean(scaled * hat, -1, keepdims=True)
    return inv * (scaled - first - hat * second)


def repeat(tile, rows, columns):
    tall = jnp.concatenate([tile] * (rows // tile.shape[0]), 0)
    return jnp.concatenate([tall] * (columns // tile.shape[1]), 1)


def layer_kernel(
    places,
    dil,
    doc,
    ga_flat,
    gs_flat,
    gf_flat,
    gm_flat,
    tok_far,
    cot_far,
    wq_far,
    wk_far,
    wv_far,
    wo_far,
    wup_far,
    wdn_far,
    out_far,
    gtok_far,
    o_query,
    o_key,
    o_value,
    o_out,
    o_up,
    o_down,
    o_gain,
    tok,
    cot,
    wq,
    wk,
    wv,
    wo,
    wup_near,
    wdn,
    gtok,
    qs,
    ks,
    vs,
    att,
    mid,
    ffn_in,
    mid_out,
    grad_pre,
    ring_h,
    ring_d,
    gffn_own,
    gffn_got,
    ffp_own,
    ffp_got,
    weights_c,
    doc_col,
    lse,
    delta,
    key_t,
    stat_own,
    stat_got,
    gain_mid_sum,
    gain_own,
    gain_got,
    item_u,
    item_d,
    got_core,
    got_y,
    got_z,
    half_own,
    half_got,
    stat_sem,
    gffn_sem,
    ffp_sem,
    item_sem,
    gain_sem,
    half_sem,
    load_sem,
    store_sem,
):
    nz, ny = places
    row, tp = lax.axis_index("row"), lax.axis_index("tp")
    core = lax.rem(row, 2)
    y_at = lax.rem(row // 2, ny)
    z_at = row // (2 * ny)
    to_x = (row, 1 - tp)
    to_core = (row + 1 - 2 * core, tp)
    to_y = (row + 2 - 4 * y_at, tp)
    to_z = [
        (lax.rem(z_at + k, nz) * (2 * ny) + lax.rem(row, 2 * ny), tp) for k in range(1, nz)
    ]
    length, width = tok.shape
    half = wdn.shape[0]
    chunks = length // CHUNK
    pairs = width // LANES
    piece = width // (nz * ny * 2)

    ga, gs, gf, gm = [
        gain[...].reshape(1, gain.shape[0]) for gain in (ga_flat, gs_flat, gf_flat, gm_flat)
    ]
    loads = [
        pltpu.make_async_copy(far, near, load_sem.at[at])
        for at, (far, near) in enumerate(
            (
                (tok_far, tok),
                (wq_far, wq),
                (wk_far, wk),
                (wv_far, wv),
                (wo_far, wo),
                (wup_far, wup_near),
                (cot_far, cot),
                (wdn_far, wdn),
            )
        )
    ]
    for load in loads:
        load.start()
    barrier = pltpu.get_barrier_semaphore()
    partners = [to_x, to_core, to_y] + to_z
    for partner in partners:
        pl.semaphore_signal(barrier, inc=1, device_id=partner, device_id_type=MESH)

    def remote(src, dst, sems, at, partner):
        return pltpu.make_async_remote_copy(
            src_ref=src,
            dst_ref=dst,
            send_sem=sems.at[0, at],
            recv_sem=sems.at[1, at],
            device_id=partner,
            device_id_type=MESH,
        )

    lane = lax.broadcasted_iota(jnp.int32, (1, LANES), 1)
    low_lane = lane < HEAD_DIM
    lane_f = [low_lane.astype(F32), 1.0 - low_lane.astype(F32)]
    lane_b = [value.astype(BF16) for value in lane_f]

    row_at = lax.broadcasted_iota(jnp.int32, (16, LANES), 0)
    col_at = lax.broadcasted_iota(jnp.int32, (16, LANES), 1)
    for head in range(HEADS):
        row_count = jnp.zeros((16, LANES), F32)
        col_count = jnp.zeros((16, LANES), F32)
        for pattern in range(dil.shape[0]):
            last = dil[pattern] - 1
            row_count += (((row_at - head) & last) == 0).astype(F32)
            col_count += (((col_at - head) & last) == 0).astype(F32)
        weights_c[head] = jnp.minimum(row_count, col_count)
    for block in range(length // LANES):
        ids = doc[:, block * LANES : (block + 1) * LANES].astype(F32)
        doc_col[block * LANES : (block + 1) * LANES, :] = jnp.broadcast_to(ids, (LANES, LANES)).T
    doc_row = doc[...].astype(F32)
    bias = gtok
    value_t = ffp_own
    gain_mid_sum[...] = jnp.zeros_like(gain_mid_sum)
    gain_own[...] = jnp.zeros_like(gain_own)

    def project(at):
        rows = rows_of(at)
        hat, _ = moments(tok[rows, :].astype(F32))
        value = (hat * ga).astype(BF16)
        qs[rows, :] = dot(value, wq[...], 1, 0).astype(BF16)
        ks[rows, :] = dot(value, wk[...], 1, 0).astype(BF16)
        vs[rows, :] = dot(value, wv[...], 1, 0).astype(BF16)

    def rows_of(at):
        return pl.ds(at * CHUNK if isinstance(at, int) else pl.multiple_of(at * CHUNK, CHUNK), CHUNK)

    def value_block(pair, block):
        down, right = 2 * block + pair // 3, lax.rem(pair, 3)
        return (
            pl.ds(pl.multiple_of(down * LANES, LANES), LANES),
            pl.ds(pl.multiple_of(right * CHUNK, CHUNK), CHUNK),
        )

    def attend(at, span):
        first = at * CHUNK
        start = first + CHUNK - span
        start_block = at + 1 - span // CHUNK
        rows, keys = rows_of(at), pl.ds(pl.multiple_of(start, CHUNK), span)
        key_off = lax.broadcasted_iota(jnp.int32, (CHUNK, LANES), 0)
        query_off = lax.broadcasted_iota(jnp.int32, (CHUNK, LANES), 1)
        for block in range(span // CHUNK):
            low = pl.multiple_of(start + block * CHUNK, CHUNK)
            key_docs = doc_col[pl.ds(low, CHUNK), :]
            for side in range(CHUNK // LANES):
                begin = pl.multiple_of(first + side * LANES, LANES)
                allowed = key_docs == doc[:, pl.ds(begin, LANES)].astype(F32)
                allowed = allowed & (key_off + low <= query_off + begin)
                bias[block * CHUNK : (block + 1) * CHUNK, side * LANES : (side + 1) * LANES] = (
                    jnp.where(allowed, 0.0, -1e30)
                )

        def flip(pair, carry):
            lanes = pl.ds(pl.multiple_of(pair * LANES, LANES), LANES)
            value_t[value_block(pair, at)] = vs[rows, lanes].T
            return carry

        lax.fori_loop(0, pairs, flip, 0)
        ones = jnp.ones((16, CHUNK), BF16)

        def pair_step(step, carry):
            group = [step * PAIR_GROUP + at for at in range(PAIR_GROUP)]
            scores = []
            for pair in group:
                lanes = pl.ds(pl.multiple_of(pair * LANES, LANES), LANES)
                query = qs[rows, lanes]
                query_two = jnp.concatenate([query * lane_b[0], query * lane_b[1]], 0)
                scores.append(dot(ks[keys, lanes], query_two, 1, 1))
            for pair, score in zip(group, scores):
                lanes = pl.ds(pl.multiple_of(pair * LANES, LANES), LANES)
                parts = []
                for side in range(2):
                    power = score[:, side * CHUNK : (side + 1) * CHUNK]
                    power = power * (HEAD_DIM**-0.5 * LOG2E) + bias[0:span, 0:CHUNK]
                    top = jnp.max(power, 0, keepdims=True)
                    expo = jnp.exp2(power - top) * repeat(weights_c[2 * pair + side], span, CHUNK)
                    expo = expo.astype(BF16)
                    total = jnp.zeros((HEAD_DIM + 16, CHUNK), F32)
                    for block in range(span // CHUNK):
                        value = value_t[value_block(pair, start_block + block)]
                        value = value[side * HEAD_DIM : (side + 1) * HEAD_DIM, :]
                        total += dot(
                            jnp.concatenate([value, ones], 0),
                            expo[block * CHUNK : (block + 1) * CHUNK, :],
                            1,
                            0,
                        )
                    summed = total[HEAD_DIM : HEAD_DIM + 1, :]
                    parts.append(total[:HEAD_DIM, :] * (1.0 / summed))
                    lse[pair, side : side + 1, rows] = top + jnp.log2(summed)
                att[rows, lanes] = jnp.concatenate(parts, 0).T
            return carry

        lax.fori_loop(0, pairs // PAIR_GROUP, pair_step, 0)

    blocks = [slice(low, low + COLUMNS) for low in range(0, half, COLUMNS)]

    def fold(value):
        return sum(value[:, low : low + LANES] for low in range(0, COLUMNS, LANES))

    def feed(at):
        rows = rows_of(at)
        hat, _ = moments(att[rows, :])
        sub = (hat * gs).astype(BF16)
        mid_res = tok[rows, :].astype(F32) + dot(sub, wo[...], 1, 0)
        mid[rows, :] = mid_res
        hat, _ = moments(mid_res)
        value = (hat * gf).astype(BF16)
        ffn_in[rows, :] = value
        sums = [jnp.zeros((CHUNK, LANES), F32)] * 4

        def products(part):
            weights = wup_near[:, :, :, :, part].reshape(width, COLUMNS)
            return dot(value, weights, 1, 0), dot(cot[rows, :], wdn[part, :], 1, 1)

        later = products(blocks[0])
        for index, part in enumerate(blocks):
            pre, grad = later
            if index + 1 < len(blocks):
                later = products(blocks[index + 1])
            ring_h[:, part] = pre
            ring_d[:, part] = grad
            act = 0.5 * pre * (1.0 + lax.erf(pre * 0.7071067811865476))
            scaled = grad * gm[:, part]
            terms = (act, act * act, scaled, scaled * act)
            sums = [total + fold(term) for total, term in zip(sums, terms)]
        sums = [jnp.sum(total, -1, keepdims=True) for total in sums]
        tile = jnp.where(lane == 0, sums[0], jnp.where(lane == 1, sums[1], 0.0))
        tile = jnp.where(lane == 2, sums[2], jnp.where(lane == 3, sums[3], tile))
        stat_own[at] = tile.T[0:8, :]
        remote(stat_own.at[at], stat_got.at[at], stat_sem, at, to_x).start()

    def gffn_copy(at):
        rows = rows_of(at)
        return remote(gffn_own.at[rows], gffn_got.at[rows], gffn_sem, at, to_x)

    def ffp_copy(at):
        rows = pl.ds(at * CHUNK, CHUNK)
        return remote(ffp_own.at[rows], ffp_got.at[rows], ffp_sem, at, to_x)

    def feed_back(at):
        rows = rows_of(at)
        remote(stat_own.at[at], stat_got.at[at], stat_sem, at, to_x).wait()
        both = stat_own[at] + stat_got[at]
        both = jnp.concatenate([both, jnp.zeros((LANES - 8, CHUNK), F32)], 0).T
        mean = both[:, 0:1] / FF
        inv = lax.rsqrt(both[:, 1:2] / FF - mean * mean + EPS)
        first = both[:, 2:3] / FF
        second = inv * (both[:, 3:4] - mean * both[:, 2:3]) / FF
        total = jnp.zeros((CHUNK, width), F32)
        for part in blocks:
            pre = ring_h[:, part]
            grad = ring_d[:, part]
            cdf = 0.5 * (1.0 + lax.erf(pre * 0.7071067811865476))
            slope = cdf + pre * (jnp.exp2(pre * pre * (-0.5 * LOG2E)) * 0.3989422804014327)
            hat = (pre * cdf - mean) * inv
            mid_out[rows, part] = (hat * gm[:, part]).astype(BF16)
            gain_part = grad * hat
            gain_mid_sum[:, part] += sum(gain_part[8 * i : 8 * i + 8, :] for i in range(CHUNK // 8))
            back = inv * (grad * gm[:, part] - first - hat * second)
            back = (back * slope).astype(BF16)
            grad_pre[rows, part] = back
            total += dot(back, wup_near[:, :, :, :, part].reshape(width, COLUMNS), 1, 1)
        gffn_own[rows, :] = total.astype(BF16)

    def project_down(at):
        rows = pl.ds(at * CHUNK, CHUNK)
        ffp_own[rows, :] = dot(mid_out[rows, :], wdn[...], 1, 0).astype(BF16)

    for load in loads[:4]:
        load.wait()
    widest = WINDOW // CHUNK

    def chunk_step(at, carry):
        project(at)
        for place in range(widest):

            @pl.when(at == place)
            def _():
                attend(place, (place + 1) * CHUNK)

        @pl.when(at >= widest)
        def _():
            attend(at, (widest + 1) * CHUNK)

        @pl.when(at == 0)
        def _():
            for load in loads[4:]:
                load.wait()
            pl.semaphore_wait(barrier, len(partners))

        @pl.when(at >= 1)
        def _():
            feed_back(at - 1)

        feed(at)

        @pl.when(at >= 1)
        def _():
            gffn_copy(at - 1).start()

        return carry

    lax.fori_loop(0, chunks, chunk_step, 0)
    for early in range(chunks - 1):
        project_down(early)
    feed_back(chunks - 1)
    gffn_copy(chunks - 1).start()

    item_a = wup_near
    items = (item_u, item_d, item_a)
    parts = half // COLUMNS

    def part_columns(part):
        if isinstance(part, int):
            return slice(part * COLUMNS, (part + 1) * COLUMNS)
        return pl.ds(pl.multiple_of(part * COLUMNS, COLUMNS), COLUMNS)

    def slot(group, part):
        return (group % 2) * parts + part

    def sem_at(group, part):
        return 8 * (group * parts + part)

    def core_copy(group, part):
        return remote(
            items[group].at[:, :, 1 - core, :, part_columns(part)],
            got_core.at[slot(group, part)],
            item_sem,
            sem_at(group, part),
            to_core,
        )

    def y_copy(group, part):
        return remote(
            items[group].at[:, 1 - y_at, core, :, part_columns(part)],
            got_y.at[slot(group, part)],
            item_sem,
            sem_at(group, part) + 1,
            to_y,
        )

    def z_copies(group, part):
        return [
            remote(
                items[group].at[lax.rem(z_at + k, nz), y_at, core, :, part_columns(part)],
                got_z.at[group * parts + part, k - 1],
                item_sem,
                sem_at(group, part) + 1 + k,
                to_z[k - 1],
            )
            for k in range(1, nz)
        ]

    def start_core(group, part):
        core_copy(group, part).start()

    def start_y(group, part):
        core_copy(group, part).wait()
        item, columns = items[group], part_columns(part)

        def add(index, carry):
            z_to, y_to = index // ny, lax.rem(index, ny)
            total = item[z_to, y_to, core, :, columns].astype(F32)
            total += got_core[slot(group, part), z_to, y_to].astype(F32)
            item[z_to, y_to, core, :, columns] = total.astype(BF16)
            return carry

        lax.fori_loop(0, nz * ny, add, 0)
        y_copy(group, part).start()

    def start_z(group, part):
        y_copy(group, part).wait()
        item, columns = items[group], part_columns(part)

        def add(z_to, carry):
            total = item[z_to, y_at, core, :, columns].astype(F32)
            total += got_y[slot(group, part), z_to].astype(F32)
            item[z_to, y_at, core, :, columns] = total.astype(BF16)
            return carry

        lax.fori_loop(0, nz, add, 0)
        for copy in z_copies(group, part):
            copy.start()

    def finish(group, part):
        for copy in z_copies(group, part):
            copy.wait()
        columns = part_columns(part)
        total = items[group][z_at, y_at, core, :, columns].astype(F32)
        for k in range(1, nz):
            total = total + got_z[group * parts + part, k - 1].astype(F32)
        if group == 2:
            half_own[:, columns] = total.astype(BF16)
        else:
            (o_up, o_down)[group][:, columns] = total

    def outer(group, left, right, part):
        columns = part_columns(part)
        product = dot(left[...], right[:, columns], 0, 0).astype(BF16)
        items[group][:, :, :, :, columns] = product.reshape(nz, ny, 2, piece, COLUMNS)
        start_core(group, part)

    gain_stage = [
        remote(gain_own, gain_got.at[at], gain_sem, at, partner)
        for at, partner in ((0, to_core), (1, to_y))
    ]
    gain_last = [
        remote(gain_own, gain_got.at[1 + k], gain_sem, 1 + k, to_z[k - 1]) for k in range(1, nz)
    ]

    def gain_add(at):
        gain_stage[at].wait()
        gain_own[...] += gain_got[at]

    def outer_up(part, carry):
        outer(0, ffn_in, grad_pre, part)

        @pl.when(part >= 1)
        def _():
            start_y(0, part - 1)

        return carry

    def outer_down(part, carry):
        outer(1, cot, mid_out, part)
        return carry

    lax.fori_loop(0, parts, outer_up, 0)
    lax.fori_loop(0, parts, outer_down, 0)
    project_down(chunks - 1)
    ffp_copy(0).start()
    start_z(0, 0)
    start_y(0, 2)

    grad_res = ffn_in
    grad_att = grad_pre
    sub_out = gffn_own
    normed = gffn_got
    def norms_back(at, carry):
        rows = pl.ds(pl.multiple_of(at * CHUNK, CHUNK), CHUNK)
        gffn_copy(at).wait()
        grad = gffn_own[rows, :].astype(F32) + gffn_got[rows, :].astype(F32)
        hat, inv = moments(mid[rows, :])
        gain_own[2:3, :] += jnp.sum(grad * hat, 0, keepdims=True)
        grad_mid = cot[rows, :].astype(F32) + norm_grad(hat, inv, gf, grad)
        gtok[rows, :] = grad_mid
        grad_low = grad_mid.astype(BF16)
        grad_res[rows, :] = grad_low
        grad = dot(grad_low, wo[...], 1, 1)
        hat, inv = moments(att[rows, :])
        sub_out[rows, :] = (hat * gs).astype(BF16)
        gain_own[1:2, :] += jnp.sum(grad * hat, 0, keepdims=True)
        grad_att[rows, width : 2 * width] = norm_grad(hat, inv, gs, grad).astype(BF16)
        hat, _ = moments(tok[rows, :].astype(F32))
        normed[rows, :] = (hat * ga).astype(BF16)
        return carry

    lax.fori_loop(0, chunks, norms_back, 0)
    for at in range(1, chunks):
        ffp_copy(at).start()
    start_z(0, 1)
    start_y(1, 0)
    for side in range(2):
        columns = slice(side * width, (side + 1) * width)
        gain_own[3 + side : 4 + side, :] = jnp.sum(gain_mid_sum[:, columns], 0, keepdims=True)
    gain_stage[0].start()

    def ring_block(which):
        ring, which = (ring_h, which) if which < 24 else (ring_d, which - 24)
        top, left = which // 12 * LANES, which % 12 * LANES
        return ring, (slice(top, top + LANES), slice(left, left + LANES))

    blocks_in_row = length // LANES
    window_blocks = WINDOW // LANES + 1
    windows = [range(max(0, at + 1 - window_blocks), at + 1) for at in range(blocks_in_row)]
    mask_first = [sum(len(one) for one in windows[:at]) for at in range(blocks_in_row)]
    sums_first = sum(len(one) for one in windows)
    key_off = lax.broadcasted_iota(jnp.int32, (LANES, LANES), 0)
    query_off = lax.broadcasted_iota(jnp.int32, (LANES, LANES), 1)
    for query_block, window in enumerate(windows):
        for index, key_block in enumerate(window):
            ring, place = ring_block(mask_first[query_block] + index)
            allowed = doc_col[key_block * LANES : (key_block + 1) * LANES, :] == (
                doc_row[:, query_block * LANES : (query_block + 1) * LANES]
            )
            if key_block == query_block:
                allowed = allowed & (key_off <= query_off)
            ring[place] = jnp.where(allowed, 0.0, -1e30)

    select = (lax.broadcasted_iota(jnp.int32, (8, LANES), 1) // HEAD_DIM) == (
        lax.broadcasted_iota(jnp.int32, (8, LANES), 0)
    )
    select = select.astype(F32).astype(BF16)
    half_width = width // 2

    def own_grads(part):
        offset = pl.multiple_of(tp * half_width + part * LANES, LANES)
        offset_up = pl.multiple_of(width + tp * half_width + part * LANES, LANES)
        right = [
            mid_out[:, pl.ds(offset, LANES)],
            mid_out[:, pl.ds(offset_up, LANES)],
            grad_pre[:, pl.ds(offset, LANES)],
        ]
        grad = dot(normed[...], jnp.concatenate(right, 1), 0, 0).astype(BF16)
        low = pl.multiple_of(part * COLUMNS, COLUMNS)
        item_a[:, :, :, :, pl.ds(low, 3 * LANES)] = grad.reshape(nz, ny, 2, piece, 3 * LANES)
        grad = dot(sub_out[...], grad_res[:, pl.ds(offset, LANES)], 0, 0).astype(BF16)
        low = pl.multiple_of(part * COLUMNS + 3 * LANES, LANES)
        item_a[:, :, :, :, pl.ds(low, LANES)] = grad.reshape(nz, ny, 2, piece, LANES)
        start_core(2, part)

    def half_copy(part):
        columns = part_columns(part)
        return remote(half_own.at[:, columns], half_got.at[:, columns], half_sem, part, to_x)

    def finish_own(part):
        finish(2, part)
        half_copy(part).start()

    def gain_step(at):
        gain_add(at)
        if at == 0:
            gain_stage[1].start()
        else:
            for copy in gain_last:
                copy.start()

    def when(condition, *events):
        @pl.when(condition)
        def _():
            for event, *arguments in events:
                event(*arguments)

    def middle(step):
        when(step == 0, (start_z, 0, 2), (gain_step, 0), (start_y, 1, 1))
        when(step == 1, (gain_step, 1), (start_z, 1, 0), (start_y, 2, 0))
        when(step == 2, (start_z, 1, 1), (start_y, 2, 1))
        when(step == 3, (start_z, 2, 1), (start_y, 2, 2))
        when(step == 4, (finish_own, 0))

    def ending(step):
        when(step < parts, (own_grads, step))
        when(step < parts, (finish, 0, step))
        when(step == 2, (start_z, 2, 0))
        when(step == 3, (start_y, 1, 2))
        when(step == 4, (start_z, 2, 2), (finish_own, 1), (finish, 1, 0))
        when(step == 5, (start_z, 1, 2), (finish, 1, 1))

    def pair_back(step, carry):
        pair = lax.rem(tp * (pairs // 2) + step, pairs)
        low = pl.multiple_of(pair * LANES, LANES)
        lanes = pl.ds(low, LANES)
        upper = pl.ds(pl.multiple_of(width + low, LANES), LANES)
        product = grad_att[:, upper].astype(F32) * att[:, lanes]
        high = product.astype(BF16)
        rest = (product - high.astype(F32)).astype(BF16)
        delta[...] = dot(select, high, 1, 1) + dot(select, rest, 1, 1)
        key_t[...] = ks[:, lanes].T
        for which in range(sums_first, sums_first + 2 * blocks_in_row):
            ring, place = ring_block(which)
            ring[place] = jnp.zeros((LANES, LANES), F32)
        weights = jnp.concatenate([weights_c[2 * pair], weights_c[2 * pair + 1]], 1)
        for query_block, window in enumerate(windows):
            if query_block == blocks_in_row // 2:
                middle(step)
            queries = slice(query_block * LANES, (query_block + 1) * LANES)
            keys = slice(window[0] * LANES, queries.stop)
            span = len(window) * LANES
            query = qs[queries, lanes]
            grad_out = grad_att[queries, upper]
            query_two = jnp.concatenate([query * lane_b[0], query * lane_b[1]], 0)
            grad_two = jnp.concatenate([grad_out * lane_b[0], grad_out * lane_b[1]], 0)
            mask = []
            for index in range(len(window)):
                ring, place = ring_block(mask_first[query_block] + index)
                mask.append(ring[place])
            mask = jnp.concatenate(mask, 0)
            mask = jnp.concatenate([mask, mask], 1)
            log_sum = jnp.concatenate([lse[pair, 0:1, queries], lse[pair, 1:2, queries]], 1)
            back = jnp.concatenate([delta[0:1, queries], delta[1:2, queries]], 1)
            power = dot(ks[keys, lanes], query_two, 1, 1) * (HEAD_DIM**-0.5 * LOG2E) + mask
            prob = jnp.exp2(power - log_sum) * repeat(weights, span, 2 * LANES)
            grad_score = prob * (dot(vs[keys, lanes], grad_two, 1, 1) - back)
            grad_score = grad_score.astype(BF16)
            dv = dot(prob.astype(BF16), grad_two, 1, 0)
            dk = dot(grad_score, query_two, 1, 0)
            dq = dot(key_t[:, keys], grad_score, 1, 0) * HEAD_DIM**-0.5
            dq = jnp.concatenate([dq[:HEAD_DIM, :LANES], dq[HEAD_DIM:, LANES:]], 0)
            mid_out[queries, lanes] = dq.T.astype(BF16)
            for index, key_block in enumerate(window):
                part = slice(index * LANES, (index + 1) * LANES)
                ring, place = ring_block(sums_first + key_block)
                ring[place] += dv[part, :]
                ring, place = ring_block(sums_first + blocks_in_row + key_block)
                ring[place] += dk[part, :]
        for block in range(blocks_in_row):
            rows = slice(block * LANES, (block + 1) * LANES)
            ring, place = ring_block(sums_first + block)
            grad_pre[rows, lanes] = ring[place].astype(BF16)
            ring, place = ring_block(sums_first + blocks_in_row + block)
            mid_out[rows, upper] = (ring[place] * HEAD_DIM**-0.5).astype(BF16)

        ending(step)
        return carry

    lax.fori_loop(0, pairs, pair_back, 0)

    stores = []

    def store(near, far, at):
        copy = pltpu.make_async_copy(near, far, store_sem.at[at])
        copy.start()
        stores.append(copy)

    def tokens_back(at, carry):
        rows = pl.ds(pl.multiple_of(at * CHUNK, CHUNK), CHUNK)
        grad = dot(mid_out[rows, 0:width], wq[...], 1, 1)
        grad += dot(mid_out[rows, width : 2 * width], wk[...], 1, 1)
        grad += dot(grad_pre[rows, 0:width], wv[...], 1, 1)
        hat, inv = moments(tok[rows, :].astype(F32))
        gtok[rows, :] += norm_grad(hat, inv, ga, grad)
        pltpu.make_async_copy(gtok.at[rows], gtok_far.at[rows], store_sem.at[at]).start()
        when(at == 1, (finish_own, 2))
        return carry

    lax.fori_loop(0, chunks, tokens_back, 0)
    finish(1, 2)
    for at in range(chunks):
        rows = pl.ds(at * CHUNK, CHUNK)
        stores.append(pltpu.make_async_copy(gtok.at[rows], gtok_far.at[rows], store_sem.at[at]))

    for copy in gain_last:
        copy.wait()
    total = gain_own[...]
    for k in range(1, nz):
        total = total + gain_got[1 + k]
    o_gain[0:8, :] = pltpu.roll(total, lax.rem(width - piece * row, width), 1)[:, :LANES]
    per_row = 2 * piece
    o_gain[8:16, :] = pltpu.roll(total, lax.rem(2 * width - per_row * row, width), 1)[:, :LANES]

    for at in range(chunks):
        rows = pl.ds(at * CHUNK, CHUNK)
        ffp_copy(at).wait()
        total = ffp_own[rows, :].astype(F32) + ffp_got[rows, :].astype(F32)
        ffp_own[rows, :] = (mid[rows, :] + total).astype(BF16)
        store(ffp_own.at[rows], out_far.at[rows], chunks + at)

    for part in range(pairs // 2):
        half_copy(part).wait()
    mine_at = pl.multiple_of(tp * half_width, LANES)
    other_at = pl.multiple_of((1 - tp) * half_width, LANES)
    for part in range(pairs // 2):
        mine, other = (
            pl.ds(pl.multiple_of(begin + part * LANES, LANES), LANES)
            for begin in (mine_at, other_at)
        )
        for index, target in enumerate((o_query, o_key, o_value, o_out)):
            low = part * COLUMNS + index * LANES
            target[:, mine] = half_own[:, low : low + LANES].astype(F32)
            target[:, other] = half_got[:, low : low + LANES].astype(F32)
    own_rows = pl.ds(pl.multiple_of(piece * row, 16), piece)
    product = wq[own_rows, :].astype(F32) * o_query[...]
    product += wk[own_rows, :].astype(F32) * o_key[...]
    product += wv[own_rows, :].astype(F32) * o_value[...]
    total = jnp.broadcast_to(jnp.sum(product, -1, keepdims=True), (piece, LANES))
    total = jnp.concatenate([total, jnp.zeros((LANES - piece, LANES), F32)], 0).T
    gain = pltpu.roll(repeat(ga, 8, width), lax.rem(width - piece * row, width), 1)
    o_gain[0:1, :] = total[0:1, :] / gain[0:1, :LANES]
    for copy in stores:
        copy.wait()


def write_kernel(places, *refs):
    far_in, gain_in, far_out, gains_out = refs[:8], refs[8], refs[9:17], refs[17:21]
    near, sems = refs[21:29], refs[29]
    g_attn, g_sub, g_ffn, g_mid = gains_out
    nz, ny = places
    row = lax.axis_index("row")
    width = far_in[0].shape[1]
    piece = far_in[2].shape[0]
    steps = []
    for at in range(8):
        length = far_in[at].shape[0]
        size = CHUNK if length > CHUNK else length
        for begin in range(0, length, size):
            rows, which = pl.ds(begin, size), len(steps)
            steps.append(
                (
                    pltpu.make_async_copy(
                        far_in[at].at[rows], near[at].at[rows], sems.at[0, which]
                    ),
                    pltpu.make_async_copy(
                        near[at].at[rows], far_out[at].at[rows], sems.at[1, which]
                    ),
                )
            )
    for load, _ in steps:
        load.start()
    tile = gain_in[...]
    g_attn[...] = tile[0, :piece]
    g_sub[...] = tile[1, :piece]
    g_ffn[...] = tile[2, :piece]
    later = (2 * piece * row) // width
    g_mid[...] = jnp.where(later == 0, tile[11, : 2 * piece], tile[12, : 2 * piece])
    for load, save in steps:
        load.wait()
        save.start()
    for _, save in steps:
        save.wait()


def fused_body(places, *args):
    (tokens, doc_ids, dilations, cotangent, w_query, w_key, w_value, w_out, w_up, w_down) = args[:10]
    gains = args[10:]
    nz, ny = places
    length, width = tokens.shape
    half = w_up.shape[1]
    piece = width // (2 * nz * ny)
    chunks = length // CHUNK
    vmem = pl.BlockSpec(memory_space=pltpu.VMEM)
    smem = pl.BlockSpec(memory_space=pltpu.SMEM)
    far = pl.BlockSpec(memory_space=pl.ANY)
    shape = jax.ShapeDtypeStruct
    low = functools.partial(pltpu.VMEM, dtype=BF16)
    full = functools.partial(pltpu.VMEM, dtype=F32)
    rows_low, rows_full = low((length, width)), full((length, width))
    item = low((nz, ny, 2, piece, half))
    square = low((width, width))
    count = 3 * half // COLUMNS
    dma = lambda number: pltpu.SemaphoreType.DMA((2, number))
    big = [
        shape((length, width), BF16),
        shape((length, width), F32),
        shape((piece, width), F32),
        shape((piece, width), F32),
        shape((piece, width), F32),
        shape((piece, width), F32),
        shape((piece, half), F32),
        shape((piece, half), F32),
    ]
    results = pl.pallas_call(
        functools.partial(layer_kernel, places),
        out_shape=big + [shape((16, LANES), F32)],
        in_specs=[smem] + [vmem] * 5 + [far] * 8,
        out_specs=[far] * 2 + [vmem] * 7,
        scratch_shapes=[
            rows_low,
            rows_low,
            square,
            square,
            square,
            square,
            item,
            low((half, width)),
            rows_full,
            rows_low,
            rows_low,
            rows_low,
            rows_full,
            rows_full,
            rows_low,
            low((length, half)),
            low((length, half)),
            full((CHUNK, half)),
            full((CHUNK, half)),
            rows_low,
            rows_low,
            rows_low,
            rows_low,
            full((HEADS, 16, LANES)),
            full((length, LANES)),
            full((width // LANES, 2, length)),
            full((8, length)),
            low((LANES, length)),
            full((chunks, 8, CHUNK)),
            full((chunks, 8, CHUNK)),
            full((8, half)),
            full((8, width)),
            full((1 + nz, 8, width)),
            item,
            item,
            low((6, nz, ny, piece, COLUMNS)),
            low((6, nz, piece, COLUMNS)),
            low((count, nz - 1, piece, COLUMNS)),
            low((piece, half)),
            low((piece, half)),
            dma(chunks),
            dma(chunks),
            dma(chunks),
            dma(8 * count),
            dma(1 + nz),
            dma(width // LANES // 2),
            pltpu.SemaphoreType.DMA((8,)),
            pltpu.SemaphoreType.DMA((2 * chunks,)),
        ],
        compiler_params=pltpu.CompilerParams(
            collective_id=0, has_side_effects=True, vmem_limit_bytes=63 * MIB
        ),
        name="layer",
    )(
        dilations,
        doc_ids.reshape(1, length),
        *gains,
        tokens,
        cotangent,
        w_query,
        w_key,
        w_value,
        w_out,
        w_up.reshape(nz, ny, 2, piece, half),
        w_down,
    )
    flat = shape((piece,), F32)
    moves = 2 * (length // CHUNK) + 6
    final = pl.pallas_call(
        functools.partial(write_kernel, places),
        out_shape=big + [flat, flat, flat, shape((2 * piece,), F32)],
        in_specs=[far] * 8 + [vmem],
        out_specs=[far] * 8 + [vmem] * 4,
        scratch_shapes=[pltpu.VMEM(one.shape, one.dtype) for one in big]
        + [pltpu.SemaphoreType.DMA((2, moves))],
        compiler_params=pltpu.CompilerParams(vmem_limit_bytes=63 * MIB),
        name="write",
    )(*results)
    return (*final[:7], final[7].T, *final[8:])


def norm_parts(value):
    row_mean = jnp.mean(value, -1, keepdims=True)
    centred = value - row_mean
    inv_std = lax.rsqrt(jnp.mean(centred * centred, -1, keepdims=True) + EPS)
    return (centred * inv_std, inv_std)


def norm_back(normed_hat, inv_std, gain, grad):
    scaled = grad * gain
    grad_value = inv_std * (
        scaled
        - jnp.mean(scaled, -1, keepdims=True)
        - normed_hat * jnp.mean(scaled * normed_hat, -1, keepdims=True)
    )
    return (grad_value, jnp.sum(grad * normed_hat, 0))


def selection(dilations, positions):
    head_ids = jnp.arange(HEADS, dtype=jnp.int32)
    left_side = positions[None, None, :] % dilations[:, None, None]
    right_side = head_ids[None, :, None] % dilations[:, None, None]
    return (left_side == right_side).astype(jnp.float32)


def pattern_weights(dilations, doc_row, query_pos, query_docs):
    key_pos = jnp.arange(doc_row.shape[0], dtype=jnp.int32)
    counts = jnp.einsum(
        "phi,phj->hij", selection(dilations, query_pos), selection(dilations, key_pos)
    )
    allowed = (query_pos[:, None] >= key_pos[None, :]) & (query_docs[:, None] == doc_row[None, :])
    return counts * allowed.astype(jnp.float32)[None]


def attn_forward(dilations, doc_row, key_heads, value_heads, query_block, query_pos, query_docs):
    score_scale = HEAD_DIM ** (-0.5)
    scores = (
        jnp.einsum("ihe,jhe->hij", query_block, key_heads, preferred_element_type=jnp.float32)
        * score_scale
    )
    weights_mult = pattern_weights(dilations, doc_row, query_pos, query_docs)
    masked = jnp.where(weights_mult > 0, scores, -1e30)
    row_max = jnp.max(masked, -1, keepdims=True)
    expo = weights_mult * jnp.exp(masked - row_max)
    totals = jnp.sum(expo, -1, keepdims=True)
    attn_prob = (expo / totals).astype(jnp.bfloat16)
    out_block = jnp.einsum(
        "hij,jhe->ihe", attn_prob, value_heads, preferred_element_type=jnp.float32
    )
    return (out_block, row_max[..., 0] + jnp.log(totals[..., 0]))


def attn_backward(
    dilations,
    doc_row,
    key_heads,
    value_heads,
    query_block,
    query_pos,
    query_docs,
    lse_block,
    grad_block,
):
    score_scale = HEAD_DIM ** (-0.5)
    scores = (
        jnp.einsum("ihe,jhe->hij", query_block, key_heads, preferred_element_type=jnp.float32)
        * score_scale
    )
    weights_mult = pattern_weights(dilations, doc_row, query_pos, query_docs)
    attn_full = weights_mult * jnp.exp(scores - lse_block[:, :, None])
    attn_low = attn_full.astype(jnp.bfloat16)
    value_part = jnp.einsum(
        "hij,ihe->jhe", attn_low, grad_block, preferred_element_type=jnp.float32
    )
    grad_prob = jnp.einsum(
        "ihe,jhe->hij", grad_block, value_heads, preferred_element_type=jnp.float32
    )
    row_delta = jnp.sum(attn_full * grad_prob, -1, keepdims=True)
    grad_scores = (attn_full * (grad_prob - row_delta)).astype(jnp.bfloat16)
    query_grad = (
        jnp.einsum("hij,jhe->ihe", grad_scores, key_heads, preferred_element_type=jnp.float32)
        * score_scale
    )
    key_part = (
        jnp.einsum("hij,ihe->jhe", grad_scores, query_block, preferred_element_type=jnp.float32)
        * score_scale
    )
    return (query_grad, key_part, value_part)


def general_body(
    tokens,
    doc_ids,
    dilations,
    cotangent,
    w_query,
    w_key,
    w_value,
    w_out,
    w_up,
    w_down,
    gain_attn,
    gain_sub,
    gain_ffn,
    gain_mid,
):
    row_len = tokens.shape[0]
    width = tokens.shape[1]
    block_rows = min(512, row_len)
    block_count = row_len // block_rows
    doc_row = doc_ids.reshape(row_len)
    row_in = tokens.astype(jnp.float32)
    attn_hat, attn_std = norm_parts(row_in)
    normed = (attn_hat * gain_attn).astype(jnp.bfloat16)
    keys_low = jnp.dot(normed, w_key, preferred_element_type=jnp.float32).astype(jnp.bfloat16)
    values_low = jnp.dot(normed, w_value, preferred_element_type=jnp.float32).astype(jnp.bfloat16)
    key_heads = keys_low.reshape(row_len, HEADS, HEAD_DIM)
    value_heads = values_low.reshape(row_len, HEADS, HEAD_DIM)
    queries = jnp.dot(normed, w_query, preferred_element_type=jnp.float32).astype(jnp.bfloat16)
    query_heads = queries.reshape(row_len, HEADS, HEAD_DIM)

    def attend(block_index):
        offset = block_index * block_rows
        query_block = lax.dynamic_slice_in_dim(query_heads, offset, block_rows, 0)
        query_pos = offset + jnp.arange(block_rows, dtype=jnp.int32)
        query_docs = lax.dynamic_slice_in_dim(doc_row, offset, block_rows, 0)
        return attn_forward(
            dilations, doc_row, key_heads, value_heads, query_block, query_pos, query_docs
        )

    out_blocks, log_sums = lax.map(attend, jnp.arange(block_count))
    attended = out_blocks.reshape(row_len, width)
    sub_hat, sub_std = norm_parts(attended)
    sub_out = (sub_hat * gain_sub).astype(jnp.bfloat16)
    mid_res = row_in + jnp.dot(sub_out, w_out, preferred_element_type=jnp.float32)
    ffn_hat, ffn_std = norm_parts(mid_res)
    ffn_in = (ffn_hat * gain_ffn).astype(jnp.bfloat16)
    hidden_pre = jnp.dot(ffn_in, w_up, preferred_element_type=jnp.float32)
    hidden_act = jax.nn.gelu(hidden_pre, approximate=False)
    sum_first, sum_second = lax.psum(
        (jnp.sum(hidden_act, -1), jnp.sum(hidden_act * hidden_act, -1)), "tp"
    )
    mid_mean = sum_first[:, None] / FF
    mid_std = lax.rsqrt(sum_second[:, None] / FF - mid_mean * mid_mean + EPS)
    mid_hat = (hidden_act - mid_mean) * mid_std
    mid_out = (mid_hat * gain_mid).astype(jnp.bfloat16)
    ffn_part = jnp.dot(mid_out, w_down, preferred_element_type=jnp.float32)
    ffn_total = lax.psum(ffn_part, "tp")
    output = (mid_res + ffn_total).astype(jnp.bfloat16)
    grad_down = jnp.einsum("lf,ld->fd", mid_out, cotangent, preferred_element_type=jnp.float32)
    grad_mid_out = jnp.einsum("ld,fd->lf", cotangent, w_down, preferred_element_type=jnp.float32)
    grad_gain_mid = jnp.sum(grad_mid_out * mid_hat, 0)
    scaled = grad_mid_out * gain_mid
    back_first, back_second = lax.psum((jnp.sum(scaled, -1), jnp.sum(scaled * mid_hat, -1)), "tp")
    grad_act = mid_std * (scaled - back_first[:, None] / FF - mid_hat * back_second[:, None] / FF)
    gelu_pull = jax.vjp(lambda value: jax.nn.gelu(value, approximate=False), hidden_pre)[1]
    grad_pre = gelu_pull(grad_act)[0].astype(jnp.bfloat16)
    grad_up = jnp.einsum("ld,lf->df", ffn_in, grad_pre, preferred_element_type=jnp.float32)
    sum_up, sum_down, sum_gain_mid = (
        lax.psum_scatter(grad_up, "row", scatter_dimension=0, tiled=True),
        lax.psum_scatter(grad_down, "row", scatter_dimension=1, tiled=True),
        lax.psum_scatter(grad_gain_mid, "row", scatter_dimension=0, tiled=True),
    )
    grad_ffn_part = jnp.einsum("lf,df->ld", grad_pre, w_up, preferred_element_type=jnp.float32)
    grad_ffn_in = lax.psum(grad_ffn_part, "tp")
    grad_mid_in, grad_gain_ffn = norm_back(ffn_hat, ffn_std, gain_ffn, grad_ffn_in)
    grad_mid_res = cotangent.astype(jnp.float32) + grad_mid_in
    grad_res_low = grad_mid_res.astype(jnp.bfloat16)
    grad_out = jnp.einsum("ld,le->de", sub_out, grad_res_low, preferred_element_type=jnp.float32)
    grad_sub_out = jnp.einsum("le,de->ld", grad_res_low, w_out, preferred_element_type=jnp.float32)
    grad_attended, grad_gain_sub = norm_back(sub_hat, sub_std, gain_sub, grad_sub_out)
    grad_att_low = grad_attended.astype(jnp.bfloat16)
    grad_heads = grad_att_low.reshape(row_len, HEADS, HEAD_DIM)

    def attend_back(running, block_index):
        key_sum, value_sum = running
        offset = block_index * block_rows
        query_block = lax.dynamic_slice_in_dim(query_heads, offset, block_rows, 0)
        query_pos = offset + jnp.arange(block_rows, dtype=jnp.int32)
        query_docs = lax.dynamic_slice_in_dim(doc_row, offset, block_rows, 0)
        grad_block = lax.dynamic_slice_in_dim(grad_heads, offset, block_rows, 0)
        query_grad, key_part, value_part = attn_backward(
            dilations,
            doc_row,
            key_heads,
            value_heads,
            query_block,
            query_pos,
            query_docs,
            log_sums[block_index],
            grad_block,
        )
        return ((key_sum + key_part, value_sum + value_part), query_grad)

    zero_heads = jnp.zeros((row_len, HEADS, HEAD_DIM), jnp.float32)
    (key_grad, value_grad), query_blocks = lax.scan(
        attend_back, (zero_heads, zero_heads), jnp.arange(block_count)
    )
    grad_queries = query_blocks.reshape(row_len, width).astype(jnp.bfloat16)
    grad_keys = key_grad.reshape(row_len, width).astype(jnp.bfloat16)
    grad_values = value_grad.reshape(row_len, width).astype(jnp.bfloat16)
    grad_query = jnp.einsum("ld,le->de", normed, grad_queries, preferred_element_type=jnp.float32)
    grad_key = jnp.einsum("ld,le->de", normed, grad_keys, preferred_element_type=jnp.float32)
    grad_value = jnp.einsum("ld,le->de", normed, grad_values, preferred_element_type=jnp.float32)
    grad_normed = (
        jnp.einsum("le,de->ld", grad_queries, w_query, preferred_element_type=jnp.float32)
        + jnp.einsum("le,de->ld", grad_keys, w_key, preferred_element_type=jnp.float32)
        + jnp.einsum("le,de->ld", grad_values, w_value, preferred_element_type=jnp.float32)
    )
    grad_row_in, grad_gain_attn = norm_back(attn_hat, attn_std, gain_attn, grad_normed)
    grad_tokens = grad_mid_res + grad_row_in
    sum_query, sum_key, sum_value, sum_out, sum_gain_attn, sum_gain_sub, sum_gain_ffn = (
        lax.psum_scatter(grad_query, "row", scatter_dimension=0, tiled=True),
        lax.psum_scatter(grad_key, "row", scatter_dimension=0, tiled=True),
        lax.psum_scatter(grad_value, "row", scatter_dimension=0, tiled=True),
        lax.psum_scatter(grad_out, "row", scatter_dimension=0, tiled=True),
        lax.psum_scatter(grad_gain_attn, "row", scatter_dimension=0, tiled=True),
        lax.psum_scatter(grad_gain_sub, "row", scatter_dimension=0, tiled=True),
        lax.psum_scatter(grad_gain_ffn, "row", scatter_dimension=0, tiled=True),
    )
    return (
        output,
        grad_tokens,
        sum_query,
        sum_key,
        sum_value,
        sum_out,
        sum_up,
        sum_down,
        sum_gain_attn,
        sum_gain_sub,
        sum_gain_ffn,
        sum_gain_mid,
    )


def solution(mesh):
    rows, columns = mesh.shape["row"], mesh.shape["tp"]
    if columns == 2 and rows == 16:
        body = functools.partial(fused_body, (rows // 4, 2))
    else:
        body = general_body
    return jax.shard_map(
        body,
        mesh=mesh,
        in_specs=(
            P("row", None),
            P("row", None),
            P(),
            P("row", None),
            P(),
            P(),
            P(),
            P(),
            P(None, "tp"),
            P("tp", None),
            P(),
            P(),
            P(),
            P("tp"),
        ),
        out_specs=(
            P("row", None),
            P("row", None),
            P("row", None),
            P("row", None),
            P("row", None),
            P("row", None),
            P("row", "tp"),
            P("tp", "row"),
            P("row"),
            P("row"),
            P("row"),
            P(("tp", "row")),
        ),
        check_vma=False,
    )
```

```python
import functools

import jax
import jax.numpy as jnp
from jax import lax
from jax.experimental import pallas as pl
from jax.experimental.pallas import tpu as pltpu
from jax.sharding import PartitionSpec as P

MESH = pl.DeviceIdType.MESH
HEADS = 12
HEAD_DIM = 64
FF = 3072
EPS = 1e-05
F32 = jnp.float32
BF16 = jnp.bfloat16
LOG2E = 1.4426950408889634
CHUNK = 256
WINDOW = 512
PAIR_GROUP = 2
COLUMNS = 512
LANES = 128
MIB = 2**20


def dot(left, right, left_dim, right_dim):
    return lax.dot_general(
        left, right, (((left_dim,), (right_dim,)), ((), ())), preferred_element_type=F32
    )


def moments(value):
    mean = jnp.mean(value, -1, keepdims=True)
    centred = value - mean
    inv = lax.rsqrt(jnp.mean(centred * centred, -1, keepdims=True) + EPS)
    return centred * inv, inv


def norm_grad(hat, inv, gain, grad):
    scaled = grad * gain
    first = jnp.mean(scaled, -1, keepdims=True)
    second = jnp.mean(scaled * hat, -1, keepdims=True)
    return inv * (scaled - first - hat * second)


def repeat(tile, rows, columns):
    tall = jnp.concatenate([tile] * (rows // tile.shape[0]), 0)
    return jnp.concatenate([tall] * (columns // tile.shape[1]), 1)


def layer_kernel(
    places,
    dil,
    doc,
    ga_flat,
    gs_flat,
    gf_flat,
    gm_flat,
    tok_far,
    cot_far,
    wq_far,
    wk_far,
    wv_far,
    wo_far,
    wup_far,
    wdn_far,
    out_far,
    gtok_far,
    o_query,
    o_key,
    o_value,
    o_out,
    o_up,
    o_down,
    o_gain,
    tok,
    cot,
    wq,
    wk,
    wv,
    wo,
    wup_near,
    wdn,
    gtok,
    qs,
    ks,
    vs,
    att,
    mid,
    ffn_in,
    mid_out,
    grad_pre,
    ring_h,
    ring_d,
    gffn_own,
    gffn_got,
    ffp_own,
    ffp_got,
    weights_c,
    doc_col,
    lse,
    delta,
    key_t,
    stat_own,
    stat_got,
    gain_mid_sum,
    gain_own,
    gain_got,
    item_u,
    item_d,
    got_core,
    got_y,
    got_z,
    half_own,
    half_got,
    stat_sem,
    gffn_sem,
    ffp_sem,
    item_sem,
    gain_sem,
    half_sem,
    load_sem,
    store_sem,
):
    nz, ny = places
    row, tp = lax.axis_index("row"), lax.axis_index("tp")
    core = lax.rem(row, 2)
    y_at = lax.rem(row // 2, ny)
    z_at = row // (2 * ny)
    to_x = (row, 1 - tp)
    to_core = (row + 1 - 2 * core, tp)
    to_y = (row + 2 - 4 * y_at, tp)
    to_z = [
        (lax.rem(z_at + k, nz) * (2 * ny) + lax.rem(row, 2 * ny), tp) for k in range(1, nz)
    ]
    length, width = tok.shape
    half = wdn.shape[0]
    chunks = length // CHUNK
    pairs = width // LANES
    piece = width // (nz * ny * 2)

    ga, gs, gf, gm = [
        gain[...].reshape(1, gain.shape[0]) for gain in (ga_flat, gs_flat, gf_flat, gm_flat)
    ]
    loads = [
        pltpu.make_async_copy(far, near, load_sem.at[at])
        for at, (far, near) in enumerate(
            (
                (tok_far, tok),
                (wq_far, wq),
                (wk_far, wk),
                (wv_far, wv),
                (wo_far, wo),
                (wup_far, wup_near),
                (cot_far, cot),
                (wdn_far, wdn),
            )
        )
    ]
    for load in loads:
        load.start()
    barrier = pltpu.get_barrier_semaphore()
    partners = [to_x, to_core, to_y] + to_z
    for partner in partners:
        pl.semaphore_signal(barrier, inc=1, device_id=partner, device_id_type=MESH)

    def remote(src, dst, sems, at, partner):
        return pltpu.make_async_remote_copy(
            src_ref=src,
            dst_ref=dst,
            send_sem=sems.at[0, at],
            recv_sem=sems.at[1, at],
            device_id=partner,
            device_id_type=MESH,
        )

    lane = lax.broadcasted_iota(jnp.int32, (1, LANES), 1)
    low_lane = lane < HEAD_DIM
    lane_f = [low_lane.astype(F32), 1.0 - low_lane.astype(F32)]
    lane_b = [value.astype(BF16) for value in lane_f]

    row_at = lax.broadcasted_iota(jnp.int32, (16, LANES), 0)
    col_at = lax.broadcasted_iota(jnp.int32, (16, LANES), 1)
    for head in range(HEADS):
        row_count = jnp.zeros((16, LANES), F32)
        col_count = jnp.zeros((16, LANES), F32)
        for pattern in range(dil.shape[0]):
            last = dil[pattern] - 1
            row_count += (((row_at - head) & last) == 0).astype(F32)
            col_count += (((col_at - head) & last) == 0).astype(F32)
        weights_c[head] = jnp.minimum(row_count, col_count)
    for block in range(length // LANES):
        ids = doc[:, block * LANES : (block + 1) * LANES].astype(F32)
        doc_col[block * LANES : (block + 1) * LANES, :] = jnp.broadcast_to(ids, (LANES, LANES)).T
    doc_row = doc[...].astype(F32)
    bias = gtok
    value_t = ffp_own
    gain_mid_sum[...] = jnp.zeros_like(gain_mid_sum)
    gain_own[...] = jnp.zeros_like(gain_own)

    def project(at):
        rows = rows_of(at)
        hat, _ = moments(tok[rows, :].astype(F32))
        value = (hat * ga).astype(BF16)
        qs[rows, :] = dot(value, wq[...], 1, 0).astype(BF16)
        ks[rows, :] = dot(value, wk[...], 1, 0).astype(BF16)
        vs[rows, :] = dot(value, wv[...], 1, 0).astype(BF16)

    def rows_of(at):
        return pl.ds(at * CHUNK if isinstance(at, int) else pl.multiple_of(at * CHUNK, CHUNK), CHUNK)

    def value_block(pair, block):
        down, right = 2 * block + pair // 3, lax.rem(pair, 3)
        return (
            pl.ds(pl.multiple_of(down * LANES, LANES), LANES),
            pl.ds(pl.multiple_of(right * CHUNK, CHUNK), CHUNK),
        )

    def attend(at, span):
        first = at * CHUNK
        start = first + CHUNK - span
        start_block = at + 1 - span // CHUNK
        rows, keys = rows_of(at), pl.ds(pl.multiple_of(start, CHUNK), span)
        key_off = lax.broadcasted_iota(jnp.int32, (CHUNK, LANES), 0)
        query_off = lax.broadcasted_iota(jnp.int32, (CHUNK, LANES), 1)
        for block in range(span // CHUNK):
            low = pl.multiple_of(start + block * CHUNK, CHUNK)
            key_docs = doc_col[pl.ds(low, CHUNK), :]
            for side in range(CHUNK // LANES):
                begin = pl.multiple_of(first + side * LANES, LANES)
                allowed = key_docs == doc[:, pl.ds(begin, LANES)].astype(F32)
                allowed = allowed & (key_off + low <= query_off + begin)
                bias[block * CHUNK : (block + 1) * CHUNK, side * LANES : (side + 1) * LANES] = (
                    jnp.where(allowed, 0.0, -1e30)
                )

        def flip(pair, carry):
            lanes = pl.ds(pl.multiple_of(pair * LANES, LANES), LANES)
            value_t[value_block(pair, at)] = vs[rows, lanes].T
            return carry

        lax.fori_loop(0, pairs, flip, 0)
        ones = jnp.ones((16, CHUNK), BF16)

        def pair_step(step, carry):
            group = [step * PAIR_GROUP + at for at in range(PAIR_GROUP)]
            scores = []
            for pair in group:
                lanes = pl.ds(pl.multiple_of(pair * LANES, LANES), LANES)
                query = qs[rows, lanes]
                query_two = jnp.concatenate([query * lane_b[0], query * lane_b[1]], 0)
                scores.append(dot(ks[keys, lanes], query_two, 1, 1))
            for pair, score in zip(group, scores):
                lanes = pl.ds(pl.multiple_of(pair * LANES, LANES), LANES)
                parts = []
                for side in range(2):
                    power = score[:, side * CHUNK : (side + 1) * CHUNK]
                    power = power * (HEAD_DIM**-0.5 * LOG2E) + bias[0:span, 0:CHUNK]
                    top = jnp.max(power, 0, keepdims=True)
                    expo = jnp.exp2(power - top) * repeat(weights_c[2 * pair + side], span, CHUNK)
                    expo = expo.astype(BF16)
                    total = jnp.zeros((HEAD_DIM + 16, CHUNK), F32)
                    for block in range(span // CHUNK):
                        value = value_t[value_block(pair, start_block + block)]
                        value = value[side * HEAD_DIM : (side + 1) * HEAD_DIM, :]
                        total += dot(
                            jnp.concatenate([value, ones], 0),
                            expo[block * CHUNK : (block + 1) * CHUNK, :],
                            1,
                            0,
                        )
                    summed = total[HEAD_DIM : HEAD_DIM + 1, :]
                    parts.append(total[:HEAD_DIM, :] * (1.0 / summed))
                    lse[pair, side : side + 1, rows] = top + jnp.log2(summed)
                att[rows, lanes] = jnp.concatenate(parts, 0).T
            return carry

        lax.fori_loop(0, pairs // PAIR_GROUP, pair_step, 0)

    blocks = [slice(low, low + COLUMNS) for low in range(0, half, COLUMNS)]

    def fold(value):
        return sum(value[:, low : low + LANES] for low in range(0, COLUMNS, LANES))

    def feed(at):
        rows = rows_of(at)
        hat, _ = moments(att[rows, :])
        sub = (hat * gs).astype(BF16)
        mid_res = tok[rows, :].astype(F32) + dot(sub, wo[...], 1, 0)
        mid[rows, :] = mid_res
        hat, _ = moments(mid_res)
        value = (hat * gf).astype(BF16)
        ffn_in[rows, :] = value
        sums = [jnp.zeros((CHUNK, LANES), F32)] * 4

        def products(part):
            weights = wup_near[:, :, :, :, part].reshape(width, COLUMNS)
            return dot(value, weights, 1, 0), dot(cot[rows, :], wdn[part, :], 1, 1)

        later = products(blocks[0])
        for index, part in enumerate(blocks):
            pre, grad = later
            if index + 1 < len(blocks):
                later = products(blocks[index + 1])
            ring_h[:, part] = pre
            ring_d[:, part] = grad
            act = 0.5 * pre * (1.0 + lax.erf(pre * 0.7071067811865476))
            scaled = grad * gm[:, part]
            terms = (act, act * act, scaled, scaled * act)
            sums = [total + fold(term) for total, term in zip(sums, terms)]
        sums = [jnp.sum(total, -1, keepdims=True) for total in sums]
        tile = jnp.where(lane == 0, sums[0], jnp.where(lane == 1, sums[1], 0.0))
        tile = jnp.where(lane == 2, sums[2], jnp.where(lane == 3, sums[3], tile))
        stat_own[at] = tile.T[0:8, :]
        remote(stat_own.at[at], stat_got.at[at], stat_sem, at, to_x).start()

    def gffn_copy(at):
        rows = rows_of(at)
        return remote(gffn_own.at[rows], gffn_got.at[rows], gffn_sem, at, to_x)

    def ffp_copy(at):
        rows = pl.ds(at * CHUNK, CHUNK)
        return remote(ffp_own.at[rows], ffp_got.at[rows], ffp_sem, at, to_x)

    def feed_back(at):
        rows = rows_of(at)
        remote(stat_own.at[at], stat_got.at[at], stat_sem, at, to_x).wait()
        both = stat_own[at] + stat_got[at]
        both = jnp.concatenate([both, jnp.zeros((LANES - 8, CHUNK), F32)], 0).T
        mean = both[:, 0:1] / FF
        inv = lax.rsqrt(both[:, 1:2] / FF - mean * mean + EPS)
        first = both[:, 2:3] / FF
        second = inv * (both[:, 3:4] - mean * both[:, 2:3]) / FF
        total = jnp.zeros((CHUNK, width), F32)
        for part in blocks:
            pre = ring_h[:, part]
            grad = ring_d[:, part]
            cdf = 0.5 * (1.0 + lax.erf(pre * 0.7071067811865476))
            slope = cdf + pre * (jnp.exp2(pre * pre * (-0.5 * LOG2E)) * 0.3989422804014327)
            hat = (pre * cdf - mean) * inv
            mid_out[rows, part] = (hat * gm[:, part]).astype(BF16)
            gain_part = grad * hat
            gain_mid_sum[:, part] += sum(gain_part[8 * i : 8 * i + 8, :] for i in range(CHUNK // 8))
            back = inv * (grad * gm[:, part] - first - hat * second)
            back = (back * slope).astype(BF16)
            grad_pre[rows, part] = back
            total += dot(back, wup_near[:, :, :, :, part].reshape(width, COLUMNS), 1, 1)
        gffn_own[rows, :] = total.astype(BF16)

    def project_down(at):
        rows = rows_of(at)
        ffp_own[rows, :] = dot(mid_out[rows, :], wdn[...], 1, 0).astype(BF16)

    for load in loads[:4]:
        load.wait()
    widest = WINDOW // CHUNK

    def early_down(at, carry):
        project_down(at)
        return carry

    def chunk_step(at, carry):
        @pl.when(at < chunks)
        def _():
            project(at)

        for place in range(widest):

            @pl.when(at == place)
            def _():
                attend(place, (place + 1) * CHUNK)

        @pl.when((at >= widest) & (at < chunks))
        def _():
            attend(at, (widest + 1) * CHUNK)

        @pl.when(at == 0)
        def _():
            for load in loads[4:]:
                load.wait()
            pl.semaphore_wait(barrier, len(partners))

        @pl.when(at == chunks)
        def _():
            lax.fori_loop(0, chunks - 1, early_down, 0)

        @pl.when(at >= 1)
        def _():
            feed_back(at - 1)

        @pl.when(at < chunks)
        def _():
            feed(at)

        @pl.when(at >= 1)
        def _():
            gffn_copy(at - 1).start()

        return carry

    lax.fori_loop(0, chunks + 1, chunk_step, 0)

    item_a = wup_near
    items = (item_u, item_d, item_a)
    parts = half // COLUMNS

    def part_columns(part):
        if isinstance(part, int):
            return slice(part * COLUMNS, (part + 1) * COLUMNS)
        return pl.ds(pl.multiple_of(part * COLUMNS, COLUMNS), COLUMNS)

    def slot(group, part):
        return (group % 2) * parts + part

    def sem_at(group, part):
        return 8 * (group * parts + part)

    def core_copy(group, part):
        return remote(
            items[group].at[:, :, 1 - core, :, part_columns(part)],
            got_core.at[slot(group, part)],
            item_sem,
            sem_at(group, part),
            to_core,
        )

    def y_copy(group, part):
        return remote(
            items[group].at[:, 1 - y_at, core, :, part_columns(part)],
            got_y.at[slot(group, part)],
            item_sem,
            sem_at(group, part) + 1,
            to_y,
        )

    def z_copies(group, part):
        return [
            remote(
                items[group].at[lax.rem(z_at + k, nz), y_at, core, :, part_columns(part)],
                got_z.at[group * parts + part, k - 1],
                item_sem,
                sem_at(group, part) + 1 + k,
                to_z[k - 1],
            )
            for k in range(1, nz)
        ]

    def start_core(group, part):
        core_copy(group, part).start()

    def start_y(group, part):
        core_copy(group, part).wait()
        item, columns = items[group], part_columns(part)

        def add(index, carry):
            z_to, y_to = index // ny, lax.rem(index, ny)
            total = item[z_to, y_to, core, :, columns].astype(F32)
            total += got_core[slot(group, part), z_to, y_to].astype(F32)
            item[z_to, y_to, core, :, columns] = total.astype(BF16)
            return carry

        lax.fori_loop(0, nz * ny, add, 0)
        y_copy(group, part).start()

    def start_z(group, part):
        y_copy(group, part).wait()
        item, columns = items[group], part_columns(part)

        def add(z_to, carry):
            total = item[z_to, y_at, core, :, columns].astype(F32)
            total += got_y[slot(group, part), z_to].astype(F32)
            item[z_to, y_at, core, :, columns] = total.astype(BF16)
            return carry

        lax.fori_loop(0, nz, add, 0)
        for copy in z_copies(group, part):
            copy.start()

    def finish(group, part):
        for copy in z_copies(group, part):
            copy.wait()
        columns = part_columns(part)
        total = items[group][z_at, y_at, core, :, columns].astype(F32)
        for k in range(1, nz):
            total = total + got_z[group * parts + part, k - 1].astype(F32)
        if group == 2:
            half_own[:, columns] = total.astype(BF16)
        else:
            (o_up, o_down)[group][:, columns] = total

    def outer(group, left, right, part):
        columns = part_columns(part)
        product = dot(left[...], right[:, columns], 0, 0).astype(BF16)
        items[group][:, :, :, :, columns] = product.reshape(nz, ny, 2, piece, COLUMNS)
        start_core(group, part)

    gain_stage = [
        remote(gain_own, gain_got.at[at], gain_sem, at, partner)
        for at, partner in ((0, to_core), (1, to_y))
    ]
    gain_last = [
        remote(gain_own, gain_got.at[1 + k], gain_sem, 1 + k, to_z[k - 1]) for k in range(1, nz)
    ]

    def gain_add(at):
        gain_stage[at].wait()
        gain_own[...] += gain_got[at]

    def outer_up(part, carry):
        outer(0, ffn_in, grad_pre, part)

        @pl.when(part >= 1)
        def _():
            start_y(0, part - 1)

        return carry

    def outer_down(part, carry):
        outer(1, cot, mid_out, part)
        return carry

    lax.fori_loop(0, parts, outer_up, 0)
    lax.fori_loop(0, parts, outer_down, 0)
    project_down(chunks - 1)
    ffp_copy(0).start()
    start_z(0, 0)
    start_y(0, 2)

    grad_res = ffn_in
    grad_att = grad_pre
    sub_out = gffn_own
    normed = gffn_got
    def norms_back(at, carry):
        rows = pl.ds(pl.multiple_of(at * CHUNK, CHUNK), CHUNK)
        gffn_copy(at).wait()
        grad = gffn_own[rows, :].astype(F32) + gffn_got[rows, :].astype(F32)
        hat, inv = moments(mid[rows, :])
        gain_own[2:3, :] += jnp.sum(grad * hat, 0, keepdims=True)
        grad_mid = cot[rows, :].astype(F32) + norm_grad(hat, inv, gf, grad)
        gtok[rows, :] = grad_mid
        grad_low = grad_mid.astype(BF16)
        grad_res[rows, :] = grad_low
        grad = dot(grad_low, wo[...], 1, 1)
        hat, inv = moments(att[rows, :])
        sub_out[rows, :] = (hat * gs).astype(BF16)
        gain_own[1:2, :] += jnp.sum(grad * hat, 0, keepdims=True)
        grad_att[rows, width : 2 * width] = norm_grad(hat, inv, gs, grad).astype(BF16)
        hat, _ = moments(tok[rows, :].astype(F32))
        normed[rows, :] = (hat * ga).astype(BF16)
        return carry

    lax.fori_loop(0, chunks, norms_back, 0)
    for at in range(1, chunks):
        ffp_copy(at).start()
    start_z(0, 1)
    start_y(1, 0)
    for side in range(2):
        columns = slice(side * width, (side + 1) * width)
        gain_own[3 + side : 4 + side, :] = jnp.sum(gain_mid_sum[:, columns], 0, keepdims=True)
    gain_stage[0].start()

    def ring_block(which):
        ring, which = (ring_h, which) if which < 24 else (ring_d, which - 24)
        top, left = which // 12 * LANES, which % 12 * LANES
        return ring, (slice(top, top + LANES), slice(left, left + LANES))

    blocks_in_row = length // LANES
    window_blocks = WINDOW // LANES + 1
    windows = [range(max(0, at + 1 - window_blocks), at + 1) for at in range(blocks_in_row)]
    mask_first = [sum(len(one) for one in windows[:at]) for at in range(blocks_in_row)]
    sums_first = sum(len(one) for one in windows)
    key_off = lax.broadcasted_iota(jnp.int32, (LANES, LANES), 0)
    query_off = lax.broadcasted_iota(jnp.int32, (LANES, LANES), 1)
    for query_block, window in enumerate(windows):
        for index, key_block in enumerate(window):
            ring, place = ring_block(mask_first[query_block] + index)
            allowed = doc_col[key_block * LANES : (key_block + 1) * LANES, :] == (
                doc_row[:, query_block * LANES : (query_block + 1) * LANES]
            )
            if key_block == query_block:
                allowed = allowed & (key_off <= query_off)
            ring[place] = jnp.where(allowed, 0.0, -1e30)

    select = (lax.broadcasted_iota(jnp.int32, (8, LANES), 1) // HEAD_DIM) == (
        lax.broadcasted_iota(jnp.int32, (8, LANES), 0)
    )
    select = select.astype(F32).astype(BF16)
    half_width = width // 2

    def own_grads(part):
        offset = pl.multiple_of(tp * half_width + part * LANES, LANES)
        offset_up = pl.multiple_of(width + tp * half_width + part * LANES, LANES)
        right = [
            mid_out[:, pl.ds(offset, LANES)],
            mid_out[:, pl.ds(offset_up, LANES)],
            grad_pre[:, pl.ds(offset, LANES)],
        ]
        grad = dot(normed[...], jnp.concatenate(right, 1), 0, 0).astype(BF16)
        low = pl.multiple_of(part * COLUMNS, COLUMNS)
        item_a[:, :, :, :, pl.ds(low, 3 * LANES)] = grad.reshape(nz, ny, 2, piece, 3 * LANES)
        grad = dot(sub_out[...], grad_res[:, pl.ds(offset, LANES)], 0, 0).astype(BF16)
        low = pl.multiple_of(part * COLUMNS + 3 * LANES, LANES)
        item_a[:, :, :, :, pl.ds(low, LANES)] = grad.reshape(nz, ny, 2, piece, LANES)
        start_core(2, part)

    def half_copy(part):
        columns = part_columns(part)
        return remote(half_own.at[:, columns], half_got.at[:, columns], half_sem, part, to_x)

    def finish_own(part):
        finish(2, part)
        half_copy(part).start()

    def gain_step(at):
        gain_add(at)
        if at == 0:
            gain_stage[1].start()
        else:
            for copy in gain_last:
                copy.start()

    def when(condition, *events):
        @pl.when(condition)
        def _():
            for event, *arguments in events:
                event(*arguments)

    def middle(step):
        when(step == 0, (start_z, 0, 2), (gain_step, 0), (start_y, 1, 1))
        when(step == 1, (gain_step, 1), (start_z, 1, 0), (start_y, 2, 0))
        when(step == 2, (start_z, 1, 1), (start_y, 2, 1))
        when(step == 3, (start_z, 2, 1), (start_y, 2, 2))
        when(step == 4, (finish_own, 0))

    def ending(step):
        when(step < parts, (own_grads, step))
        when(step < parts, (finish, 0, step))
        when(step == 2, (start_z, 2, 0))
        when(step == 3, (start_y, 1, 2))
        when(step == 4, (start_z, 2, 2), (finish_own, 1), (finish, 1, 0))
        when(step == 5, (start_z, 1, 2), (finish, 1, 1))

    def pair_back(step, carry):
        pair = lax.rem(tp * (pairs // 2) + step, pairs)
        low = pl.multiple_of(pair * LANES, LANES)
        lanes = pl.ds(low, LANES)
        upper = pl.ds(pl.multiple_of(width + low, LANES), LANES)
        product = grad_att[:, upper].astype(F32) * att[:, lanes]
        high = product.astype(BF16)
        rest = (product - high.astype(F32)).astype(BF16)
        delta[...] = dot(select, high, 1, 1) + dot(select, rest, 1, 1)
        key_t[...] = ks[:, lanes].T
        for which in range(sums_first, sums_first + 2 * blocks_in_row):
            ring, place = ring_block(which)
            ring[place] = jnp.zeros((LANES, LANES), F32)
        weights = jnp.concatenate([weights_c[2 * pair], weights_c[2 * pair + 1]], 1)
        for query_block, window in enumerate(windows):
            if query_block == blocks_in_row // 2:
                middle(step)
            queries = slice(query_block * LANES, (query_block + 1) * LANES)
            keys = slice(window[0] * LANES, queries.stop)
            span = len(window) * LANES
            query = qs[queries, lanes]
            grad_out = grad_att[queries, upper]
            query_two = jnp.concatenate([query * lane_b[0], query * lane_b[1]], 0)
            grad_two = jnp.concatenate([grad_out * lane_b[0], grad_out * lane_b[1]], 0)
            mask = []
            for index in range(len(window)):
                ring, place = ring_block(mask_first[query_block] + index)
                mask.append(ring[place])
            mask = jnp.concatenate(mask, 0)
            mask = jnp.concatenate([mask, mask], 1)
            log_sum = jnp.concatenate([lse[pair, 0:1, queries], lse[pair, 1:2, queries]], 1)
            back = jnp.concatenate([delta[0:1, queries], delta[1:2, queries]], 1)
            power = dot(ks[keys, lanes], query_two, 1, 1) * (HEAD_DIM**-0.5 * LOG2E) + mask
            prob = jnp.exp2(power - log_sum) * repeat(weights, span, 2 * LANES)
            grad_score = prob * (dot(vs[keys, lanes], grad_two, 1, 1) - back)
            grad_score = grad_score.astype(BF16)
            dv = dot(prob.astype(BF16), grad_two, 1, 0)
            dk = dot(grad_score, query_two, 1, 0)
            dq = dot(key_t[:, keys], grad_score, 1, 0) * HEAD_DIM**-0.5
            dq = jnp.concatenate([dq[:HEAD_DIM, :LANES], dq[HEAD_DIM:, LANES:]], 0)
            mid_out[queries, lanes] = dq.T.astype(BF16)
            for index, key_block in enumerate(window):
                part = slice(index * LANES, (index + 1) * LANES)
                ring, place = ring_block(sums_first + key_block)
                ring[place] += dv[part, :]
                ring, place = ring_block(sums_first + blocks_in_row + key_block)
                ring[place] += dk[part, :]
        for block in range(blocks_in_row):
            rows = slice(block * LANES, (block + 1) * LANES)
            ring, place = ring_block(sums_first + block)
            grad_pre[rows, lanes] = ring[place].astype(BF16)
            ring, place = ring_block(sums_first + blocks_in_row + block)
            mid_out[rows, upper] = (ring[place] * HEAD_DIM**-0.5).astype(BF16)

        ending(step)
        return carry

    lax.fori_loop(0, pairs, pair_back, 0)

    stores = []

    def store(near, far, at):
        copy = pltpu.make_async_copy(near, far, store_sem.at[at])
        copy.start()
        stores.append(copy)

    def tokens_back(at, carry):
        rows = pl.ds(pl.multiple_of(at * CHUNK, CHUNK), CHUNK)
        grad = dot(mid_out[rows, 0:width], wq[...], 1, 1)
        grad += dot(mid_out[rows, width : 2 * width], wk[...], 1, 1)
        grad += dot(grad_pre[rows, 0:width], wv[...], 1, 1)
        hat, inv = moments(tok[rows, :].astype(F32))
        gtok[rows, :] += norm_grad(hat, inv, ga, grad)
        pltpu.make_async_copy(gtok.at[rows], gtok_far.at[rows], store_sem.at[at]).start()
        when(at == 1, (finish_own, 2))
        return carry

    lax.fori_loop(0, chunks, tokens_back, 0)
    finish(1, 2)
    for at in range(chunks):
        rows = pl.ds(at * CHUNK, CHUNK)
        stores.append(pltpu.make_async_copy(gtok.at[rows], gtok_far.at[rows], store_sem.at[at]))

    for copy in gain_last:
        copy.wait()
    total = gain_own[...]
    for k in range(1, nz):
        total = total + gain_got[1 + k]
    o_gain[0:8, :] = pltpu.roll(total, lax.rem(width - piece * row, width), 1)[:, :LANES]
    per_row = 2 * piece
    o_gain[8:16, :] = pltpu.roll(total, lax.rem(2 * width - per_row * row, width), 1)[:, :LANES]

    for at in range(chunks):
        rows = pl.ds(at * CHUNK, CHUNK)
        ffp_copy(at).wait()
        total = ffp_own[rows, :].astype(F32) + ffp_got[rows, :].astype(F32)
        ffp_own[rows, :] = (mid[rows, :] + total).astype(BF16)
        store(ffp_own.at[rows], out_far.at[rows], chunks + at)

    for part in range(pairs // 2):
        half_copy(part).wait()
    mine_at = pl.multiple_of(tp * half_width, LANES)
    other_at = pl.multiple_of((1 - tp) * half_width, LANES)
    for part in range(pairs // 2):
        mine, other = (
            pl.ds(pl.multiple_of(begin + part * LANES, LANES), LANES)
            for begin in (mine_at, other_at)
        )
        for index, target in enumerate((o_query, o_key, o_value, o_out)):
            low = part * COLUMNS + index * LANES
            target[:, mine] = half_own[:, low : low + LANES].astype(F32)
            target[:, other] = half_got[:, low : low + LANES].astype(F32)
    own_rows = pl.ds(pl.multiple_of(piece * row, 16), piece)
    product = wq[own_rows, :].astype(F32) * o_query[...]
    product += wk[own_rows, :].astype(F32) * o_key[...]
    product += wv[own_rows, :].astype(F32) * o_value[...]
    total = jnp.broadcast_to(jnp.sum(product, -1, keepdims=True), (piece, LANES))
    total = jnp.concatenate([total, jnp.zeros((LANES - piece, LANES), F32)], 0).T
    gain = pltpu.roll(repeat(ga, 8, width), lax.rem(width - piece * row, width), 1)
    o_gain[0:1, :] = total[0:1, :] / gain[0:1, :LANES]
    for copy in stores:
        copy.wait()


def write_kernel(places, *refs):
    far_in, gain_in, far_out, gains_out = refs[:8], refs[8], refs[9:17], refs[17:21]
    near, sems = refs[21:29], refs[29]
    g_attn, g_sub, g_ffn, g_mid = gains_out
    nz, ny = places
    row = lax.axis_index("row")
    width = far_in[0].shape[1]
    piece = far_in[2].shape[0]
    steps = []
    for at in range(8):
        length = far_in[at].shape[0]
        size = CHUNK if length > CHUNK else length
        for begin in range(0, length, size):
            rows, which = pl.ds(begin, size), len(steps)
            steps.append(
                (
                    pltpu.make_async_copy(
                        far_in[at].at[rows], near[at].at[rows], sems.at[0, which]
                    ),
                    pltpu.make_async_copy(
                        near[at].at[rows], far_out[at].at[rows], sems.at[1, which]
                    ),
                )
            )
    for load, _ in steps:
        load.start()
    tile = gain_in[...]
    g_attn[...] = tile[0, :piece]
    g_sub[...] = tile[1, :piece]
    g_ffn[...] = tile[2, :piece]
    later = (2 * piece * row) // width
    g_mid[...] = jnp.where(later == 0, tile[11, : 2 * piece], tile[12, : 2 * piece])
    for load, save in steps:
        load.wait()
        save.start()
    for _, save in steps:
        save.wait()


def fused_body(places, *args):
    (tokens, doc_ids, dilations, cotangent, w_query, w_key, w_value, w_out, w_up, w_down) = args[:10]
    gains = args[10:]
    nz, ny = places
    length, width = tokens.shape
    half = w_up.shape[1]
    piece = width // (2 * nz * ny)
    chunks = length // CHUNK
    vmem = pl.BlockSpec(memory_space=pltpu.VMEM)
    smem = pl.BlockSpec(memory_space=pltpu.SMEM)
    far = pl.BlockSpec(memory_space=pl.ANY)
    shape = jax.ShapeDtypeStruct
    low = functools.partial(pltpu.VMEM, dtype=BF16)
    full = functools.partial(pltpu.VMEM, dtype=F32)
    rows_low, rows_full = low((length, width)), full((length, width))
    item = low((nz, ny, 2, piece, half))
    square = low((width, width))
    count = 3 * half // COLUMNS
    dma = lambda number: pltpu.SemaphoreType.DMA((2, number))
    big = [
        shape((length, width), BF16),
        shape((length, width), F32),
        shape((piece, width), F32),
        shape((piece, width), F32),
        shape((piece, width), F32),
        shape((piece, width), F32),
        shape((piece, half), F32),
        shape((piece, half), F32),
    ]
    results = pl.pallas_call(
        functools.partial(layer_kernel, places),
        out_shape=big + [shape((16, LANES), F32)],
        in_specs=[smem] + [vmem] * 5 + [far] * 8,
        out_specs=[far] * 2 + [vmem] * 7,
        scratch_shapes=[
            rows_low,
            rows_low,
            square,
            square,
            square,
            square,
            item,
            low((half, width)),
            rows_full,
            rows_low,
            rows_low,
            rows_low,
            rows_full,
            rows_full,
            rows_low,
            low((length, half)),
            low((length, half)),
            full((CHUNK, half)),
            full((CHUNK, half)),
            rows_low,
            rows_low,
            rows_low,
            rows_low,
            full((HEADS, 16, LANES)),
            full((length, LANES)),
            full((width // LANES, 2, length)),
            full((8, length)),
            low((LANES, length)),
            full((chunks, 8, CHUNK)),
            full((chunks, 8, CHUNK)),
            full((8, half)),
            full((8, width)),
            full((1 + nz, 8, width)),
            item,
            item,
            low((6, nz, ny, piece, COLUMNS)),
            low((6, nz, piece, COLUMNS)),
            low((count, nz - 1, piece, COLUMNS)),
            low((piece, half)),
            low((piece, half)),
            dma(chunks),
            dma(chunks),
            dma(chunks),
            dma(8 * count),
            dma(1 + nz),
            dma(width // LANES // 2),
            pltpu.SemaphoreType.DMA((8,)),
            pltpu.SemaphoreType.DMA((2 * chunks,)),
        ],
        compiler_params=pltpu.CompilerParams(
            collective_id=0, has_side_effects=True, vmem_limit_bytes=63 * MIB
        ),
        name="layer",
    )(
        dilations,
        doc_ids.reshape(1, length),
        *gains,
        tokens,
        cotangent,
        w_query,
        w_key,
        w_value,
        w_out,
        w_up.reshape(nz, ny, 2, piece, half),
        w_down,
    )
    flat = shape((piece,), F32)
    moves = 2 * (length // CHUNK) + 6
    final = pl.pallas_call(
        functools.partial(write_kernel, places),
        out_shape=big + [flat, flat, flat, shape((2 * piece,), F32)],
        in_specs=[far] * 8 + [vmem],
        out_specs=[far] * 8 + [vmem] * 4,
        scratch_shapes=[pltpu.VMEM(one.shape, one.dtype) for one in big]
        + [pltpu.SemaphoreType.DMA((2, moves))],
        compiler_params=pltpu.CompilerParams(vmem_limit_bytes=63 * MIB),
        name="write",
    )(*results)
    return (*final[:7], final[7].T, *final[8:])


def norm_parts(value):
    row_mean = jnp.mean(value, -1, keepdims=True)
    centred = value - row_mean
    inv_std = lax.rsqrt(jnp.mean(centred * centred, -1, keepdims=True) + EPS)
    return (centred * inv_std, inv_std)


def norm_back(normed_hat, inv_std, gain, grad):
    scaled = grad * gain
    grad_value = inv_std * (
        scaled
        - jnp.mean(scaled, -1, keepdims=True)
        - normed_hat * jnp.mean(scaled * normed_hat, -1, keepdims=True)
    )
    return (grad_value, jnp.sum(grad * normed_hat, 0))


def selection(dilations, positions):
    head_ids = jnp.arange(HEADS, dtype=jnp.int32)
    left_side = positions[None, None, :] % dilations[:, None, None]
    right_side = head_ids[None, :, None] % dilations[:, None, None]
    return (left_side == right_side).astype(jnp.float32)


def pattern_weights(dilations, doc_row, query_pos, query_docs):
    key_pos = jnp.arange(doc_row.shape[0], dtype=jnp.int32)
    counts = jnp.einsum(
        "phi,phj->hij", selection(dilations, query_pos), selection(dilations, key_pos)
    )
    allowed = (query_pos[:, None] >= key_pos[None, :]) & (query_docs[:, None] == doc_row[None, :])
    return counts * allowed.astype(jnp.float32)[None]


def attn_forward(dilations, doc_row, key_heads, value_heads, query_block, query_pos, query_docs):
    score_scale = HEAD_DIM ** (-0.5)
    scores = (
        jnp.einsum("ihe,jhe->hij", query_block, key_heads, preferred_element_type=jnp.float32)
        * score_scale
    )
    weights_mult = pattern_weights(dilations, doc_row, query_pos, query_docs)
    masked = jnp.where(weights_mult > 0, scores, -1e30)
    row_max = jnp.max(masked, -1, keepdims=True)
    expo = weights_mult * jnp.exp(masked - row_max)
    totals = jnp.sum(expo, -1, keepdims=True)
    attn_prob = (expo / totals).astype(jnp.bfloat16)
    out_block = jnp.einsum(
        "hij,jhe->ihe", attn_prob, value_heads, preferred_element_type=jnp.float32
    )
    return (out_block, row_max[..., 0] + jnp.log(totals[..., 0]))


def attn_backward(
    dilations,
    doc_row,
    key_heads,
    value_heads,
    query_block,
    query_pos,
    query_docs,
    lse_block,
    grad_block,
):
    score_scale = HEAD_DIM ** (-0.5)
    scores = (
        jnp.einsum("ihe,jhe->hij", query_block, key_heads, preferred_element_type=jnp.float32)
        * score_scale
    )
    weights_mult = pattern_weights(dilations, doc_row, query_pos, query_docs)
    attn_full = weights_mult * jnp.exp(scores - lse_block[:, :, None])
    attn_low = attn_full.astype(jnp.bfloat16)
    value_part = jnp.einsum(
        "hij,ihe->jhe", attn_low, grad_block, preferred_element_type=jnp.float32
    )
    grad_prob = jnp.einsum(
        "ihe,jhe->hij", grad_block, value_heads, preferred_element_type=jnp.float32
    )
    row_delta = jnp.sum(attn_full * grad_prob, -1, keepdims=True)
    grad_scores = (attn_full * (grad_prob - row_delta)).astype(jnp.bfloat16)
    query_grad = (
        jnp.einsum("hij,jhe->ihe", grad_scores, key_heads, preferred_element_type=jnp.float32)
        * score_scale
    )
    key_part = (
        jnp.einsum("hij,ihe->jhe", grad_scores, query_block, preferred_element_type=jnp.float32)
        * score_scale
    )
    return (query_grad, key_part, value_part)


def general_body(
    tokens,
    doc_ids,
    dilations,
    cotangent,
    w_query,
    w_key,
    w_value,
    w_out,
    w_up,
    w_down,
    gain_attn,
    gain_sub,
    gain_ffn,
    gain_mid,
):
    row_len = tokens.shape[0]
    width = tokens.shape[1]
    block_rows = min(512, row_len)
    block_count = row_len // block_rows
    doc_row = doc_ids.reshape(row_len)
    row_in = tokens.astype(jnp.float32)
    attn_hat, attn_std = norm_parts(row_in)
    normed = (attn_hat * gain_attn).astype(jnp.bfloat16)
    keys_low = jnp.dot(normed, w_key, preferred_element_type=jnp.float32).astype(jnp.bfloat16)
    values_low = jnp.dot(normed, w_value, preferred_element_type=jnp.float32).astype(jnp.bfloat16)
    key_heads = keys_low.reshape(row_len, HEADS, HEAD_DIM)
    value_heads = values_low.reshape(row_len, HEADS, HEAD_DIM)
    queries = jnp.dot(normed, w_query, preferred_element_type=jnp.float32).astype(jnp.bfloat16)
    query_heads = queries.reshape(row_len, HEADS, HEAD_DIM)

    def attend(block_index):
        offset = block_index * block_rows
        query_block = lax.dynamic_slice_in_dim(query_heads, offset, block_rows, 0)
        query_pos = offset + jnp.arange(block_rows, dtype=jnp.int32)
        query_docs = lax.dynamic_slice_in_dim(doc_row, offset, block_rows, 0)
        return attn_forward(
            dilations, doc_row, key_heads, value_heads, query_block, query_pos, query_docs
        )

    out_blocks, log_sums = lax.map(attend, jnp.arange(block_count))
    attended = out_blocks.reshape(row_len, width)
    sub_hat, sub_std = norm_parts(attended)
    sub_out = (sub_hat * gain_sub).astype(jnp.bfloat16)
    mid_res = row_in + jnp.dot(sub_out, w_out, preferred_element_type=jnp.float32)
    ffn_hat, ffn_std = norm_parts(mid_res)
    ffn_in = (ffn_hat * gain_ffn).astype(jnp.bfloat16)
    hidden_pre = jnp.dot(ffn_in, w_up, preferred_element_type=jnp.float32)
    hidden_act = jax.nn.gelu(hidden_pre, approximate=False)
    sum_first, sum_second = lax.psum(
        (jnp.sum(hidden_act, -1), jnp.sum(hidden_act * hidden_act, -1)), "tp"
    )
    mid_mean = sum_first[:, None] / FF
    mid_std = lax.rsqrt(sum_second[:, None] / FF - mid_mean * mid_mean + EPS)
    mid_hat = (hidden_act - mid_mean) * mid_std
    mid_out = (mid_hat * gain_mid).astype(jnp.bfloat16)
    ffn_part = jnp.dot(mid_out, w_down, preferred_element_type=jnp.float32)
    ffn_total = lax.psum(ffn_part, "tp")
    output = (mid_res + ffn_total).astype(jnp.bfloat16)
    grad_down = jnp.einsum("lf,ld->fd", mid_out, cotangent, preferred_element_type=jnp.float32)
    grad_mid_out = jnp.einsum("ld,fd->lf", cotangent, w_down, preferred_element_type=jnp.float32)
    grad_gain_mid = jnp.sum(grad_mid_out * mid_hat, 0)
    scaled = grad_mid_out * gain_mid
    back_first, back_second = lax.psum((jnp.sum(scaled, -1), jnp.sum(scaled * mid_hat, -1)), "tp")
    grad_act = mid_std * (scaled - back_first[:, None] / FF - mid_hat * back_second[:, None] / FF)
    gelu_pull = jax.vjp(lambda value: jax.nn.gelu(value, approximate=False), hidden_pre)[1]
    grad_pre = gelu_pull(grad_act)[0].astype(jnp.bfloat16)
    grad_up = jnp.einsum("ld,lf->df", ffn_in, grad_pre, preferred_element_type=jnp.float32)
    sum_up, sum_down, sum_gain_mid = (
        lax.psum_scatter(grad_up, "row", scatter_dimension=0, tiled=True),
        lax.psum_scatter(grad_down, "row", scatter_dimension=1, tiled=True),
        lax.psum_scatter(grad_gain_mid, "row", scatter_dimension=0, tiled=True),
    )
    grad_ffn_part = jnp.einsum("lf,df->ld", grad_pre, w_up, preferred_element_type=jnp.float32)
    grad_ffn_in = lax.psum(grad_ffn_part, "tp")
    grad_mid_in, grad_gain_ffn = norm_back(ffn_hat, ffn_std, gain_ffn, grad_ffn_in)
    grad_mid_res = cotangent.astype(jnp.float32) + grad_mid_in
    grad_res_low = grad_mid_res.astype(jnp.bfloat16)
    grad_out = jnp.einsum("ld,le->de", sub_out, grad_res_low, preferred_element_type=jnp.float32)
    grad_sub_out = jnp.einsum("le,de->ld", grad_res_low, w_out, preferred_element_type=jnp.float32)
    grad_attended, grad_gain_sub = norm_back(sub_hat, sub_std, gain_sub, grad_sub_out)
    grad_att_low = grad_attended.astype(jnp.bfloat16)
    grad_heads = grad_att_low.reshape(row_len, HEADS, HEAD_DIM)

    def attend_back(running, block_index):
        key_sum, value_sum = running
        offset = block_index * block_rows
        query_block = lax.dynamic_slice_in_dim(query_heads, offset, block_rows, 0)
        query_pos = offset + jnp.arange(block_rows, dtype=jnp.int32)
        query_docs = lax.dynamic_slice_in_dim(doc_row, offset, block_rows, 0)
        grad_block = lax.dynamic_slice_in_dim(grad_heads, offset, block_rows, 0)
        query_grad, key_part, value_part = attn_backward(
            dilations,
            doc_row,
            key_heads,
            value_heads,
            query_block,
            query_pos,
            query_docs,
            log_sums[block_index],
            grad_block,
        )
        return ((key_sum + key_part, value_sum + value_part), query_grad)

    zero_heads = jnp.zeros((row_len, HEADS, HEAD_DIM), jnp.float32)
    (key_grad, value_grad), query_blocks = lax.scan(
        attend_back, (zero_heads, zero_heads), jnp.arange(block_count)
    )
    grad_queries = query_blocks.reshape(row_len, width).astype(jnp.bfloat16)
    grad_keys = key_grad.reshape(row_len, width).astype(jnp.bfloat16)
    grad_values = value_grad.reshape(row_len, width).astype(jnp.bfloat16)
    grad_query = jnp.einsum("ld,le->de", normed, grad_queries, preferred_element_type=jnp.float32)
    grad_key = jnp.einsum("ld,le->de", normed, grad_keys, preferred_element_type=jnp.float32)
    grad_value = jnp.einsum("ld,le->de", normed, grad_values, preferred_element_type=jnp.float32)
    grad_normed = (
        jnp.einsum("le,de->ld", grad_queries, w_query, preferred_element_type=jnp.float32)
        + jnp.einsum("le,de->ld", grad_keys, w_key, preferred_element_type=jnp.float32)
        + jnp.einsum("le,de->ld", grad_values, w_value, preferred_element_type=jnp.float32)
    )
    grad_row_in, grad_gain_attn = norm_back(attn_hat, attn_std, gain_attn, grad_normed)
    grad_tokens = grad_mid_res + grad_row_in
    sum_query, sum_key, sum_value, sum_out, sum_gain_attn, sum_gain_sub, sum_gain_ffn = (
        lax.psum_scatter(grad_query, "row", scatter_dimension=0, tiled=True),
        lax.psum_scatter(grad_key, "row", scatter_dimension=0, tiled=True),
        lax.psum_scatter(grad_value, "row", scatter_dimension=0, tiled=True),
        lax.psum_scatter(grad_out, "row", scatter_dimension=0, tiled=True),
        lax.psum_scatter(grad_gain_attn, "row", scatter_dimension=0, tiled=True),
        lax.psum_scatter(grad_gain_sub, "row", scatter_dimension=0, tiled=True),
        lax.psum_scatter(grad_gain_ffn, "row", scatter_dimension=0, tiled=True),
    )
    return (
        output,
        grad_tokens,
        sum_query,
        sum_key,
        sum_value,
        sum_out,
        sum_up,
        sum_down,
        sum_gain_attn,
        sum_gain_sub,
        sum_gain_ffn,
        sum_gain_mid,
    )


def solution(mesh):
    rows, columns = mesh.shape["row"], mesh.shape["tp"]
    if columns == 2 and rows == 16:
        body = functools.partial(fused_body, (rows // 4, 2))
    else:
        body = general_body
    return jax.shard_map(
        body,
        mesh=mesh,
        in_specs=(
            P("row", None),
            P("row", None),
            P(),
            P("row", None),
            P(),
            P(),
            P(),
            P(),
            P(None, "tp"),
            P("tp", None),
            P(),
            P(),
            P(),
            P("tp"),
        ),
        out_specs=(
            P("row", None),
            P("row", None),
            P("row", None),
            P("row", None),
            P("row", None),
            P("row", None),
            P("row", "tp"),
            P("tp", "row"),
            P("row"),
            P("row"),
            P("row"),
            P(("tp", "row")),
        ),
        check_vma=False,
    )
```
